512 devices in a mesh: tm: 8 (over z_hi, core), space: 64 (over z_lo, y, x).
Axes of the slice: x: 4, y: 8, z: 8 (z_hi: 4, z_lo: 2; z = z_hi * 2 + z_lo), core: 2. Of those that a mesh axis runs over, the one named last changes fastest.
Arguments:
- equilibrium: float32 [16, 512, 128], P('tm', 'space'), may hold values from -6 to 6
- measurement: float32 [512, 128], P('space'), may hold values from -12 to 12
- coding_masks: int32 [16, 512, 128], P('tm', 'space'), may hold values 0 or 1
- upstream: float32 [16, 512, 128], P('tm', 'space'), may hold values from -6 to 6
- saved_second: bfloat16 [16, 64, 512, 128], P('tm', None, 'space'), may hold values from -8 to 8
- conv_first: bfloat16 [9, 64], replicated, may hold values from -2 to 2
- conv_second: bfloat16 [9, 64, 64], replicated, may hold values from -0.25 to 0.25
- conv_third: bfloat16 [9, 64], replicated, may hold values from -0.75 to 0.75
Outputs:
- adjoint: float32 [16, 512, 128], P('tm', 'space')
- measurement_grad: float32 [512, 128], P('space')
- grad_first: float32 [9, 64], replicated
- grad_second: float32 [9, 64, 64], replicated
- grad_third: float32 [9, 64], replicated
The draws below stay inside these ranges and needn't reach their ends.
All inputs are finite; a program needn't handle non-finite values. No bound on the sum of `coding_masks` on one device may be relied on, other than what follows from the above.
Results may differ from the reference program's by a relative error of at most 0.013.
Values may be sent and summed in bfloat16 or wider, within the bound.
No kernel may reach another device: no remote copies, remote signals or barrier semaphores. Data moves between devices by JAX's collectives and lax.ppermute only.
A program may use at most 64 MiB of HBM per device.

```python
import math
import jax
import jax.numpy as jnp
from jax import lax

C = 64
COLS = 128
ITERS = 3
FRAMES = 16
ROWS = 512


def touch_ends(array, own_key, low, largest):
    spot = [jax.random.randint(jax.random.fold_in(own_key, axis), (), 0, length) for axis, length in enumerate(array.shape)]
    main_axis = array.shape.index(max(array.shape))
    beside = spot[:main_axis] + [(spot[main_axis] + 1) % array.shape[main_axis]] + spot[main_axis + 1:]
    return array.at[tuple(spot)].set(low).at[tuple(beside)].set(largest)


def steps_of(own_key, shape, cuts, least, high):
    loudness = 1.0
    for axis_at, blocks in cuts:
        steps = jax.random.uniform(jax.random.fold_in(jax.random.fold_in(own_key, 6), axis_at), (blocks,), jnp.float32, least / len(cuts), high / len(cuts))
        loudness = loudness * jnp.repeat(jnp.exp(steps), shape[axis_at] // blocks).reshape((-1,) + (1,) * (len(shape) - 1 - axis_at))
    return loudness


def noise(stream_key, dims, deviation, most, pieces=(), kind=jnp.bfloat16):
    drawn = jax.random.normal(stream_key, dims, jnp.float32) * deviation
    if len(pieces) > 0:
        drawn = steps_of(stream_key, dims, pieces, -0.22, 0.18) * drawn
    return jnp.clip(drawn, min=-most, max=most).astype(kind)


def setup_inputs(seed: int = 0) -> dict:
    seeds = jax.random.split(jax.random.key(seed), 9)
    return {
        "equilibrium": noise(seeds[0], (FRAMES, ROWS, COLS), 1.0, 6.0, ((0, 8), (1, 64)), jnp.float32),
        "measurement": noise(seeds[1], (ROWS, COLS), 2.0, 12.0, ((0, 64),), jnp.float32),
        "coding_masks": touch_ends((jax.random.randint(seeds[2], (FRAMES, ROWS, COLS), 0, 2) < 1).astype(jnp.int32), jax.random.fold_in(seeds[2], 1), 0, 1),
        "upstream": noise(seeds[3], (FRAMES, ROWS, COLS), 1.0, 6.0, ((0, 8), (1, 64)), jnp.float32),
        "saved_second": noise(seeds[4], (FRAMES, C, ROWS, COLS), 1.5, 8.0, ((0, 8), (2, 64))),
        "conv_first": noise(seeds[5], (9, C), 9 ** -0.5, 2.0),
        "conv_second": noise(seeds[6], (9, C, C), (9 * C) ** -0.5, 0.25),
        "conv_third": noise(seeds[7], (9, C), C ** -0.5, 0.75),
    }


KERNEL_TAPS = [(row_step, col_step) for row_step in (-1, 0, 1) for col_step in (-1, 0, 1)]

def silu_slope(value):
    logistic = jax.nn.sigmoid(value)
    return logistic * (1.0 + value * (1.0 - logistic))

def padded(field):
    widths = [(0, 0)] * (field.ndim - 2) + [(1, 1), (1, 1)]
    return jnp.pad(field, widths)

def window(field, row_step, col_step):
    height = field.shape[-2] - 2
    breadth = field.shape[-1] - 2
    return field[..., 1 + row_step:1 + row_step + height, 1 + col_step:1 + col_step + breadth]

def frame_parts(source, adjoint_f, saved, conv_first, conv_second, conv_third):
    first_f = conv_first.astype(jnp.float32)
    second_f = conv_second.astype(jnp.float32)
    third_f = conv_third.astype(jnp.float32)
    source_pad = padded(source)
    first_pre = jnp.zeros((first_f.shape[1],) + source.shape, jnp.float32)
    for tap_index, (row_step, col_step) in enumerate(KERNEL_TAPS):
        first_pre = first_pre + first_f[tap_index][:, None, None] * window(source_pad, row_step, col_step)[None]
    adjoint_pad = padded(adjoint_f)
    third_back = jnp.zeros(first_pre.shape, jnp.float32)
    for tap_index, (row_step, col_step) in enumerate(KERNEL_TAPS):
        third_back = third_back + third_f[tap_index][:, None, None] * window(adjoint_pad, -row_step, -col_step)[None]
    d_second = (silu_slope(saved.astype(jnp.float32)) * third_back).astype(jnp.bfloat16)
    second_pad = padded(d_second.astype(jnp.float32))
    second_back = jnp.zeros(first_pre.shape, jnp.float32)
    for tap_index, (row_step, col_step) in enumerate(KERNEL_TAPS):
        second_back = second_back + jnp.einsum('oc,orw->crw', second_f[tap_index], window(second_pad, -row_step, -col_step), precision=lax.Precision.HIGHEST)
    d_first = (silu_slope(first_pre) * second_back).astype(jnp.bfloat16)
    first_pad = padded(d_first.astype(jnp.float32))
    first_back = jnp.zeros(source.shape, jnp.float32)
    for tap_index, (row_step, col_step) in enumerate(KERNEL_TAPS):
        first_back = first_back + jnp.einsum('o,orw->rw', first_f[tap_index], window(first_pad, -row_step, -col_step), precision=lax.Precision.HIGHEST)
    return (adjoint_f + first_back, first_pre, second_pad, first_pad, adjoint_pad)

def reference(equilibrium, measurement, coding_masks, upstream, saved_second, conv_first, conv_second, conv_third):
    masks = coding_masks.astype(jnp.float32)
    step_size = 1.0 / FRAMES
    frame_sum = lax.optimization_barrier(jnp.sum(masks * equilibrium, axis=0))
    source = equilibrium - step_size * masks * (frame_sum - measurement)[None]

    def frame_map(bundle):
        return frame_parts(bundle[0], bundle[1], bundle[2], conv_first, conv_second, conv_third)[0]
    adjoint = upstream
    for sweep_index in range(ITERS):
        mapped = lax.map(frame_map, (source, adjoint, saved_second))
        totals = lax.optimization_barrier(jnp.sum(masks * mapped, axis=0))
        adjoint = upstream + mapped - step_size * masks * totals[None]

    def final_frame(carry, bundle):
        source_f, adjoint_f, saved_f = bundle
        mapped_f, first_pre, second_pad, first_pad, adjoint_pad = frame_parts(source_f, adjoint_f, saved_f, conv_first, conv_second, conv_third)
        hidden_first = jax.nn.silu(first_pre).astype(jnp.bfloat16).astype(jnp.float32)
        hidden_second = jax.nn.silu(saved_f.astype(jnp.float32))
        first_terms = []
        second_terms = []
        third_terms = []
        for row_step, col_step in KERNEL_TAPS:
            second_terms.append(jnp.einsum('orw,crw->oc', window(second_pad, -row_step, -col_step), hidden_first, precision=lax.Precision.HIGHEST))
            first_terms.append(lax.optimization_barrier(jnp.sum(window(first_pad, -row_step, -col_step) * source_f[None], axis=(1, 2))))
            third_terms.append(lax.optimization_barrier(jnp.sum(hidden_second * window(adjoint_pad, -row_step, -col_step)[None], axis=(1, 2))))
        return ((carry[0] + jnp.stack(first_terms), carry[1] + jnp.stack(second_terms), carry[2] + jnp.stack(third_terms)), mapped_f)
    start_grads = (jnp.zeros((9, C), jnp.float32), jnp.zeros((9, C, C), jnp.float32), jnp.zeros((9, C), jnp.float32))
    grads, mapped = lax.scan(final_frame, start_grads, (source, adjoint, saved_second))
    measurement_grad = step_size * lax.optimization_barrier(jnp.sum(masks * mapped, axis=0))
    scale = 1.0 / math.sqrt(FRAMES * ROWS * COLS)
    return (adjoint, measurement_grad, grads[0] * scale, grads[1] * scale, grads[2] * scale)
```

```python
import functools
import math

import jax
import jax.numpy as jnp
from jax import lax
from jax.experimental import pallas as pl
from jax.experimental.pallas import tpu as pltpu
from jax.sharding import Mesh, PartitionSpec as P

ITERS = 3
C = 64
W = 128
LANES = 2 * W
R = 8
HALO = 6
EXT = R + 2 * HALO
SMALL = 16
Q = 16
PIECE = 32
BF = jnp.bfloat16
F32 = jnp.float32

TM = ("zh", "core")
SPACE = ("zl", "y", "x")


def roll_cols(value, step):
    if step == 0:
        return value
    lane = lax.broadcasted_iota(jnp.int32, (value.shape[0], W), 1)
    edge = 0 if step > 0 else W - 1
    halves = []
    for frame in range(2):
        half = value[:, frame * W:(frame + 1) * W]
        half = pltpu.roll(half, step % W, 1)
        halves.append(jnp.where(lane == edge, 0.0, half))
    return jnp.concatenate(halves, axis=1)


def slope_parts(value):
    logistic = 0.5 * jnp.tanh(0.5 * value) + 0.5
    return logistic, logistic * (1.0 + value * (1.0 - logistic))


def put_slot(ref, at, count, value):
    for frame in range(2):
        ref[frame, pl.ds(at, count, stride=Q), :] = value[:, frame * W:(frame + 1) * W]


def take_slot(ref, at, count):
    return jnp.concatenate(
        [ref[frame, pl.ds(at, count, stride=Q), :] for frame in range(2)], axis=1)


def put_rows(ref, at, value):
    for frame in range(2):
        ref[frame, at:at + value.shape[0], :] = value[:, frame * W:(frame + 1) * W]


def take_rows(ref, first, last):
    return jnp.concatenate([ref[frame, first:last, :] for frame in range(2)], axis=1)


def fill_shifted(field, copies, sign):
    count = field.shape[0]
    for slot, step in enumerate((-1, 0, 1)):
        shifted = roll_cols(field, sign * step)
        high = shifted.astype(BF).astype(F32)
        put_slot(copies, slot, count, high)
        put_slot(copies, 3 + slot, count, shifted - high)


def dot(left, right):
    return jnp.dot(left, right, preferred_element_type=F32)


def dot_nt(left, right):
    return lax.dot_general(left, right, (((1,), (1,)), ((), ())), preferred_element_type=F32)


def adjoint_map(first, field, gate2, gate1, third_w, second_w, first_w, copies, d2, d1, taps):
    rows = EXT - 2 * first
    fill_shifted(field, copies, 1)
    for k in range(rows - 2):
        third = dot(third_w, take_rows(copies, k * Q, (k + 3) * Q).astype(BF))
        at = first + k
        d2[k * C:(k + 1) * C, :] = (gate2[at * C:(at + 1) * C, :] * third).astype(BF)
    for k in range(rows - 4):
        parts = dot(second_w, d2[k * C:(k + 3) * C, :])
        total = (
            roll_cols(parts[:C], -1) + parts[C:2 * C] + roll_cols(parts[2 * C:], 1)
        )
        at = first + k
        row = (gate1[at * C:(at + 1) * C, :] * total).astype(BF)
        d1[k * C:(k + 1) * C, :] = row
        put_rows(taps, k * Q, dot(first_w, row))
    count = rows - 6
    result = field[3:3 + count]
    for j in (-1, 0, 1):
        column = None
        for i in (-1, 0, 1):
            tap = 3 * (i + 1) + (j + 1)
            part = take_slot(taps, (1 - i) * Q + tap, count)
            column = part if column is None else column + part
        result = result + roll_cols(column, j)
    return result


def masked_sum(masks, field):
    product = masks * field
    return product[:, :W] + product[:, W:]


def twice(field):
    return jnp.concatenate([field, field], axis=1)


def gathered_sum(ref):
    total = ref[0]
    for k in range(1, ref.shape[0]):
        total = total + ref[k]
    return total


def unpack_kernel(step, low, own, high, part, up, masks, base, small):
    pieces = ((low, 0, HALO), (own, HALO, R), (high, HALO + R, HALO))
    for ref, at, count in pieces:
        put_rows(small, at * SMALL, ref[...].astype(F32).reshape(count * SMALL, LANES))
    def channel(slot):
        return take_slot(small, slot, EXT)
    up[...] = channel(0) + channel(1)
    mask = channel(4)
    masks[...] = mask
    fixed = channel(2) + channel(3)
    pair = channel(5)
    snapshot = pair[:, :W] + pair[:, W:]
    base[...] = fixed + step * mask * twice(snapshot)
    total = masked_sum(mask, fixed)
    for k in range(part.shape[0]):
        part[k, 0:EXT, :] = total
        part[k, EXT:, :] = jnp.zeros((part.shape[1] - EXT, W), F32)


def first_kernel(step, inside, low, own, high, sums, up, masks, base, third_w, second_w, first_w,
                 forward_w, part, moved, gate2, gate1, hidden, inputs, copies, d2, d1, taps):
    before = inside[0]
    after = inside[1]
    frame_sum = gathered_sum(sums)[:EXT]
    denoiser_input = base[...] - step * masks[...] * twice(frame_sum)
    copies[...] = jnp.zeros_like(copies)
    fill_shifted(denoiser_input, copies, -1)
    inputs[...] = take_rows(copies, (HALO - 1) * Q, (HALO + R + 1) * Q).astype(BF)

    def inside_of(at):
        if at < HALO:
            return before
        if at >= HALO + R:
            return after
        return None

    for k in range(EXT - 4):
        at = k + 2
        value = dot(forward_w[...], take_rows(copies, (at - 1) * Q, (at + 2) * Q).astype(BF))
        logistic, slope = slope_parts(value)
        keep = inside_of(at)
        gate1[k * C:(k + 1) * C, :] = slope if keep is None else slope * keep
        if keep is None:
            own_at = at - HALO
            hidden[own_at * C:(own_at + 1) * C, :] = (value * logistic).astype(BF)
    for k in range(EXT - 2):
        at = k + 1
        if at < HALO:
            value = low[at]
        elif at < HALO + R:
            value = own[at - HALO]
        else:
            value = high[at - HALO - R]
        slope = slope_parts(value.astype(F32))[1]
        keep = inside_of(at)
        gate2[k * C:(k + 1) * C, :] = slope if keep is None else slope * keep
    field = adjoint_map(0, up[...], gate2, gate1, third_w[...], second_w[...], first_w[...],
                        copies, d2, d1, taps)
    finish_wide(field, before, after, masks, part, moved)


def finish_wide(field, before, after, masks, part, moved):
    count = EXT - 6
    row = lax.broadcasted_iota(jnp.int32, field.shape, 0)
    keep = jnp.where(row < HALO - 3, before, jnp.where(row >= HALO - 3 + R, after, 1.0))
    field = field * keep
    moved[...] = field
    total = masked_sum(masks[3:3 + count, :], field)
    for k in range(part.shape[0]):
        part[k, 0:count, :] = total
        part[k, count:, :] = jnp.zeros((part.shape[1] - count, W), F32)


def narrow_field(step, sums, moved, up, masks):
    count = EXT - 6
    totals = gathered_sum(sums)[:count]
    return up[3:3 + count, :] + moved[...] - step * masks[3:3 + count, :] * twice(totals)


def second_kernel(step, sums, moved, up, masks, gate2, gate1, third_w, second_w, first_w,
                  part, out, copies, d2, d1, taps):
    copies[...] = jnp.zeros_like(copies)
    field = narrow_field(step, sums, moved, up, masks)
    result = adjoint_map(3, field, gate2, gate1, third_w[...], second_w[...], first_w[...],
                         copies, d2, d1, taps)
    out[...] = result
    total = masked_sum(masks[HALO:HALO + R, :], result)
    for k in range(part.shape[0]):
        part[k] = total


def update_kernel(step, sums, moved, up, masks, out):
    totals = gathered_sum(sums)
    out[...] = (up[HALO:HALO + R, :] + moved[...]
                - step * masks[HALO:HALO + R, :] * twice(totals))


def third_kernel(inside, low, own, high, masks, gate2, gate1, third_w, second_w, first_w,
                 part, moved, copies, d2, d1, taps, whole):
    copies[...] = jnp.zeros_like(copies)
    whole[0:HALO, :] = low[R - HALO:, :]
    whole[HALO:HALO + R, :] = own[...]
    whole[HALO + R:, :] = high[:HALO, :]
    field = adjoint_map(0, whole[...], gate2, gate1, third_w[...], second_w[...], first_w[...],
                        copies, d2, d1, taps)
    finish_wide(field, inside[0], inside[1], masks, part, moved)


def last_kernel(step, sums, moved, up, masks, gate2, gate1, saved, hidden, inputs, third_w,
                second_w, first_w, adjoint, grads, copies, d2, d1, taps, total):
    copies[...] = jnp.zeros_like(copies)
    field = narrow_field(step, sums, moved, up, masks)
    adjoint[0] = field[3:3 + R, :W]
    adjoint[1] = field[3:3 + R, W:]
    result = adjoint_map(3, field, gate2, gate1, third_w[...], second_w[...], first_w[...],
                         copies, d2, d1, taps)
    snapshot = masked_sum(masks[HALO:HALO + R, :], result)
    left = []
    right = []
    left_first = []
    right_first = []
    left_third = []
    right_third = []
    for r in range(R):
        left.append(d2[(r + 1) * C:(r + 4) * C, :])
        value = hidden[r * C:(r + 1) * C, :].astype(F32)
        right.append(jnp.concatenate(
            [roll_cols(value, 1), value, roll_cols(value, -1)], axis=0).astype(BF))
        left_first.append(inputs[r * Q:(r + 3) * Q, :])
        right_first.append(d1[(r + 1) * C:(r + 2) * C, :])
        left_third.append(take_rows(copies, (r + 2) * Q, (r + 5) * Q).astype(BF))
        wide = saved[r].astype(F32)
        right_third.append((wide * slope_parts(wide)[0]).astype(BF))
    def join(parts):
        return jnp.concatenate(parts, axis=1)
    second = dot_nt(join(left), join(right))
    first = dot_nt(join(left_first), join(right_first))
    third = dot_nt(join(left_third), join(right_third))
    total[:, 0:3 * C] = second
    total[0:3 * Q, 3 * C:] = first
    total[3 * Q:6 * Q, 3 * C:] = third
    total[6 * Q:, 3 * C:] = jnp.zeros((3 * C - 6 * Q, C), F32)
    count = grads.shape[0]
    rows = 3 * C // count
    lines = R // count
    for k in range(count):
        tail = jnp.zeros((grads.shape[1] - rows, LANES), F32)
        row = lax.broadcasted_iota(jnp.int32, tail.shape, 0)
        for line in range(lines):
            one = snapshot[k * lines + line:k * lines + line + 1, :]
            tail = jnp.where(row == line, twice(one), tail)
        grads[k] = jnp.concatenate([total[k * rows:(k + 1) * rows, :], tail], axis=0).astype(BF)


def reduce_kernel(received, out):
    total = received[0].astype(F32)
    for k in range(1, received.shape[0]):
        total = total + received[k].astype(F32)
    total = total.astype(BF)
    for k in range(out.shape[0]):
        out[k] = total


def join_kernel(rows, received, mine, out):
    total = received[0].astype(F32)
    for k in range(1, received.shape[0]):
        total = total + received[k].astype(F32)
    row = lax.broadcasted_iota(jnp.int32, total.shape, 0)
    total = jnp.where(row < rows, total, mine[0].astype(F32)).astype(BF)
    for k in range(out.shape[0]):
        out[k] = total


def output_kernel(step, scale, received, snapshot, first, second, third, total):
    count = received.shape[0]
    rows = 3 * C // count
    lines = R // count
    for k in range(count):
        piece = received[k].astype(F32)
        total[k * rows:(k + 1) * rows, :] = piece[:rows] * scale
        snapshot[k * lines:(k + 1) * lines, :] = step * piece[rows:rows + lines, :W]
    for i in (-1, 0, 1):
        for j in (-1, 0, 1):
            tap = 3 * (i + 1) + (j + 1)
            back = 1 - i
            ahead = 1 + i
            second[tap] = total[back * C:(back + 1) * C, (j + 1) * C:(j + 2) * C]
            at = ahead * Q + j + 1
            first[tap:tap + 1, :] = total[at:at + 1, 3 * C:] + total[at + 3:at + 4, 3 * C:]
            at = 3 * Q + back * Q + j + 1
            third[tap:tap + 1, :] = total[at:at + 1, 3 * C:] + total[at + 3:at + 4, 3 * C:]


def call(kernel, outs, scratch, *operands, specs=None):
    grid = () if specs is None else (1,)
    if specs is None:
        specs = [pl.BlockSpec(memory_space=pltpu.VMEM)] * len(operands)
    return pl.pallas_call(
        kernel,
        grid=grid,
        out_shape=[jax.ShapeDtypeStruct(shape, dtype) for shape, dtype in outs],
        in_specs=specs,
        out_specs=[pl.BlockSpec(memory_space=pltpu.VMEM)] * len(outs),
        scratch_shapes=[pltpu.VMEM(shape, dtype) for shape, dtype in scratch],
        compiler_params=pltpu.CompilerParams(vmem_limit_bytes=40 * 2**20),
    )(*operands)


def split_parts(field):
    high = field.astype(BF)
    return high, (field - high.astype(F32)).astype(BF)


def by_row(field):
    return jnp.transpose(field, (1, 0, 2)).reshape(R, LANES)


def pad_slots(weight):
    both = jnp.concatenate([weight, weight, jnp.zeros((3, Q - 6, C), BF)], axis=1)
    return jnp.transpose(both.reshape(3 * Q, C))


def exchange(value, axis):
    return lax.all_to_all(value, axis, 0, 0, tiled=True)


def from_neighbours(value):
    count = lax.axis_size(SPACE)
    forward = [(i, i + 1) for i in range(count - 1)]
    backward = [(i + 1, i) for i in range(count - 1)]
    return forward, backward


def per_device(equilibrium, measurement, coding_masks, upstream, saved_second, conv_first,
               conv_second, conv_third):
    frames = lax.axis_size(TM)
    tiles = lax.axis_size(SPACE)
    total_frames = 2 * frames
    step = 1.0 / total_frames
    scale = 1.0 / math.sqrt(total_frames * R * tiles * W)
    forward = [(i, i + 1) for i in range(tiles - 1)]
    backward = [(i + 1, i) for i in range(tiles - 1)]
    place = lax.axis_index(SPACE)
    inside = jnp.stack([place > 0, place < tiles - 1]).astype(F32)

    saved = jnp.transpose(saved_second, (2, 1, 0, 3)).reshape(R, C, LANES)
    channels = [*split_parts(by_row(upstream)), *split_parts(by_row(equilibrium)),
                by_row(coding_masks).astype(BF),
                jnp.concatenate(split_parts(measurement), axis=1)]
    channels += [jnp.zeros((R, LANES), BF)] * (SMALL - len(channels))
    pack = jnp.concatenate([saved, jnp.stack(channels, axis=1)], axis=1)
    low = lax.ppermute(pack[R - HALO:], SPACE, forward)
    high = lax.ppermute(pack[:HALO], SPACE, backward)

    first_taps = conv_first.reshape(3, 3, C)
    forward_w = pad_slots(first_taps)
    third_w = pad_slots(conv_third.reshape(3, 3, C)[::-1])
    second_w = jnp.transpose(
        conv_second.reshape(3, 3, C, C)[::-1], (1, 3, 0, 2)).reshape(3 * C, 3 * C)
    first_w = jnp.concatenate([conv_first, jnp.zeros((Q - 9, C), BF)], axis=0)

    def rows_of(count, channels_at, width):
        return pl.BlockSpec((count, width, LANES), lambda _: (0, channels_at, 0))

    whole = pl.BlockSpec(memory_space=pltpu.VMEM)
    scalars = pl.BlockSpec(memory_space=pltpu.SMEM)
    ext = ((EXT, LANES), F32)
    part, up, masks, base = call(
        functools.partial(unpack_kernel, step),
        [((frames, 24, W), F32), ext, ext, ext],
        [((2, EXT * SMALL, W), F32)],
        low, pack, high,
        specs=[rows_of(HALO, C // SMALL, SMALL), rows_of(R, C // SMALL, SMALL),
               rows_of(HALO, C // SMALL, SMALL)])
    sums = exchange(part, TM)

    narrow = EXT - 6
    weights = (third_w, second_w, first_w)
    wide_scratch = [((2, EXT * Q, W), F32), (((EXT - 2) * C, LANES), BF),
                    (((EXT - 4) * C, LANES), BF), ((2, (EXT - 4) * Q, W), F32)]
    slim_scratch = [((2, narrow * Q, W), F32), (((narrow - 2) * C, LANES), BF),
                    (((narrow - 4) * C, LANES), BF), ((2, (narrow - 4) * Q, W), F32)]
    wide_outs = [((frames, 16, W), F32), ((narrow, LANES), F32)]
    part, moved, gate2, gate1, hidden, inputs = call(
        functools.partial(first_kernel, step),
        wide_outs + [(((EXT - 2) * C, LANES), F32), (((EXT - 4) * C, LANES), F32),
                     ((R * C, LANES), BF), (((R + 2) * Q, LANES), BF)],
        wide_scratch,
        inside, low, pack, high, sums, up, masks, base, *weights, forward_w,
        specs=[scalars, rows_of(HALO, 0, C), rows_of(R, 0, C), rows_of(HALO, 0, C)] + [whole] * 8)
    sums = exchange(part, TM)

    part, moved = call(
        functools.partial(second_kernel, step),
        [((frames, R, W), F32), ((R, LANES), F32)], slim_scratch,
        sums, moved, up, masks, gate2, gate1, *weights)
    sums = exchange(part, TM)

    field, = call(functools.partial(update_kernel, step), [((R, LANES), F32)], [],
                  sums, moved, up, masks)
    field_low = lax.ppermute(field, SPACE, forward)
    field_high = lax.ppermute(field, SPACE, backward)
    part, moved = call(
        third_kernel, wide_outs, wide_scratch + [ext],
        inside, field_low, field, field_high, masks, gate2, gate1, *weights,
        specs=[scalars] + [whole] * 9)
    sums = exchange(part, TM)

    piece = 3 * C // frames + max(8, R // frames)
    adjoint, grads = call(
        functools.partial(last_kernel, step),
        [((2, R, W), F32), ((frames, piece, LANES), BF)],
        slim_scratch + [((3 * C, LANES), F32)],
        sums, moved, up, masks, gate2, gate1, pack, hidden, inputs, *weights,
        specs=[whole] * 6 + [rows_of(R, 0, C)] + [whole] * 5)

    mine = exchange(grads, TM)
    count_y = lax.axis_size("y")
    count_near = lax.axis_size(("zl", "x"))
    mine, = call(reduce_kernel, [((count_y, piece, LANES), BF)], [], mine)
    received = exchange(mine, "y")
    received, = call(reduce_kernel, [((count_near, piece, LANES), BF)], [], received)
    received = exchange(received, ("zl", "x"))
    received, = call(functools.partial(join_kernel, 3 * C // frames),
                     [((frames, piece, LANES), BF)], [], received, mine)
    received = exchange(received, TM)
    snapshot, grad_first, grad_second, grad_third = call(
        functools.partial(output_kernel, step, scale),
        [((R, W), F32), ((9, C), F32), ((9, C, C), F32), ((9, C), F32)],
        [((3 * C, LANES), F32)], received)
    return adjoint, snapshot, grad_first, grad_second, grad_third


AXES = (("zh", 4), ("core", 2), ("zl", 2), ("y", 8), ("x", 4))


def solution(mesh, axes=AXES):
    names = tuple(name for name, _ in axes)
    sizes = tuple(size for _, size in axes)
    fine = Mesh(mesh.devices.reshape(sizes), names)
    placed = (
        P(TM, SPACE, None),
        P(SPACE, None),
        P(TM, SPACE, None),
        P(TM, SPACE, None),
        P(TM, None, SPACE, None),
        P(),
        P(),
        P(),
    )
    return jax.shard_map(
        per_device,
        mesh=fine,
        in_specs=placed,
        out_specs=(P(TM, SPACE, None), P(SPACE, None), P(), P(), P()),
        check_vma=False,
    )
```

```python
import functools
import math

import jax
import jax.numpy as jnp
from jax import lax
from jax.experimental import pallas as pl
from jax.experimental.pallas import tpu as pltpu
from jax.sharding import Mesh, PartitionSpec as P

ITERS = 3
C = 64
W = 128
LANES = 2 * W
R = 8
HALO = 6
EXT = R + 2 * HALO
SMALL = 16
Q = 16
PIECE = 32
BF = jnp.bfloat16
F32 = jnp.float32

TM = ("zh", "core")
SPACE = ("zl", "y", "x")
NEAR = ("core", "zl", "x")
FAR = ("zh", "y")


def roll_cols(value, step):
    if step == 0:
        return value
    lane = lax.broadcasted_iota(jnp.int32, (value.shape[0], W), 1)
    edge = 0 if step > 0 else W - 1
    halves = []
    for frame in range(2):
        half = value[:, frame * W:(frame + 1) * W]
        half = pltpu.roll(half, step % W, 1)
        halves.append(jnp.where(lane == edge, 0.0, half))
    return jnp.concatenate(halves, axis=1)


def slope_parts(value):
    logistic = 0.5 * jnp.tanh(0.5 * value) + 0.5
    return logistic, logistic * (1.0 + value * (1.0 - logistic))


def put_slot(ref, at, count, value):
    for frame in range(2):
        ref[frame, pl.ds(at, count, stride=Q), :] = value[:, frame * W:(frame + 1) * W]


def take_slot(ref, at, count):
    return jnp.concatenate(
        [ref[frame, pl.ds(at, count, stride=Q), :] for frame in range(2)], axis=1)


def put_rows(ref, at, value):
    for frame in range(2):
        ref[frame, at:at + value.shape[0], :] = value[:, frame * W:(frame + 1) * W]


def take_rows(ref, first, last):
    return jnp.concatenate([ref[frame, first:last, :] for frame in range(2)], axis=1)


def fill_shifted(field, copies, sign):
    count = field.shape[0]
    for slot, step in enumerate((-1, 0, 1)):
        shifted = roll_cols(field, sign * step)
        high = shifted.astype(BF).astype(F32)
        put_slot(copies, slot, count, high)
        put_slot(copies, 3 + slot, count, shifted - high)


def dot(left, right):
    return jnp.dot(left, right, preferred_element_type=F32)


def dot_nt(left, right):
    return lax.dot_general(left, right, (((1,), (1,)), ((), ())), preferred_element_type=F32)


def back_rows(first, field, gate2, third_w, second_w, copies, d2):
    rows = EXT - 2 * first
    fill_shifted(field, copies, 1)
    for k in range(rows - 2):
        third = dot(third_w, take_rows(copies, k * Q, (k + 3) * Q).astype(BF))
        at = first + k
        d2[k * C:(k + 1) * C, :] = (gate2[at * C:(at + 1) * C, :] * third).astype(BF)
    for k in range(rows - 4):
        parts = dot(second_w, d2[k * C:(k + 3) * C, :])
        total = (
            roll_cols(parts[:C], -1) + parts[C:2 * C] + roll_cols(parts[2 * C:], 1)
        )
        yield k, total


def adjoint_map(first, field, gate2, gate1, third_w, second_w, first_w, copies, d2, d1, taps):
    for k, total in back_rows(first, field, gate2, third_w, second_w, copies, d2):
        at = first + k
        row = (gate1[at * C:(at + 1) * C, :] * total).astype(BF)
        d1[k * C:(k + 1) * C, :] = row
        put_rows(taps, k * Q, dot(first_w, row))
    return map_end(first, field, taps)


def map_end(first, field, taps):
    count = EXT - 2 * first - 6
    result = field[3:3 + count]
    for j in (-1, 0, 1):
        column = None
        for i in (-1, 0, 1):
            tap = 3 * (i + 1) + (j + 1)
            part = take_slot(taps, (1 - i) * Q + tap, count)
            column = part if column is None else column + part
        result = result + roll_cols(column, j)
    return result


def masked_sum(masks, field):
    product = masks * field
    return product[:, :W] + product[:, W:]


def twice(field):
    return jnp.concatenate([field, field], axis=1)


def gathered_sum(ref):
    total = ref[0]
    for k in range(1, ref.shape[0]):
        total = total + ref[k]
    return total


def pack_kernel(upstream, equilibrium, masks, measurement, saved, out, small):
    small[...] = jnp.zeros_like(small)
    for frame in range(2):
        fields = (*split_parts(upstream[frame]), *split_parts(equilibrium[frame]),
                  masks[frame].astype(F32), split_parts(measurement[...])[frame])
        for slot, field in enumerate(fields):
            small[frame, pl.ds(slot, R, stride=SMALL), :] = field.astype(F32)
        lanes = slice(frame * W, (frame + 1) * W)
        out[:, C:, lanes] = small[frame].astype(BF).reshape(R, SMALL, W)
        out[:, :C, lanes] = jnp.swapaxes(saved[frame].astype(F32), 0, 1).astype(BF)


def weights_kernel(first, second, third, forward_w, third_w, second_w, first_w):
    forward = first[...].astype(F32)
    backward = third[...].astype(F32)
    pad = jnp.zeros((Q - 6, C), F32)
    ahead = []
    back = []
    for i in range(3):
        row = forward[3 * i:3 * i + 3]
        ahead += [row, row, pad]
        row = backward[6 - 3 * i:9 - 3 * i]
        back += [row, row, pad]
        for j in range(3):
            tile = second[3 * (2 - i) + j].astype(F32)
            second_w[j * C:(j + 1) * C, i * C:(i + 1) * C] = jnp.transpose(tile).astype(BF)
    forward_w[...] = jnp.transpose(jnp.concatenate(ahead, axis=0)).astype(BF)
    third_w[...] = jnp.transpose(jnp.concatenate(back, axis=0)).astype(BF)
    first_w[...] = jnp.concatenate([forward, jnp.zeros((Q - 9, C), F32)], axis=0).astype(BF)


def unpack_kernel(step, low, own, high, part, up, masks, base, small):
    pieces = ((low, 0, HALO), (own, HALO, R), (high, HALO + R, HALO))
    for ref, at, count in pieces:
        put_rows(small, at * SMALL, ref[...].astype(F32).reshape(count * SMALL, LANES))
    def channel(slot):
        return take_slot(small, slot, EXT)
    up[...] = channel(0) + channel(1)
    mask = channel(4)
    masks[...] = mask
    fixed = channel(2) + channel(3)
    pair = channel(5)
    snapshot = pair[:, :W] + pair[:, W:]
    base[...] = fixed + step * mask * twice(snapshot)
    total = masked_sum(mask, fixed)
    for k in range(part.shape[0]):
        part[k, 0:EXT, :] = total
        part[k, EXT:, :] = jnp.zeros((part.shape[1] - EXT, W), F32)


def keep_row(value, at, before, after):
    if at < HALO:
        return value * before
    if at >= HALO + R:
        return value * after
    return value


def early_kernel(inside, low, own, high, up, third_w, second_w, gate2, back, copies, d2):
    copies[...] = jnp.zeros_like(copies)
    for k in range(EXT - 2):
        at = k + 1
        if at < HALO:
            value = low[at]
        elif at < HALO + R:
            value = own[at - HALO]
        else:
            value = high[at - HALO - R]
        slope = slope_parts(value.astype(F32))[1]
        gate2[k * C:(k + 1) * C, :] = keep_row(slope, at, inside[0], inside[1])
    for k, total in back_rows(0, up[...], gate2, third_w[...], second_w[...], copies, d2):
        back[k * C:(k + 1) * C, :] = total


def first_kernel(step, inside, sums, up, masks, base, back, first_w, forward_w,
                 part, moved, gate1, hidden, inputs, copies, taps):
    frame_sum = gathered_sum(sums)[:EXT]
    denoiser_input = base[...] - step * masks[...] * twice(frame_sum)
    copies[...] = jnp.zeros_like(copies)
    fill_shifted(denoiser_input, copies, -1)
    inputs[...] = take_rows(copies, (HALO - 1) * Q, (HALO + R + 1) * Q).astype(BF)
    for k in range(EXT - 4):
        at = k + 2
        value = dot(forward_w[...], take_rows(copies, (at - 1) * Q, (at + 2) * Q).astype(BF))
        logistic, slope = slope_parts(value)
        slope = keep_row(slope, at, inside[0], inside[1])
        gate1[k * C:(k + 1) * C, :] = slope
        if HALO <= at < HALO + R:
            own_at = at - HALO
            hidden[own_at * C:(own_at + 1) * C, :] = (value * logistic).astype(BF)
        row = (slope * back[k * C:(k + 1) * C, :]).astype(BF)
        put_rows(taps, k * Q, dot(first_w[...], row))
    field = map_end(0, up[...], taps)
    finish_wide(field, inside[0], inside[1], masks, part, moved)


def finish_wide(field, before, after, masks, part, moved):
    count = EXT - 6
    row = lax.broadcasted_iota(jnp.int32, field.shape, 0)
    keep = jnp.where(row < HALO - 3, before, jnp.where(row >= HALO - 3 + R, after, 1.0))
    field = field * keep
    moved[...] = field
    total = masked_sum(masks[3:3 + count, :], field)
    for k in range(part.shape[0]):
        part[k, 0:count, :] = total
        part[k, count:, :] = jnp.zeros((part.shape[1] - count, W), F32)


def narrow_field(step, sums, moved, up, masks):
    count = EXT - 6
    totals = gathered_sum(sums)[:count]
    return up[3:3 + count, :] + moved[...] - step * masks[3:3 + count, :] * twice(totals)


def second_kernel(step, sums, moved, up, masks, gate2, gate1, third_w, second_w, first_w,
                  part, out, copies, d2, d1, taps):
    copies[...] = jnp.zeros_like(copies)
    field = narrow_field(step, sums, moved, up, masks)
    result = adjoint_map(3, field, gate2, gate1, third_w[...], second_w[...], first_w[...],
                         copies, d2, d1, taps)
    out[...] = result
    total = masked_sum(masks[HALO:HALO + R, :], result)
    for k in range(part.shape[0]):
        part[k] = total


def update_kernel(step, sums, moved, up, masks, out):
    totals = gathered_sum(sums)
    out[...] = (up[HALO:HALO + R, :] + moved[...]
                - step * masks[HALO:HALO + R, :] * twice(totals))


def third_kernel(inside, low, own, high, masks, gate2, gate1, third_w, second_w, first_w,
                 part, moved, copies, d2, d1, taps, whole):
    copies[...] = jnp.zeros_like(copies)
    whole[0:HALO, :] = low[R - HALO:, :]
    whole[HALO:HALO + R, :] = own[...]
    whole[HALO + R:, :] = high[:HALO, :]
    field = adjoint_map(0, whole[...], gate2, gate1, third_w[...], second_w[...], first_w[...],
                        copies, d2, d1, taps)
    finish_wide(field, inside[0], inside[1], masks, part, moved)


def last_kernel(step, sums, moved, up, masks, gate2, gate1, saved, hidden, inputs, third_w,
                second_w, first_w, adjoint, grads, copies, d2, d1, taps, total):
    copies[...] = jnp.zeros_like(copies)
    field = narrow_field(step, sums, moved, up, masks)
    adjoint[0] = field[3:3 + R, :W]
    adjoint[1] = field[3:3 + R, W:]
    result = adjoint_map(3, field, gate2, gate1, third_w[...], second_w[...], first_w[...],
                         copies, d2, d1, taps)
    snapshot = masked_sum(masks[HALO:HALO + R, :], result)
    left = []
    right = []
    left_first = []
    right_first = []
    left_third = []
    right_third = []
    for r in range(R):
        left.append(d2[(r + 1) * C:(r + 4) * C, :])
        value = hidden[r * C:(r + 1) * C, :].astype(F32)
        right.append(jnp.concatenate(
            [roll_cols(value, 1), value, roll_cols(value, -1)], axis=0).astype(BF))
        left_first.append(inputs[r * Q:(r + 3) * Q, :])
        right_first.append(d1[(r + 1) * C:(r + 2) * C, :])
        left_third.append(take_rows(copies, (r + 2) * Q, (r + 5) * Q).astype(BF))
        wide = saved[r].astype(F32)
        right_third.append((wide * slope_parts(wide)[0]).astype(BF))
    def join(parts):
        return jnp.concatenate(parts, axis=1)
    second = dot_nt(join(left), join(right))
    first = dot_nt(join(left_first), join(right_first))
    third = dot_nt(join(left_third), join(right_third))
    total[0:3 * C, 0:3 * C] = second
    total[0:3 * Q, 3 * C:] = first
    total[3 * Q:6 * Q, 3 * C:] = third
    total[6 * Q:, 3 * C:] = jnp.zeros((total.shape[0] - 6 * Q, C), F32)
    total[3 * C:, 0:3 * C] = jnp.zeros((total.shape[0] - 3 * C, 3 * C), F32)
    count = grads.shape[0]
    rows = 3 * C // count
    line = lax.broadcasted_iota(jnp.int32, grads.shape[1:], 0)
    extra = jnp.zeros(grads.shape[1:], F32)
    for k in range(R // 2):
        pair = jnp.concatenate([snapshot[2 * k:2 * k + 1], snapshot[2 * k + 1:2 * k + 2]], axis=1)
        extra = jnp.where(line == rows + k, pair, extra)
    for k in range(count):
        grads[k] = jnp.where(line < rows, total[k * rows:k * rows + grads.shape[1], :],
                             extra).astype(BF)


def reduce_pieces(rows, place, stride, received):
    count = received.shape[0]
    total = received[0].astype(F32)
    for k in range(1, count):
        total = total + received[k].astype(F32)
    extra = received[place].astype(F32)
    for k in range(1, count // stride):
        extra = extra + received[place + k * stride].astype(F32)
    line = lax.broadcasted_iota(jnp.int32, total.shape, 0)
    return jnp.where(line < rows, total, extra)


def near_kernel(rows, stride, place, received, out):
    total = reduce_pieces(rows, place[0], stride, received).astype(BF)
    for k in range(out.shape[0]):
        out[k] = total


def far_kernel(rows, stride, step, place, received, out, snapshot):
    total = reduce_pieces(rows, place[0], stride, received)
    for k in range(R // 2):
        snapshot[2 * k:2 * k + 1, :] = step * total[rows + k:rows + k + 1, :W]
        snapshot[2 * k + 1:2 * k + 2, :] = step * total[rows + k:rows + k + 1, W:]
    total = total.astype(BF)
    for k in range(out.shape[0]):
        out[k] = total


def output_kernel(scale, received, first, second, third, total):
    count = received.shape[0]
    rows = 3 * C // count
    for k in range(count):
        total[k * rows:(k + 1) * rows, :] = received[k].astype(F32)[:rows] * scale
    for i in (-1, 0, 1):
        for j in (-1, 0, 1):
            tap = 3 * (i + 1) + (j + 1)
            back = 1 - i
            ahead = 1 + i
            second[tap] = total[back * C:(back + 1) * C, (j + 1) * C:(j + 2) * C]
            at = ahead * Q + j + 1
            first[tap:tap + 1, :] = total[at:at + 1, 3 * C:] + total[at + 3:at + 4, 3 * C:]
            at = 3 * Q + back * Q + j + 1
            third[tap:tap + 1, :] = total[at:at + 1, 3 * C:] + total[at + 3:at + 4, 3 * C:]


def call(kernel, outs, scratch, *operands, specs=None, cost=None):
    grid = () if specs is None else (1,)
    if specs is None:
        specs = [pl.BlockSpec(memory_space=pltpu.VMEM)] * len(operands)
    return pl.pallas_call(
        kernel,
        grid=grid,
        out_shape=[jax.ShapeDtypeStruct(shape, dtype) for shape, dtype in outs],
        in_specs=specs,
        out_specs=[pl.BlockSpec(memory_space=pltpu.VMEM)] * len(outs),
        scratch_shapes=[pltpu.VMEM(shape, dtype) for shape, dtype in scratch],
        compiler_params=pltpu.CompilerParams(vmem_limit_bytes=40 * 2**20),
        cost_estimate=cost,
    )(*operands)


def split_parts(field):
    high = field.astype(BF)
    return high, (field - high.astype(F32)).astype(BF)


def exchange(value, axis):
    return lax.all_to_all(value, axis, 0, 0, tiled=True)


def per_device(equilibrium, measurement, coding_masks, upstream, saved_second, conv_first,
               conv_second, conv_third):
    frames = lax.axis_size(TM)
    tiles = lax.axis_size(SPACE)
    total_frames = 2 * frames
    step = 1.0 / total_frames
    scale = 1.0 / math.sqrt(total_frames * R * tiles * W)
    forward = [(i, i + 1) for i in range(tiles - 1)]
    backward = [(i + 1, i) for i in range(tiles - 1)]
    place = lax.axis_index(SPACE)
    inside = jnp.stack([place > 0, place < tiles - 1]).astype(F32)

    pack, = call(
        pack_kernel, [((R, C + SMALL, LANES), BF)], [((2, R * SMALL, W), F32)],
        upstream, equilibrium, coding_masks, measurement, saved_second)
    low = lax.ppermute(pack[R - HALO:], SPACE, forward)
    high = lax.ppermute(pack[:HALO], SPACE, backward)

    forward_w, third_w, second_w, first_w = call(
        weights_kernel,
        [((C, 3 * Q), BF), ((C, 3 * Q), BF), ((3 * C, 3 * C), BF), ((Q, C), BF)], [],
        conv_first, conv_second, conv_third,
        cost=pl.CostEstimate(flops=2 * 10**6, bytes_accessed=10**6, transcendentals=0))

    def rows_of(count, channels_at, width):
        return pl.BlockSpec((count, width, LANES), lambda _: (0, channels_at, 0))

    whole = pl.BlockSpec(memory_space=pltpu.VMEM)
    scalars = pl.BlockSpec(memory_space=pltpu.SMEM)
    ext = ((EXT, LANES), F32)
    part, up, masks, base = call(
        functools.partial(unpack_kernel, step),
        [((frames, 24, W), F32), ext, ext, ext],
        [((2, EXT * SMALL, W), F32)],
        low, pack, high,
        specs=[rows_of(HALO, C // SMALL, SMALL), rows_of(R, C // SMALL, SMALL),
               rows_of(HALO, C // SMALL, SMALL)])
    sums = exchange(part, TM)

    narrow = EXT - 6
    weights = (third_w, second_w, first_w)
    copies = ((2, EXT * Q, W), F32)
    d2 = (((EXT - 2) * C, LANES), BF)
    d1 = (((EXT - 4) * C, LANES), BF)
    taps = ((2, (EXT - 4) * Q, W), F32)
    slim_scratch = [((2, narrow * Q, W), F32), (((narrow - 2) * C, LANES), BF),
                    (((narrow - 4) * C, LANES), BF), ((2, (narrow - 4) * Q, W), F32)]
    wide_outs = [((frames, 16, W), F32), ((narrow, LANES), F32)]
    gate2, back = call(
        early_kernel,
        [(((EXT - 2) * C, LANES), F32), (((EXT - 4) * C, LANES), F32)], [copies, d2],
        inside, low, pack, high, up, third_w, second_w,
        specs=[scalars, rows_of(HALO, 0, C), rows_of(R, 0, C), rows_of(HALO, 0, C)] + [whole] * 3,
        cost=pl.CostEstimate(flops=10**9, bytes_accessed=8 * 10**6, transcendentals=3 * 10**5))
    part, moved, gate1, hidden, inputs = call(
        functools.partial(first_kernel, step),
        wide_outs + [(((EXT - 4) * C, LANES), F32), ((R * C, LANES), BF),
                     (((R + 2) * Q, LANES), BF)],
        [copies, taps],
        inside, sums, up, masks, base, back, first_w, forward_w,
        specs=[scalars] + [whole] * 7)
    sums = exchange(part, TM)

    part, moved = call(
        functools.partial(second_kernel, step),
        [((frames, R, W), F32), ((R, LANES), F32)], slim_scratch,
        sums, moved, up, masks, gate2, gate1, *weights)
    sums = exchange(part, TM)

    field, = call(functools.partial(update_kernel, step), [((R, LANES), F32)], [],
                  sums, moved, up, masks)
    field_low = lax.ppermute(field, SPACE, forward)
    field_high = lax.ppermute(field, SPACE, backward)
    part, moved = call(
        third_kernel, wide_outs, [copies, d2, d1, taps, ext],
        inside, field_low, field, field_high, masks, gate2, gate1, *weights,
        specs=[scalars] + [whole] * 9)
    sums = exchange(part, TM)

    near_sizes = [lax.axis_size(name) for name in NEAR]
    far_sizes = [lax.axis_size(name) for name in FAR]
    near_count = math.prod(near_sizes)
    far_count = math.prod(far_sizes)
    rows = 3 * C // near_count
    piece = -(-(rows + R // 2) // 16) * 16
    adjoint, grads = call(
        functools.partial(last_kernel, step),
        [((2, R, W), F32), ((near_count, piece, LANES), BF)],
        slim_scratch + [((3 * C + piece, LANES), F32)],
        sums, moved, up, masks, gate2, gate1, pack, hidden, inputs, *weights,
        specs=[whole] * 6 + [rows_of(R, 0, C)] + [whole] * 5)

    received = exchange(grads, NEAR)
    near_stride = near_count // near_sizes[0]
    near_place = lax.axis_index(NEAR[1:])[None]
    far_stride = far_count // far_sizes[0]
    far_place = lax.axis_index(FAR[1:])[None]
    received, = call(
        functools.partial(near_kernel, rows, near_stride),
        [((far_count, piece, LANES), BF)], [], near_place, received, specs=[scalars, whole])
    received = exchange(received, FAR)
    received, snapshot = call(
        functools.partial(far_kernel, rows, far_stride, step),
        [((near_count, piece, LANES), BF), ((R, W), F32)], [], far_place, received,
        specs=[scalars, whole])
    received = exchange(received, NEAR)
    grad_first, grad_second, grad_third = call(
        functools.partial(output_kernel, scale),
        [((9, C), F32), ((9, C, C), F32), ((9, C), F32)],
        [((3 * C, LANES), F32)], received)
    return adjoint, snapshot, grad_first, grad_second, grad_third


AXES = (("zh", 4), ("core", 2), ("zl", 2), ("y", 8), ("x", 4))


def solution(mesh, axes=AXES):
    names = tuple(name for name, _ in axes)
    sizes = tuple(size for _, size in axes)
    fine = Mesh(mesh.devices.reshape(sizes), names)
    placed = (
        P(TM, SPACE, None),
        P(SPACE, None),
        P(TM, SPACE, None),
        P(TM, SPACE, None),
        P(TM, None, SPACE, None),
        P(),
        P(),
        P(),
    )
    return jax.shard_map(
        per_device,
        mesh=fine,
        in_specs=placed,
        out_specs=(P(TM, SPACE, None), P(SPACE, None), P(), P(), P()),
        check_vma=False,
    )
```

```python
import functools
import math

import jax
import jax.numpy as jnp
from jax import lax
from jax.experimental import pallas as pl
from jax.experimental.pallas import tpu as pltpu
from jax.sharding import Mesh, PartitionSpec as P

ITERS = 3
C = 64
W = 128
LANES = 2 * W
R = 8
HALO = 6
EXT = R + 2 * HALO
SMALL = 16
Q = 16
PIECE = 32
BF = jnp.bfloat16
F32 = jnp.float32

TM = ("zh", "core")
SPACE = ("zl", "y", "x")
NEAR = ("core", "zl", "x")
FAR = ("zh", "y")


def roll_cols(value, step):
    if step == 0:
        return value
    lane = lax.broadcasted_iota(jnp.int32, (value.shape[0], W), 1)
    edge = 0 if step > 0 else W - 1
    halves = []
    for frame in range(2):
        half = value[:, frame * W:(frame + 1) * W]
        half = pltpu.roll(half, step % W, 1)
        halves.append(jnp.where(lane == edge, 0.0, half))
    return jnp.concatenate(halves, axis=1)


def slope_parts(value):
    logistic = 0.5 * jnp.tanh(0.5 * value) + 0.5
    return logistic, logistic * (1.0 + value * (1.0 - logistic))


def put_slot(ref, at, count, value):
    for frame in range(2):
        ref[frame, pl.ds(at, count, stride=Q), :] = value[:, frame * W:(frame + 1) * W]


def take_slot(ref, at, count):
    return jnp.concatenate(
        [ref[frame, pl.ds(at, count, stride=Q), :] for frame in range(2)], axis=1)


def put_rows(ref, at, value):
    for frame in range(2):
        ref[frame, at:at + value.shape[0], :] = value[:, frame * W:(frame + 1) * W]


def take_rows(ref, first, last):
    return jnp.concatenate([ref[frame, first:last, :] for frame in range(2)], axis=1)


def fill_shifted(field, copies, sign):
    count = field.shape[0]
    for slot, step in enumerate((-1, 0, 1)):
        shifted = roll_cols(field, sign * step)
        high = shifted.astype(BF).astype(F32)
        put_slot(copies, slot, count, high)
        put_slot(copies, 3 + slot, count, shifted - high)


def dot(left, right):
    return jnp.dot(left, right, preferred_element_type=F32)


def dot_nt(left, right):
    return lax.dot_general(left, right, (((1,), (1,)), ((), ())), preferred_element_type=F32)


def back_rows(first, field, gate2, third_w, second_w, copies, d2):
    rows = EXT - 2 * first
    fill_shifted(field, copies, 1)
    for k in range(rows - 2):
        third = dot(third_w, take_rows(copies, k * Q, (k + 3) * Q).astype(BF))
        at = first + k
        d2[k * C:(k + 1) * C, :] = (gate2[at * C:(at + 1) * C, :] * third).astype(BF)
    for k in range(rows - 4):
        parts = dot(second_w, d2[k * C:(k + 3) * C, :])
        total = (
            roll_cols(parts[:C], -1) + parts[C:2 * C] + roll_cols(parts[2 * C:], 1)
        )
        yield k, total


def adjoint_map(first, field, gate2, gate1, third_w, second_w, first_w, copies, d2, d1, taps):
    for k, total in back_rows(first, field, gate2, third_w, second_w, copies, d2):
        at = first + k
        row = (gate1[at * C:(at + 1) * C, :] * total).astype(BF)
        d1[k * C:(k + 1) * C, :] = row
    return map_end(first, field, first_w, d1, taps)


def map_end(first, field, first_w, d1, taps):
    count = EXT - 2 * first - 6
    for k in range(count + 2):
        put_rows(taps, k * Q, dot(first_w, d1[k * C:(k + 1) * C, :]))
    result = field[3:3 + count]
    for j in (-1, 0, 1):
        column = None
        for i in (-1, 0, 1):
            tap = 3 * (i + 1) + (j + 1)
            part = take_slot(taps, (1 - i) * Q + tap, count)
            column = part if column is None else column + part
        result = result + roll_cols(column, j)
    return result


def masked_sum(masks, field):
    product = masks * field
    return product[:, :W] + product[:, W:]


def twice(field):
    return jnp.concatenate([field, field], axis=1)


def gathered_sum(ref):
    total = ref[0]
    for k in range(1, ref.shape[0]):
        total = total + ref[k]
    return total


def pack_kernel(upstream, equilibrium, masks, measurement, saved, out, top, bottom, small):
    small[...] = jnp.zeros_like(small)
    for frame in range(2):
        fields = (*split_parts(upstream[frame]), *split_parts(equilibrium[frame]),
                  masks[frame].astype(F32), split_parts(measurement[...])[frame])
        for slot, field in enumerate(fields):
            small[frame, pl.ds(slot, R, stride=SMALL), :] = field.astype(F32)
        lanes = slice(frame * W, (frame + 1) * W)
        out[:, C:, lanes] = small[frame].astype(BF).reshape(R, SMALL, W)
        out[:, :C, lanes] = jnp.swapaxes(saved[frame].astype(F32), 0, 1).astype(BF)
    top[...] = out[:HALO]
    bottom[...] = out[R - HALO:]


def weights_kernel(first, second, third, forward_w, third_w, second_w, first_w):
    forward = first[...].astype(F32)
    backward = third[...].astype(F32)
    pad = jnp.zeros((Q - 6, C), F32)
    ahead = []
    back = []
    for i in range(3):
        row = forward[3 * i:3 * i + 3]
        ahead += [row, row, pad]
        row = backward[6 - 3 * i:9 - 3 * i]
        back += [row, row, pad]
        for j in range(3):
            tile = second[3 * (2 - i) + j].astype(F32)
            second_w[j * C:(j + 1) * C, i * C:(i + 1) * C] = jnp.transpose(tile).astype(BF)
    forward_w[...] = jnp.transpose(jnp.concatenate(ahead, axis=0)).astype(BF)
    third_w[...] = jnp.transpose(jnp.concatenate(back, axis=0)).astype(BF)
    first_w[...] = jnp.concatenate([forward, jnp.zeros((Q - 9, C), F32)], axis=0).astype(BF)


def unpack_kernel(step, low, own, high, part, up, masks, base, small):
    pieces = ((low, 0, HALO), (own, HALO, R), (high, HALO + R, HALO))
    for ref, at, count in pieces:
        put_rows(small, at * SMALL, ref[...].astype(F32).reshape(count * SMALL, LANES))
    def channel(slot):
        return take_slot(small, slot, EXT)
    up[...] = channel(0) + channel(1)
    mask = channel(4)
    masks[...] = mask
    fixed = channel(2) + channel(3)
    pair = channel(5)
    snapshot = pair[:, :W] + pair[:, W:]
    base[...] = fixed + step * mask * twice(snapshot)
    total = masked_sum(mask, fixed)
    for k in range(part.shape[0]):
        part[k, 0:EXT, :] = total
        part[k, EXT:, :] = jnp.zeros((part.shape[1] - EXT, W), F32)


def keep_row(value, at, before, after):
    if at < HALO:
        return value * before
    if at >= HALO + R:
        return value * after
    return value


def early_kernel(inside, low, own, high, up, third_w, second_w, gate2, back, copies, d2):
    copies[...] = jnp.zeros_like(copies)
    for k in range(EXT - 2):
        at = k + 1
        if at < HALO:
            value = low[at]
        elif at < HALO + R:
            value = own[at - HALO]
        else:
            value = high[at - HALO - R]
        slope = slope_parts(value.astype(F32))[1]
        gate2[k * C:(k + 1) * C, :] = keep_row(slope, at, inside[0], inside[1])
    for k, total in back_rows(0, up[...], gate2, third_w[...], second_w[...], copies, d2):
        back[k * C:(k + 1) * C, :] = total


def first_kernel(step, inside, sums, up, masks, base, back, first_w, forward_w,
                 part, moved, gate1, hidden, inputs, copies, d1, taps):
    frame_sum = gathered_sum(sums)[:EXT]
    denoiser_input = base[...] - step * masks[...] * twice(frame_sum)
    copies[...] = jnp.zeros_like(copies)
    fill_shifted(denoiser_input, copies, -1)
    inputs[...] = take_rows(copies, (HALO - 1) * Q, (HALO + R + 1) * Q).astype(BF)
    for k in range(EXT - 4):
        at = k + 2
        value = dot(forward_w[...], take_rows(copies, (at - 1) * Q, (at + 2) * Q).astype(BF))
        logistic, slope = slope_parts(value)
        slope = keep_row(slope, at, inside[0], inside[1])
        gate1[k * C:(k + 1) * C, :] = slope
        if HALO <= at < HALO + R:
            own_at = at - HALO
            hidden[own_at * C:(own_at + 1) * C, :] = (value * logistic).astype(BF)
        d1[k * C:(k + 1) * C, :] = (slope * back[k * C:(k + 1) * C, :]).astype(BF)
    field = map_end(0, up[...], first_w[...], d1, taps)
    finish_wide(field, inside[0], inside[1], masks, part, moved)


def finish_wide(field, before, after, masks, part, moved):
    count = EXT - 6
    row = lax.broadcasted_iota(jnp.int32, field.shape, 0)
    keep = jnp.where(row < HALO - 3, before, jnp.where(row >= HALO - 3 + R, after, 1.0))
    field = field * keep
    moved[...] = field
    total = masked_sum(masks[3:3 + count, :], field)
    for k in range(part.shape[0]):
        part[k, 0:count, :] = total
        part[k, count:, :] = jnp.zeros((part.shape[1] - count, W), F32)


def narrow_field(step, sums, moved, up, masks):
    count = EXT - 6
    totals = gathered_sum(sums)[:count]
    return up[3:3 + count, :] + moved[...] - step * masks[3:3 + count, :] * twice(totals)


def second_kernel(step, sums, moved, up, masks, gate2, gate1, third_w, second_w, first_w,
                  part, out, copies, d2, d1, taps):
    copies[...] = jnp.zeros_like(copies)
    field = narrow_field(step, sums, moved, up, masks)
    result = adjoint_map(3, field, gate2, gate1, third_w[...], second_w[...], first_w[...],
                         copies, d2, d1, taps)
    out[...] = result
    total = masked_sum(masks[HALO:HALO + R, :], result)
    for k in range(part.shape[0]):
        part[k] = total


def update_kernel(step, sums, moved, up, masks, out):
    totals = gathered_sum(sums)
    out[...] = (up[HALO:HALO + R, :] + moved[...]
                - step * masks[HALO:HALO + R, :] * twice(totals))


def third_kernel(inside, low, own, high, masks, gate2, gate1, third_w, second_w, first_w,
                 part, moved, copies, d2, d1, taps, whole):
    copies[...] = jnp.zeros_like(copies)
    whole[0:HALO, :] = low[R - HALO:, :]
    whole[HALO:HALO + R, :] = own[...]
    whole[HALO + R:, :] = high[:HALO, :]
    field = adjoint_map(0, whole[...], gate2, gate1, third_w[...], second_w[...], first_w[...],
                        copies, d2, d1, taps)
    finish_wide(field, inside[0], inside[1], masks, part, moved)


def last_kernel(step, sums, moved, up, masks, gate2, gate1, saved, hidden, inputs, third_w,
                second_w, first_w, adjoint, grads, copies, d2, d1, taps, total):
    copies[...] = jnp.zeros_like(copies)
    field = narrow_field(step, sums, moved, up, masks)
    adjoint[0] = field[3:3 + R, :W]
    adjoint[1] = field[3:3 + R, W:]
    result = adjoint_map(3, field, gate2, gate1, third_w[...], second_w[...], first_w[...],
                         copies, d2, d1, taps)
    snapshot = masked_sum(masks[HALO:HALO + R, :], result)
    left = []
    right = []
    left_first = []
    right_first = []
    left_third = []
    right_third = []
    for r in range(R):
        left.append(d2[(r + 1) * C:(r + 4) * C, :])
        value = hidden[r * C:(r + 1) * C, :].astype(F32)
        right.append(jnp.concatenate(
            [roll_cols(value, 1), value, roll_cols(value, -1)], axis=0).astype(BF))
        left_first.append(inputs[r * Q:(r + 3) * Q, :])
        right_first.append(d1[(r + 1) * C:(r + 2) * C, :])
        left_third.append(take_rows(copies, (r + 2) * Q, (r + 5) * Q).astype(BF))
        wide = saved[r].astype(F32)
        right_third.append((wide * slope_parts(wide)[0]).astype(BF))
    def join(parts):
        return jnp.concatenate(parts, axis=1)
    second = dot_nt(join(left), join(right))
    first = dot_nt(join(left_first), join(right_first))
    third = dot_nt(join(left_third), join(right_third))
    total[0:3 * C, 0:3 * C] = second
    total[0:3 * Q, 3 * C:] = first
    total[3 * Q:6 * Q, 3 * C:] = third
    total[6 * Q:, 3 * C:] = jnp.zeros((total.shape[0] - 6 * Q, C), F32)
    total[3 * C:, 0:3 * C] = jnp.zeros((total.shape[0] - 3 * C, 3 * C), F32)
    count = grads.shape[0]
    rows = 3 * C // count
    line = lax.broadcasted_iota(jnp.int32, grads.shape[1:], 0)
    extra = jnp.zeros(grads.shape[1:], F32)
    for k in range(R // 2):
        pair = jnp.concatenate([snapshot[2 * k:2 * k + 1], snapshot[2 * k + 1:2 * k + 2]], axis=1)
        extra = jnp.where(line == rows + k, pair, extra)
    for k in range(count):
        grads[k] = jnp.where(line < rows, total[k * rows:k * rows + grads.shape[1], :],
                             extra).astype(BF)


def reduce_pieces(rows, place, stride, received):
    count = received.shape[0]
    total = received[0].astype(F32)
    for k in range(1, count):
        total = total + received[k].astype(F32)
    extra = received[place].astype(F32)
    for k in range(1, count // stride):
        extra = extra + received[place + k * stride].astype(F32)
    line = lax.broadcasted_iota(jnp.int32, total.shape, 0)
    return jnp.where(line < rows, total, extra)


def near_kernel(rows, stride, place, received, out):
    total = reduce_pieces(rows, place[0], stride, received).astype(BF)
    for k in range(out.shape[0]):
        out[k] = total


def far_kernel(rows, stride, step, place, received, out, snapshot):
    total = reduce_pieces(rows, place[0], stride, received)
    for k in range(R // 2):
        snapshot[2 * k:2 * k + 1, :] = step * total[rows + k:rows + k + 1, :W]
        snapshot[2 * k + 1:2 * k + 2, :] = step * total[rows + k:rows + k + 1, W:]
    total = total.astype(BF)
    for k in range(out.shape[0]):
        out[k] = total


def output_kernel(scale, received, first, second, third, total):
    count = received.shape[0]
    rows = 3 * C // count
    for k in range(count):
        total[k * rows:(k + 1) * rows, :] = received[k].astype(F32)[:rows] * scale
    for i in (-1, 0, 1):
        for j in (-1, 0, 1):
            tap = 3 * (i + 1) + (j + 1)
            back = 1 - i
            ahead = 1 + i
            second[tap] = total[back * C:(back + 1) * C, (j + 1) * C:(j + 2) * C]
            at = ahead * Q + j + 1
            first[tap:tap + 1, :] = total[at:at + 1, 3 * C:] + total[at + 3:at + 4, 3 * C:]
            at = 3 * Q + back * Q + j + 1
            third[tap:tap + 1, :] = total[at:at + 1, 3 * C:] + total[at + 3:at + 4, 3 * C:]


def call(kernel, outs, scratch, *operands, specs=None, cost=None, limit=40):
    grid = () if specs is None else (1,)
    if specs is None:
        specs = [pl.BlockSpec(memory_space=pltpu.VMEM)] * len(operands)
    return pl.pallas_call(
        kernel,
        grid=grid,
        out_shape=[jax.ShapeDtypeStruct(shape, dtype) for shape, dtype in outs],
        in_specs=specs,
        out_specs=[pl.BlockSpec(memory_space=pltpu.VMEM)] * len(outs),
        scratch_shapes=[pltpu.VMEM(shape, dtype) for shape, dtype in scratch],
        compiler_params=pltpu.CompilerParams(vmem_limit_bytes=limit * 2**20),
        cost_estimate=cost,
    )(*operands)


def full_block(*shape):
    return pl.BlockSpec(shape, lambda _: (0,) * len(shape))


def split_parts(field):
    high = field.astype(BF)
    return high, (field - high.astype(F32)).astype(BF)


def exchange(value, axis):
    return lax.all_to_all(value, axis, 0, 0, tiled=True)


def per_device(equilibrium, measurement, coding_masks, upstream, saved_second, conv_first,
               conv_second, conv_third):
    frames = lax.axis_size(TM)
    tiles = lax.axis_size(SPACE)
    total_frames = 2 * frames
    step = 1.0 / total_frames
    scale = 1.0 / math.sqrt(total_frames * R * tiles * W)
    forward = [(i, i + 1) for i in range(tiles - 1)]
    backward = [(i + 1, i) for i in range(tiles - 1)]
    place = lax.axis_index(SPACE)
    inside = jnp.stack([place > 0, place < tiles - 1]).astype(F32)

    edge = ((HALO, C + SMALL, LANES), BF)
    pack, top, bottom = call(
        pack_kernel, [((R, C + SMALL, LANES), BF), edge, edge], [((2, R * SMALL, W), F32)],
        upstream, equilibrium, coding_masks, measurement, saved_second,
        specs=[full_block(2, R, W)] * 3 + [full_block(R, W), full_block(2, C, R, W)], limit=60)
    low = lax.ppermute(bottom, SPACE, forward)
    high = lax.ppermute(top, SPACE, backward)

    forward_w, third_w, second_w, first_w = call(
        weights_kernel,
        [((C, 3 * Q), BF), ((C, 3 * Q), BF), ((3 * C, 3 * C), BF), ((Q, C), BF)], [],
        conv_first, conv_second, conv_third,
        specs=[full_block(9, C), full_block(9, C, C), full_block(9, C)],
        cost=pl.CostEstimate(flops=2 * 10**6, bytes_accessed=10**6, transcendentals=0))

    def rows_of(count, channels_at, width):
        return pl.BlockSpec((count, width, LANES), lambda _: (0, channels_at, 0))

    whole = pl.BlockSpec(memory_space=pltpu.VMEM)
    scalars = pl.BlockSpec(memory_space=pltpu.SMEM)
    ext = ((EXT, LANES), F32)
    part, up, masks, base = call(
        functools.partial(unpack_kernel, step),
        [((frames, 24, W), F32), ext, ext, ext],
        [((2, EXT * SMALL, W), F32)],
        low, pack, high,
        specs=[rows_of(HALO, C // SMALL, SMALL), rows_of(R, C // SMALL, SMALL),
               rows_of(HALO, C // SMALL, SMALL)])
    sums = exchange(part, TM)

    narrow = EXT - 6
    weights = (third_w, second_w, first_w)
    copies = ((2, EXT * Q, W), F32)
    d2 = (((EXT - 2) * C, LANES), BF)
    d1 = (((EXT - 4) * C, LANES), BF)
    taps = ((2, (EXT - 4) * Q, W), F32)
    slim_scratch = [((2, narrow * Q, W), F32), (((narrow - 2) * C, LANES), BF),
                    (((narrow - 4) * C, LANES), BF), ((2, (narrow - 4) * Q, W), F32)]
    wide_outs = [((frames, 16, W), F32), ((narrow, LANES), F32)]
    gate2, back = call(
        early_kernel,
        [(((EXT - 2) * C, LANES), F32), (((EXT - 4) * C, LANES), F32)], [copies, d2],
        inside, low, pack, high, up, third_w, second_w,
        specs=[scalars, rows_of(HALO, 0, C), rows_of(R, 0, C), rows_of(HALO, 0, C)] + [whole] * 3,
        cost=pl.CostEstimate(flops=10**9, bytes_accessed=8 * 10**6, transcendentals=3 * 10**5))
    part, moved, gate1, hidden, inputs = call(
        functools.partial(first_kernel, step),
        wide_outs + [(((EXT - 4) * C, LANES), F32), ((R * C, LANES), BF),
                     (((R + 2) * Q, LANES), BF)],
        [copies, d1, taps],
        inside, sums, up, masks, base, back, first_w, forward_w,
        specs=[scalars] + [whole] * 7)
    sums = exchange(part, TM)

    part, moved = call(
        functools.partial(second_kernel, step),
        [((frames, R, W), F32), ((R, LANES), F32)], slim_scratch,
        sums, moved, up, masks, gate2, gate1, *weights)
    sums = exchange(part, TM)

    field, = call(functools.partial(update_kernel, step), [((R, LANES), F32)], [],
                  sums, moved, up, masks)
    field_low = lax.ppermute(field, SPACE, forward)
    field_high = lax.ppermute(field, SPACE, backward)
    part, moved = call(
        third_kernel, wide_outs, [copies, d2, d1, taps, ext],
        inside, field_low, field, field_high, masks, gate2, gate1, *weights,
        specs=[scalars] + [whole] * 9)
    sums = exchange(part, TM)

    near_sizes = [lax.axis_size(name) for name in NEAR]
    far_sizes = [lax.axis_size(name) for name in FAR]
    near_count = math.prod(near_sizes)
    far_count = math.prod(far_sizes)
    rows = 3 * C // near_count
    piece = -(-(rows + R // 2) // 16) * 16
    adjoint, grads = call(
        functools.partial(last_kernel, step),
        [((2, R, W), F32), ((near_count, piece, LANES), BF)],
        slim_scratch + [((3 * C + piece, LANES), F32)],
        sums, moved, up, masks, gate2, gate1, pack, hidden, inputs, *weights,
        specs=[whole] * 6 + [rows_of(R, 0, C)] + [whole] * 5)

    received = exchange(grads, NEAR)
    near_stride = near_count // near_sizes[0]
    near_place = lax.axis_index(NEAR[1:])[None]
    far_stride = far_count // far_sizes[0]
    far_place = lax.axis_index(FAR[1:])[None]
    received, = call(
        functools.partial(near_kernel, rows, near_stride),
        [((far_count, piece, LANES), BF)], [], near_place, received, specs=[scalars, whole])
    received = exchange(received, FAR)
    received, snapshot = call(
        functools.partial(far_kernel, rows, far_stride, step),
        [((near_count, piece, LANES), BF), ((R, W), F32)], [], far_place, received,
        specs=[scalars, whole])
    received = exchange(received, NEAR)
    grad_first, grad_second, grad_third = call(
        functools.partial(output_kernel, scale),
        [((9, C), F32), ((9, C, C), F32), ((9, C), F32)],
        [((3 * C, LANES), F32)], received)
    return adjoint, snapshot, grad_first, grad_second, grad_third


AXES = (("zh", 4), ("core", 2), ("zl", 2), ("y", 8), ("x", 4))


def solution(mesh, axes=AXES):
    names = tuple(name for name, _ in axes)
    sizes = tuple(size for _, size in axes)
    fine = Mesh(mesh.devices.reshape(sizes), names)
    placed = (
        P(TM, SPACE, None),
        P(SPACE, None),
        P(TM, SPACE, None),
        P(TM, SPACE, None),
        P(TM, None, SPACE, None),
        P(),
        P(),
        P(),
    )
    return jax.shard_map(
        per_device,
        mesh=fine,
        in_specs=placed,
        out_specs=(P(TM, SPACE, None), P(SPACE, None), P(), P(), P()),
        check_vma=False,
    )
```

```python
import functools
import math

import jax
import jax.numpy as jnp
from jax import lax
from jax.experimental import pallas as pl
from jax.experimental.pallas import tpu as pltpu
from jax.sharding import Mesh, PartitionSpec as P

ITERS = 3
C = 64
W = 128
LANES = 2 * W
R = 8
HALO = 6
EXT = R + 2 * HALO
EDGE = HALO - 1
FIELDS = 6
Q = 16
PIECE = 32
BF = jnp.bfloat16
F32 = jnp.float32

TM = ("zh", "core")
SPACE = ("zl", "y", "x")
NEAR = ("core", "zl", "x")
FAR = ("zh", "y")


def roll_cols(value, step):
    if step == 0:
        return value
    lane = lax.broadcasted_iota(jnp.int32, (value.shape[0], W), 1)
    edge = 0 if step > 0 else W - 1
    halves = []
    for frame in range(2):
        half = value[:, frame * W:(frame + 1) * W]
        half = pltpu.roll(half, step % W, 1)
        halves.append(jnp.where(lane == edge, 0.0, half))
    return jnp.concatenate(halves, axis=1)


def slope_parts(value):
    logistic = 0.5 * jnp.tanh(0.5 * value) + 0.5
    return logistic, logistic * (1.0 + value * (1.0 - logistic))


def put_slot(ref, at, count, value):
    for frame in range(2):
        ref[frame, pl.ds(at, count, stride=Q), :] = value[:, frame * W:(frame + 1) * W]


def take_slot(ref, at, count):
    return jnp.concatenate(
        [ref[frame, pl.ds(at, count, stride=Q), :] for frame in range(2)], axis=1)


def put_rows(ref, at, value):
    for frame in range(2):
        ref[frame, at:at + value.shape[0], :] = value[:, frame * W:(frame + 1) * W]


def take_rows(ref, first, last):
    return jnp.concatenate([ref[frame, first:last, :] for frame in range(2)], axis=1)


def fill_shifted(field, copies, sign):
    count = field.shape[0]
    for slot, step in enumerate((-1, 0, 1)):
        shifted = roll_cols(field, sign * step)
        high = shifted.astype(BF).astype(F32)
        put_slot(copies, slot, count, high)
        put_slot(copies, 3 + slot, count, shifted - high)


def dot(left, right):
    return jnp.dot(left, right, preferred_element_type=F32)


def dot_nt(left, right):
    return lax.dot_general(left, right, (((1,), (1,)), ((), ())), preferred_element_type=F32)


def back_rows(first, field, gate2, third_w, second_w, copies, d2):
    rows = EXT - 2 * first
    fill_shifted(field, copies, 1)
    for k in range(rows - 2):
        third = dot(third_w, take_rows(copies, k * Q, (k + 3) * Q).astype(BF))
        at = first + k
        d2[k * C:(k + 1) * C, :] = (gate2[at * C:(at + 1) * C, :] * third).astype(BF)
    for k in range(rows - 4):
        parts = dot(second_w, d2[k * C:(k + 3) * C, :])
        total = (
            roll_cols(parts[:C], -1) + parts[C:2 * C] + roll_cols(parts[2 * C:], 1)
        )
        yield k, total


def adjoint_map(first, field, gate2, gate1, third_w, second_w, first_w, copies, d2, d1, taps):
    for k, total in back_rows(first, field, gate2, third_w, second_w, copies, d2):
        at = first + k
        row = (gate1[at * C:(at + 1) * C, :] * total).astype(BF)
        d1[k * C:(k + 1) * C, :] = row
    return map_end(first, field, first_w, d1, taps)


def map_end(first, field, first_w, d1, taps):
    count = EXT - 2 * first - 6
    for k in range(count + 2):
        put_rows(taps, k * Q, dot(first_w, d1[k * C:(k + 1) * C, :]))
    result = field[3:3 + count]
    for j in (-1, 0, 1):
        column = None
        for i in (-1, 0, 1):
            tap = 3 * (i + 1) + (j + 1)
            part = take_slot(taps, (1 - i) * Q + tap, count)
            column = part if column is None else column + part
        result = result + roll_cols(column, j)
    return result


def masked_sum(masks, field):
    product = masks * field
    return product[:, :W] + product[:, W:]


def twice(field):
    return jnp.concatenate([field, field], axis=1)


def gathered_sum(ref):
    total = ref[0]
    for k in range(1, ref.shape[0]):
        total = total + ref[k]
    return total


def pack_kernel(upstream, equilibrium, masks, measurement, saved, out, top, bottom, own_fields,
                up_in, fixed_in, masks_in, snapshot_in, saved_in, sems):
    copies = [
        pltpu.make_async_copy(source, target, sems.at[k])
        for k, (source, target) in enumerate((
            (saved, saved_in), (upstream, up_in), (equilibrium, fixed_in), (masks, masks_in),
            (measurement, snapshot_in)))
    ]
    for copy in copies:
        copy.start()
    for copy in copies[1:]:
        copy.wait()

    def by_frame(ref):
        return jnp.concatenate([ref[0], ref[1]], axis=1)

    up = by_frame(up_in)
    fixed = by_frame(fixed_in)
    mask = by_frame(masks_in).astype(F32)
    snapshot = snapshot_in[...]
    for k, field in enumerate((up, mask, fixed, twice(snapshot))):
        own_fields[k * R:(k + 1) * R, :] = field
    fields = (*split_parts(up), *split_parts(fixed), mask.astype(BF),
              jnp.concatenate(split_parts(snapshot), axis=1))
    for k in range(0, len(fields), 2):
        pair = jnp.concatenate([field.astype(F32) for field in fields[k:k + 2]], axis=0).astype(BF)
        at = EDGE * C + k * R
        top[at:at + 2 * R, :] = pair
        bottom[at:at + 2 * R, :] = pair
    copies[0].wait()
    for frame in range(2):
        lanes = slice(frame * W, (frame + 1) * W)
        rows = jnp.swapaxes(saved_in[frame].astype(F32), 0, 1).astype(BF).reshape(R * C, W)
        out[:, lanes] = rows
        top[:EDGE * C, lanes] = rows[:EDGE * C]
        bottom[:EDGE * C, lanes] = rows[(R - EDGE) * C:]


def stage_kernel(first, second, third, saved, own_fields, forward_w, third_w, second_w, first_w,
                 gate2, hidden2, fields):
    fields[...] = own_fields[...]
    for r in range(R):
        value = saved_row(saved, r).astype(F32)
        logistic, slope = slope_parts(value)
        gate2[r * C:(r + 1) * C, :] = slope
        hidden2[r * C:(r + 1) * C, :] = (value * logistic).astype(BF)
    forward = first[...].astype(F32)
    backward = third[...].astype(F32)
    pad = jnp.zeros((Q - 6, C), F32)
    ahead = []
    back = []
    for i in range(3):
        row = forward[3 * i:3 * i + 3]
        ahead += [row, row, pad]
        row = backward[6 - 3 * i:9 - 3 * i]
        back += [row, row, pad]
        for j in range(3):
            tile = second[3 * (2 - i) + j].astype(F32)
            second_w[j * C:(j + 1) * C, i * C:(i + 1) * C] = jnp.transpose(tile).astype(BF)
    forward_w[...] = jnp.transpose(jnp.concatenate(ahead, axis=0)).astype(BF)
    third_w[...] = jnp.transpose(jnp.concatenate(back, axis=0)).astype(BF)
    first_w[...] = jnp.concatenate([forward, jnp.zeros((Q - 9, C), F32)], axis=0).astype(BF)


def unpack_kernel(step, low, own_fields, high, part, up, masks, base, fixed, snapshot):
    for k, target in enumerate((up, masks, fixed, snapshot)):
        target[HALO:HALO + R, :] = own_fields[k * R:(k + 1) * R, :]
    for ref, at, first in ((low, 0, R - HALO), (high, HALO + R, 0)):
        fields = ref[EDGE * C:EDGE * C + FIELDS * R, :].astype(F32)

        def field(k):
            return fields[k * R:(k + 1) * R]

        for target, value in ((up, field(0) + field(1)), (fixed, field(2) + field(3)),
                              (masks, field(4)),
                              (snapshot, twice(field(5)[:, :W] + field(5)[:, W:]))):
            target[at:at + HALO, :] = value[first:first + HALO]
    total = masked_sum(masks[...], fixed[...])
    for k in range(part.shape[0]):
        part[k, 0:EXT, :] = total
        part[k, EXT:, :] = jnp.zeros((part.shape[1] - EXT, W), F32)
    base[...] = fixed[...] + step * masks[...] * snapshot[...]


def saved_row(ref, at):
    return ref[at * C:(at + 1) * C, :]


def keep_row(value, at, before, after):
    if at < HALO:
        return value * before
    if at >= HALO + R:
        return value * after
    return value


def early_kernel(inside, low, own, high, up, third_w, second_w, gate2, back, copies, d2):
    copies[...] = jnp.zeros_like(copies)
    for k in range(EXT - 2):
        at = k + 1
        if HALO <= at < HALO + R:
            gate2[k * C:(k + 1) * C, :] = saved_row(own, at - HALO)
        else:
            value = saved_row(low, k) if at < HALO else saved_row(high, at - HALO - R)
            slope = slope_parts(value.astype(F32))[1]
            gate2[k * C:(k + 1) * C, :] = keep_row(slope, at, inside[0], inside[1])
    for k, total in back_rows(0, up[...], gate2, third_w[...], second_w[...], copies, d2):
        back[k * C:(k + 1) * C, :] = total


def first_kernel(step, inside, sums, up, masks, base, back, first_w, forward_w,
                 part, moved, gate1, hidden, inputs, copies, d1, taps):
    frame_sum = gathered_sum(sums)[:EXT]
    denoiser_input = base[...] - step * masks[...] * twice(frame_sum)
    copies[...] = jnp.zeros_like(copies)
    fill_shifted(denoiser_input, copies, -1)
    inputs[...] = take_rows(copies, (HALO - 1) * Q, (HALO + R + 1) * Q).astype(BF)
    for k in range(EXT - 4):
        at = k + 2
        value = dot(forward_w[...], take_rows(copies, (at - 1) * Q, (at + 2) * Q).astype(BF))
        logistic, slope = slope_parts(value)
        slope = keep_row(slope, at, inside[0], inside[1])
        gate1[k * C:(k + 1) * C, :] = slope
        if HALO <= at < HALO + R:
            own_at = at - HALO
            hidden[own_at * C:(own_at + 1) * C, :] = (value * logistic).astype(BF)
        d1[k * C:(k + 1) * C, :] = (slope * back[k * C:(k + 1) * C, :]).astype(BF)
    field = map_end(0, up[...], first_w[...], d1, taps)
    finish_wide(field, inside[0], inside[1], masks, part, moved)


def finish_wide(field, before, after, masks, part, moved):
    count = EXT - 6
    row = lax.broadcasted_iota(jnp.int32, field.shape, 0)
    keep = jnp.where(row < HALO - 3, before, jnp.where(row >= HALO - 3 + R, after, 1.0))
    field = field * keep
    moved[...] = field
    total = masked_sum(masks[3:3 + count, :], field)
    for k in range(part.shape[0]):
        part[k, 0:count, :] = total
        part[k, count:, :] = jnp.zeros((part.shape[1] - count, W), F32)


def narrow_field(step, sums, moved, up, masks):
    count = EXT - 6
    totals = gathered_sum(sums)[:count]
    return up[3:3 + count, :] + moved[...] - step * masks[3:3 + count, :] * twice(totals)


def second_kernel(step, sums, moved, up, masks, gate2, gate1, third_w, second_w, first_w,
                  part, out, copies, d2, d1, taps):
    copies[...] = jnp.zeros_like(copies)
    field = narrow_field(step, sums, moved, up, masks)
    result = adjoint_map(3, field, gate2, gate1, third_w[...], second_w[...], first_w[...],
                         copies, d2, d1, taps)
    out[...] = result
    total = masked_sum(masks[HALO:HALO + R, :], result)
    for k in range(part.shape[0]):
        part[k] = total


def update_kernel(step, sums, moved, up, masks, out):
    totals = gathered_sum(sums)
    out[...] = (up[HALO:HALO + R, :] + moved[...]
                - step * masks[HALO:HALO + R, :] * twice(totals))


def third_kernel(inside, low, own, high, masks, gate2, gate1, third_w, second_w, first_w,
                 part, moved, copies, d2, d1, taps, whole):
    copies[...] = jnp.zeros_like(copies)
    whole[0:HALO, :] = low[R - HALO:, :]
    whole[HALO:HALO + R, :] = own[...]
    whole[HALO + R:, :] = high[:HALO, :]
    field = adjoint_map(0, whole[...], gate2, gate1, third_w[...], second_w[...], first_w[...],
                        copies, d2, d1, taps)
    finish_wide(field, inside[0], inside[1], masks, part, moved)


def last_kernel(step, sums, moved, up, masks, gate2, gate1, hidden2, hidden, inputs, third_w,
                second_w, first_w, adjoint, grads, copies, d2, d1, taps, total):
    copies[...] = jnp.zeros_like(copies)
    field = narrow_field(step, sums, moved, up, masks)
    adjoint[0] = field[3:3 + R, :W]
    adjoint[1] = field[3:3 + R, W:]
    result = adjoint_map(3, field, gate2, gate1, third_w[...], second_w[...], first_w[...],
                         copies, d2, d1, taps)
    snapshot = masked_sum(masks[HALO:HALO + R, :], result)
    left = []
    right = []
    left_first = []
    right_first = []
    left_third = []
    right_third = []
    for r in range(R):
        left.append(d2[(r + 1) * C:(r + 4) * C, :])
        value = hidden[r * C:(r + 1) * C, :].astype(F32)
        right.append(jnp.concatenate(
            [roll_cols(value, 1), value, roll_cols(value, -1)], axis=0).astype(BF))
        left_first.append(inputs[r * Q:(r + 3) * Q, :])
        right_first.append(d1[(r + 1) * C:(r + 2) * C, :])
        left_third.append(take_rows(copies, (r + 2) * Q, (r + 5) * Q).astype(BF))
        right_third.append(saved_row(hidden2, r))
    def join(parts):
        return jnp.concatenate(parts, axis=1)
    second = dot_nt(join(left), join(right))
    first = dot_nt(join(left_first), join(right_first))
    third = dot_nt(join(left_third), join(right_third))
    total[0:3 * C, 0:3 * C] = second
    total[0:3 * Q, 3 * C:] = first
    total[3 * Q:6 * Q, 3 * C:] = third
    total[6 * Q:, 3 * C:] = jnp.zeros((total.shape[0] - 6 * Q, C), F32)
    total[3 * C:, 0:3 * C] = jnp.zeros((total.shape[0] - 3 * C, 3 * C), F32)
    count = grads.shape[0]
    rows = 3 * C // count
    line = lax.broadcasted_iota(jnp.int32, grads.shape[1:], 0)
    extra = jnp.zeros(grads.shape[1:], F32)
    for k in range(R // 2):
        pair = jnp.concatenate([snapshot[2 * k:2 * k + 1], snapshot[2 * k + 1:2 * k + 2]], axis=1)
        extra = jnp.where(line == rows + k, pair, extra)
    for k in range(count):
        grads[k] = jnp.where(line < rows, total[k * rows:k * rows + grads.shape[1], :],
                             extra).astype(BF)


def reduce_pieces(rows, place, stride, received):
    count = received.shape[0]
    total = received[0].astype(F32)
    for k in range(1, count):
        total = total + received[k].astype(F32)
    extra = received[place].astype(F32)
    for k in range(1, count // stride):
        extra = extra + received[place + k * stride].astype(F32)
    line = lax.broadcasted_iota(jnp.int32, total.shape, 0)
    return jnp.where(line < rows, total, extra)


def near_kernel(rows, stride, place, received, out):
    total = reduce_pieces(rows, place[0], stride, received).astype(BF)
    for k in range(out.shape[0]):
        out[k] = total


def far_kernel(rows, stride, step, place, received, out, snapshot):
    total = reduce_pieces(rows, place[0], stride, received)
    for k in range(R // 2):
        snapshot[2 * k:2 * k + 1, :] = step * total[rows + k:rows + k + 1, :W]
        snapshot[2 * k + 1:2 * k + 2, :] = step * total[rows + k:rows + k + 1, W:]
    total = total.astype(BF)
    for k in range(out.shape[0]):
        out[k] = total


def output_kernel(scale, received, first, second, third, total):
    count = received.shape[0]
    rows = 3 * C // count
    for k in range(count):
        total[k * rows:(k + 1) * rows, :] = received[k].astype(F32)[:rows] * scale
    for i in (-1, 0, 1):
        for j in (-1, 0, 1):
            tap = 3 * (i + 1) + (j + 1)
            back = 1 - i
            ahead = 1 + i
            second[tap] = total[back * C:(back + 1) * C, (j + 1) * C:(j + 2) * C]
            at = ahead * Q + j + 1
            first[tap:tap + 1, :] = total[at:at + 1, 3 * C:] + total[at + 3:at + 4, 3 * C:]
            at = 3 * Q + back * Q + j + 1
            third[tap:tap + 1, :] = total[at:at + 1, 3 * C:] + total[at + 3:at + 4, 3 * C:]


def call(kernel, outs, scratch, *operands, specs=None, cost=None, sems=0, limit=40):
    if specs is None:
        specs = [pl.BlockSpec(memory_space=pltpu.VMEM)] * len(operands)
    return pl.pallas_call(
        kernel,
        out_shape=[jax.ShapeDtypeStruct(shape, dtype) for shape, dtype in outs],
        in_specs=specs,
        out_specs=[pl.BlockSpec(memory_space=pltpu.VMEM)] * len(outs),
        scratch_shapes=[pltpu.VMEM(shape, dtype) for shape, dtype in scratch]
        + [pltpu.SemaphoreType.DMA((sems,))] * (sems > 0),
        compiler_params=pltpu.CompilerParams(vmem_limit_bytes=limit * 2**20),
        cost_estimate=cost,
    )(*operands)


def split_parts(field):
    high = field.astype(BF)
    return high, (field - high.astype(F32)).astype(BF)


def exchange(value, axis):
    return lax.all_to_all(value, axis, 0, 0, tiled=True)


def per_device(equilibrium, measurement, coding_masks, upstream, saved_second, conv_first,
               conv_second, conv_third):
    frames = lax.axis_size(TM)
    tiles = lax.axis_size(SPACE)
    total_frames = 2 * frames
    step = 1.0 / total_frames
    scale = 1.0 / math.sqrt(total_frames * R * tiles * W)
    forward = [(i, i + 1) for i in range(tiles - 1)]
    backward = [(i + 1, i) for i in range(tiles - 1)]
    place = lax.axis_index(SPACE)
    inside = jnp.stack([place > 0, place < tiles - 1]).astype(F32)

    hbm = pl.BlockSpec(memory_space=pltpu.HBM)
    edge = ((EDGE * C + FIELDS * R, LANES), BF)
    fields = ((4 * R, LANES), F32)
    frame = ((2, R, W), F32)
    own, top, bottom, own_fields = call(
        pack_kernel, [((R * C, LANES), BF), edge, edge, fields],
        [frame, frame, ((2, R, W), jnp.int32), ((R, W), F32), ((2, C, R, W), BF)],
        upstream, equilibrium, coding_masks, measurement, saved_second,
        specs=[hbm] * 5, sems=5, limit=60)
    low = lax.ppermute(bottom, SPACE, forward)
    high = lax.ppermute(top, SPACE, backward)

    forward_w, third_w, second_w, first_w, gate2_own, hidden2, own_fields = call(
        stage_kernel,
        [((C, 3 * Q), BF), ((C, 3 * Q), BF), ((3 * C, 3 * C), BF), ((Q, C), BF),
         ((R * C, LANES), F32), ((R * C, LANES), BF), fields], [],
        conv_first, conv_second, conv_third, own, own_fields,
        cost=pl.CostEstimate(flops=2 * 10**6, bytes_accessed=10**6, transcendentals=0))

    whole = pl.BlockSpec(memory_space=pltpu.VMEM)
    scalars = pl.BlockSpec(memory_space=pltpu.SMEM)
    ext = ((EXT, LANES), F32)
    part, up, masks, base = call(
        functools.partial(unpack_kernel, step),
        [((frames, 24, W), F32), ext, ext, ext], [ext, ext],
        low, own_fields, high)
    sums = exchange(part, TM)

    narrow = EXT - 6
    weights = (third_w, second_w, first_w)
    copies = ((2, EXT * Q, W), F32)
    d2 = (((EXT - 2) * C, LANES), BF)
    d1 = (((EXT - 4) * C, LANES), BF)
    taps = ((2, (EXT - 4) * Q, W), F32)
    slim_scratch = [((2, narrow * Q, W), F32), (((narrow - 2) * C, LANES), BF),
                    (((narrow - 4) * C, LANES), BF), ((2, (narrow - 4) * Q, W), F32)]
    wide_outs = [((frames, 16, W), F32), ((narrow, LANES), F32)]
    gate2, back = call(
        early_kernel,
        [(((EXT - 2) * C, LANES), F32), (((EXT - 4) * C, LANES), F32)], [copies, d2],
        inside, low, gate2_own, high, up, third_w, second_w,
        specs=[scalars] + [whole] * 6,
        cost=pl.CostEstimate(flops=10**9, bytes_accessed=8 * 10**6, transcendentals=3 * 10**5))
    part, moved, gate1, hidden, inputs = call(
        functools.partial(first_kernel, step),
        wide_outs + [(((EXT - 4) * C, LANES), F32), ((R * C, LANES), BF),
                     (((R + 2) * Q, LANES), BF)],
        [copies, d1, taps],
        inside, sums, up, masks, base, back, first_w, forward_w,
        specs=[scalars] + [whole] * 7)
    sums = exchange(part, TM)

    part, moved = call(
        functools.partial(second_kernel, step),
        [((frames, R, W), F32), ((R, LANES), F32)], slim_scratch,
        sums, moved, up, masks, gate2, gate1, *weights)
    sums = exchange(part, TM)

    field, = call(functools.partial(update_kernel, step), [((R, LANES), F32)], [],
                  sums, moved, up, masks)
    field_low = lax.ppermute(field, SPACE, forward)
    field_high = lax.ppermute(field, SPACE, backward)
    part, moved = call(
        third_kernel, wide_outs, [copies, d2, d1, taps, ext],
        inside, field_low, field, field_high, masks, gate2, gate1, *weights,
        specs=[scalars] + [whole] * 9)
    sums = exchange(part, TM)

    near_sizes = [lax.axis_size(name) for name in NEAR]
    far_sizes = [lax.axis_size(name) for name in FAR]
    near_count = math.prod(near_sizes)
    far_count = math.prod(far_sizes)
    rows = 3 * C // near_count
    piece = -(-(rows + R // 2) // 16) * 16
    adjoint, grads = call(
        functools.partial(last_kernel, step),
        [((2, R, W), F32), ((near_count, piece, LANES), BF)],
        slim_scratch + [((3 * C + piece, LANES), F32)],
        sums, moved, up, masks, gate2, gate1, hidden2, hidden, inputs, *weights)

    received = exchange(grads, NEAR)
    near_stride = near_count // near_sizes[0]
    near_place = lax.axis_index(NEAR[1:])[None]
    far_stride = far_count // far_sizes[0]
    far_place = lax.axis_index(FAR[1:])[None]
    received, = call(
        functools.partial(near_kernel, rows, near_stride),
        [((far_count, piece, LANES), BF)], [], near_place, received, specs=[scalars, whole])
    received = exchange(received, FAR)
    received, snapshot = call(
        functools.partial(far_kernel, rows, far_stride, step),
        [((near_count, piece, LANES), BF), ((R, W), F32)], [], far_place, received,
        specs=[scalars, whole])
    received = exchange(received, NEAR)
    grad_first, grad_second, grad_third = call(
        functools.partial(output_kernel, scale),
        [((9, C), F32), ((9, C, C), F32), ((9, C), F32)],
        [((3 * C, LANES), F32)], received)
    return adjoint, snapshot, grad_first, grad_second, grad_third


AXES = (("zh", 4), ("core", 2), ("zl", 2), ("y", 8), ("x", 4))


def solution(mesh, axes=AXES):
    names = tuple(name for name, _ in axes)
    sizes = tuple(size for _, size in axes)
    fine = Mesh(mesh.devices.reshape(sizes), names)
    placed = (
        P(TM, SPACE, None),
        P(SPACE, None),
        P(TM, SPACE, None),
        P(TM, SPACE, None),
        P(TM, None, SPACE, None),
        P(),
        P(),
        P(),
    )
    return jax.shard_map(
        per_device,
        mesh=fine,
        in_specs=placed,
        out_specs=(P(TM, SPACE, None), P(SPACE, None), P(), P(), P()),
        check_vma=False,
    )
```

```python
import functools
import math

import jax
import jax.numpy as jnp
from jax import lax
from jax.experimental import pallas as pl
from jax.experimental.pallas import tpu as pltpu
from jax.sharding import Mesh, PartitionSpec as P

ITERS = 3
C = 64
W = 128
LANES = 2 * W
R = 8
HALO = 6
EXT = R + 2 * HALO
EDGE = HALO - 1
FIELDS = 6
Q = 16
PIECE = 32
BF = jnp.bfloat16
F32 = jnp.float32

TM = ("zh", "core")
SPACE = ("zl", "y", "x")
NEAR = ("core", "zl", "x")
FAR = ("zh", "y")


def roll_cols(value, step):
    if step == 0:
        return value
    lane = lax.broadcasted_iota(jnp.int32, (value.shape[0], W), 1)
    edge = 0 if step > 0 else W - 1
    halves = []
    for frame in range(2):
        half = value[:, frame * W:(frame + 1) * W]
        half = pltpu.roll(half, step % W, 1)
        halves.append(jnp.where(lane == edge, 0.0, half))
    return jnp.concatenate(halves, axis=1)


def slope_parts(value):
    logistic = 0.5 * jnp.tanh(0.5 * value) + 0.5
    return logistic, logistic * (1.0 + value * (1.0 - logistic))


def put_slot(ref, at, count, value):
    for frame in range(2):
        ref[frame, pl.ds(at, count, stride=Q), :] = value[:, frame * W:(frame + 1) * W]


def take_slot(ref, at, count):
    return jnp.concatenate(
        [ref[frame, pl.ds(at, count, stride=Q), :] for frame in range(2)], axis=1)


def put_rows(ref, at, value):
    for frame in range(2):
        ref[frame, at:at + value.shape[0], :] = value[:, frame * W:(frame + 1) * W]


def take_rows(ref, first, last):
    return jnp.concatenate([ref[frame, first:last, :] for frame in range(2)], axis=1)


def fill_shifted(field, copies, sign):
    count = field.shape[0]
    for slot, step in enumerate((-1, 0, 1)):
        shifted = roll_cols(field, sign * step)
        high = shifted.astype(BF).astype(F32)
        put_slot(copies, slot, count, high)
        put_slot(copies, 3 + slot, count, shifted - high)


def dot(left, right):
    return jnp.dot(left, right, preferred_element_type=F32)


def dot_nt(left, right):
    return lax.dot_general(left, right, (((1,), (1,)), ((), ())), preferred_element_type=F32)


def back_rows(first, field, gate2, third_w, second_w, copies, d2):
    rows = EXT - 2 * first
    fill_shifted(field, copies, 1)
    for k in range(rows - 2):
        third = dot(third_w, take_rows(copies, k * Q, (k + 3) * Q).astype(BF))
        at = first + k
        d2[k * C:(k + 1) * C, :] = (gate2[at * C:(at + 1) * C, :] * third).astype(BF)
    for k in range(rows - 4):
        parts = dot(second_w, d2[k * C:(k + 3) * C, :])
        total = (
            roll_cols(parts[:C], -1) + parts[C:2 * C] + roll_cols(parts[2 * C:], 1)
        )
        yield k, total


def adjoint_map(first, field, gate2, gate1, third_w, second_w, first_w, copies, d2, d1, taps):
    for k, total in back_rows(first, field, gate2, third_w, second_w, copies, d2):
        at = first + k
        row = (gate1[at * C:(at + 1) * C, :] * total).astype(BF)
        d1[k * C:(k + 1) * C, :] = row
    return map_end(first, field, first_w, d1, taps)


def map_end(first, field, first_w, d1, taps):
    count = EXT - 2 * first - 6
    for k in range(count + 2):
        put_rows(taps, k * Q, dot(first_w, d1[k * C:(k + 1) * C, :]))
    result = field[3:3 + count]
    for j in (-1, 0, 1):
        column = None
        for i in (-1, 0, 1):
            tap = 3 * (i + 1) + (j + 1)
            part = take_slot(taps, (1 - i) * Q + tap, count)
            column = part if column is None else column + part
        result = result + roll_cols(column, j)
    return result


def masked_sum(masks, field):
    product = masks * field
    return product[:, :W] + product[:, W:]


def twice(field):
    return jnp.concatenate([field, field], axis=1)


def gathered_sum(ref):
    total = ref[0]
    for k in range(1, ref.shape[0]):
        total = total + ref[k]
    return total


def pack_kernel(upstream, equilibrium, masks, measurement, saved, out, top, bottom, own_fields,
                up_in, fixed_in, masks_in, snapshot_in, saved_in, sems):
    copies = [
        pltpu.make_async_copy(source, target, sems.at[k])
        for k, (source, target) in enumerate((
            (saved, saved_in), (upstream, up_in), (equilibrium, fixed_in), (masks, masks_in),
            (measurement, snapshot_in)))
    ]
    for copy in copies:
        copy.start()
    for copy in copies[1:]:
        copy.wait()

    def by_frame(ref):
        return jnp.concatenate([ref[0], ref[1]], axis=1)

    up = by_frame(up_in)
    fixed = by_frame(fixed_in)
    mask = by_frame(masks_in).astype(F32)
    snapshot = snapshot_in[...]
    for k, field in enumerate((up, mask, fixed, twice(snapshot))):
        own_fields[k * R:(k + 1) * R, :] = field
    fields = (*split_parts(up), *split_parts(fixed), mask.astype(BF),
              jnp.concatenate(split_parts(snapshot), axis=1))
    for k in range(0, len(fields), 2):
        pair = jnp.concatenate([field.astype(F32) for field in fields[k:k + 2]], axis=0).astype(BF)
        at = EDGE * C + k * R
        top[at:at + 2 * R, :] = pair
        bottom[at:at + 2 * R, :] = pair
    copies[0].wait()
    for frame in range(2):
        lanes = slice(frame * W, (frame + 1) * W)
        rows = jnp.swapaxes(saved_in[frame].astype(F32), 0, 1).astype(BF).reshape(R * C, W)
        out[:, lanes] = rows
        top[:EDGE * C, lanes] = rows[:EDGE * C]
        bottom[:EDGE * C, lanes] = rows[(R - EDGE) * C:]


def stage_kernel(first, second, third, saved, own_fields, forward_w, third_w, second_w, first_w,
                 gate2, hidden2, fields):
    fields[...] = own_fields[...]
    for r in range(R):
        value = saved_row(saved, r).astype(F32)
        logistic, slope = slope_parts(value)
        gate2[r * C:(r + 1) * C, :] = slope
        hidden2[r * C:(r + 1) * C, :] = (value * logistic).astype(BF)
    forward = first[...].astype(F32)
    backward = third[...].astype(F32)
    pad = jnp.zeros((Q - 6, C), F32)
    ahead = []
    back = []
    for i in range(3):
        row = forward[3 * i:3 * i + 3]
        ahead += [row, row, pad]
        row = backward[6 - 3 * i:9 - 3 * i]
        back += [row, row, pad]
        for j in range(3):
            tile = second[3 * (2 - i) + j].astype(F32)
            second_w[j * C:(j + 1) * C, i * C:(i + 1) * C] = jnp.transpose(tile).astype(BF)
    forward_w[...] = jnp.transpose(jnp.concatenate(ahead, axis=0)).astype(BF)
    third_w[...] = jnp.transpose(jnp.concatenate(back, axis=0)).astype(BF)
    first_w[...] = jnp.concatenate([forward, jnp.zeros((Q - 9, C), F32)], axis=0).astype(BF)


def unpack_kernel(step, low, own_fields, high, _, part, up, masks, base, fixed, snapshot):
    for k, target in enumerate((up, masks, fixed, snapshot)):
        target[HALO:HALO + R, :] = own_fields[k * R:(k + 1) * R, :]
    for ref, at, first in ((low, 0, R - HALO), (high, HALO + R, 0)):
        fields = ref[EDGE * C:EDGE * C + FIELDS * R, :].astype(F32)

        def field(k):
            return fields[k * R:(k + 1) * R]

        for target, value in ((up, field(0) + field(1)), (fixed, field(2) + field(3)),
                              (masks, field(4)),
                              (snapshot, twice(field(5)[:, :W] + field(5)[:, W:]))):
            target[at:at + HALO, :] = value[first:first + HALO]
    total = masked_sum(masks[...], fixed[...])
    for k in range(part.shape[0]):
        part[k, 0:EXT, :] = total
        part[k, EXT:, :] = jnp.zeros((part.shape[1] - EXT, W), F32)
    base[...] = fixed[...] + step * masks[...] * snapshot[...]


def saved_row(ref, at):
    return ref[at * C:(at + 1) * C, :]


def keep_row(value, at, before, after):
    if at < HALO:
        return value * before
    if at >= HALO + R:
        return value * after
    return value


def early_kernel(inside, low, own, high, up, third_w, second_w, gate2, back, copies, d2):
    copies[...] = jnp.zeros_like(copies)
    for k in range(EXT - 2):
        at = k + 1
        if HALO <= at < HALO + R:
            gate2[k * C:(k + 1) * C, :] = saved_row(own, at - HALO)
        else:
            value = saved_row(low, k) if at < HALO else saved_row(high, at - HALO - R)
            slope = slope_parts(value.astype(F32))[1]
            gate2[k * C:(k + 1) * C, :] = keep_row(slope, at, inside[0], inside[1])
    for k, total in back_rows(0, up[...], gate2, third_w[...], second_w[...], copies, d2):
        back[k * C:(k + 1) * C, :] = total


def first_kernel(step, inside, sums, up, masks, base, back, first_w, forward_w,
                 part, moved, gate1, hidden, inputs, copies, d1, taps):
    frame_sum = gathered_sum(sums)[:EXT]
    denoiser_input = base[...] - step * masks[...] * twice(frame_sum)
    copies[...] = jnp.zeros_like(copies)
    fill_shifted(denoiser_input, copies, -1)
    inputs[...] = take_rows(copies, (HALO - 1) * Q, (HALO + R + 1) * Q).astype(BF)
    for k in range(EXT - 4):
        at = k + 2
        value = dot(forward_w[...], take_rows(copies, (at - 1) * Q, (at + 2) * Q).astype(BF))
        logistic, slope = slope_parts(value)
        slope = keep_row(slope, at, inside[0], inside[1])
        gate1[k * C:(k + 1) * C, :] = slope
        if HALO <= at < HALO + R:
            own_at = at - HALO
            hidden[own_at * C:(own_at + 1) * C, :] = (value * logistic).astype(BF)
        d1[k * C:(k + 1) * C, :] = (slope * back[k * C:(k + 1) * C, :]).astype(BF)
    field = map_end(0, up[...], first_w[...], d1, taps)
    finish_wide(field, inside[0], inside[1], masks, part, moved)


def finish_wide(field, before, after, masks, part, moved):
    count = EXT - 6
    row = lax.broadcasted_iota(jnp.int32, field.shape, 0)
    keep = jnp.where(row < HALO - 3, before, jnp.where(row >= HALO - 3 + R, after, 1.0))
    field = field * keep
    moved[...] = field
    total = masked_sum(masks[3:3 + count, :], field)
    for k in range(part.shape[0]):
        part[k, 0:count, :] = total
        part[k, count:, :] = jnp.zeros((part.shape[1] - count, W), F32)


def narrow_field(step, sums, moved, up, masks):
    count = EXT - 6
    totals = gathered_sum(sums)[:count]
    return up[3:3 + count, :] + moved[...] - step * masks[3:3 + count, :] * twice(totals)


def second_kernel(step, sums, moved, up, masks, gate2, gate1, third_w, second_w, first_w,
                  part, out, copies, d2, d1, taps):
    copies[...] = jnp.zeros_like(copies)
    field = narrow_field(step, sums, moved, up, masks)
    result = adjoint_map(3, field, gate2, gate1, third_w[...], second_w[...], first_w[...],
                         copies, d2, d1, taps)
    out[...] = result
    total = masked_sum(masks[HALO:HALO + R, :], result)
    half = jnp.concatenate([total[:R // 2], total[R // 2:]], axis=1)
    for k in range(part.shape[0]):
        part[k, 0:R, :] = result
        part[k, R:, :] = half


def pair_total(received, first):
    count = received.shape[0] // 2
    half = received[first, R:, :]
    for k in range(1, count):
        half = half + received[first + k, R:, :]
    return jnp.concatenate([half[:, :W], half[:, W:]], axis=0)


def update_kernel(step, place, received, moved, up, masks, out):
    totals = pair_total(received, place[0])
    out[...] = (up[HALO:HALO + R, :] + moved[...]
                - step * masks[HALO:HALO + R, :] * twice(totals))


def third_kernel(step, inside, place, received, own, near, up, masks, gate2, gate1, third_w,
                 second_w, first_w, part, moved, copies, d2, d1, taps, whole):
    copies[...] = jnp.zeros_like(copies)
    totals = twice(pair_total(received, place[1]))
    theirs = received[place[2], 0:R, :]
    after_rows = slice(HALO + R, EXT)
    low = (up[0:HALO, :] + theirs[R - HALO:]
           - step * masks[0:HALO, :] * totals[R - HALO:]) * inside[0]
    high = (up[after_rows, :] + theirs[:HALO]
            - step * masks[after_rows, :] * totals[:HALO]) * inside[1]
    odd = place[3] == 1
    whole[0:HALO, :] = jnp.where(odd, near[R - HALO:, :], low)
    whole[HALO:HALO + R, :] = own[...]
    whole[HALO + R:, :] = jnp.where(odd, high, near[:HALO, :])
    field = adjoint_map(0, whole[...], gate2, gate1, third_w[...], second_w[...], first_w[...],
                        copies, d2, d1, taps)
    finish_wide(field, inside[0], inside[1], masks, part, moved)


def last_kernel(step, sums, moved, up, masks, gate2, gate1, hidden2, hidden, inputs, third_w,
                second_w, first_w, adjoint, grads, copies, d2, d1, taps, total):
    copies[...] = jnp.zeros_like(copies)
    field = narrow_field(step, sums, moved, up, masks)
    adjoint[0] = field[3:3 + R, :W]
    adjoint[1] = field[3:3 + R, W:]
    result = adjoint_map(3, field, gate2, gate1, third_w[...], second_w[...], first_w[...],
                         copies, d2, d1, taps)
    snapshot = masked_sum(masks[HALO:HALO + R, :], result)
    left = []
    right = []
    left_first = []
    right_first = []
    left_third = []
    right_third = []
    for r in range(R):
        left.append(d2[(r + 1) * C:(r + 4) * C, :])
        value = hidden[r * C:(r + 1) * C, :].astype(F32)
        right.append(jnp.concatenate(
            [roll_cols(value, 1), value, roll_cols(value, -1)], axis=0).astype(BF))
        left_first.append(inputs[r * Q:(r + 3) * Q, :])
        right_first.append(d1[(r + 1) * C:(r + 2) * C, :])
        left_third.append(take_rows(copies, (r + 2) * Q, (r + 5) * Q).astype(BF))
        right_third.append(saved_row(hidden2, r))
    def join(parts):
        return jnp.concatenate(parts, axis=1)
    second = dot_nt(join(left), join(right))
    first = dot_nt(join(left_first), join(right_first))
    third = dot_nt(join(left_third), join(right_third))
    total[0:3 * C, 0:3 * C] = second
    total[0:3 * Q, 3 * C:] = first
    total[3 * Q:6 * Q, 3 * C:] = third
    total[6 * Q:, 3 * C:] = jnp.zeros((total.shape[0] - 6 * Q, C), F32)
    total[3 * C:, 0:3 * C] = jnp.zeros((total.shape[0] - 3 * C, 3 * C), F32)
    count = grads.shape[0]
    rows = 3 * C // count
    line = lax.broadcasted_iota(jnp.int32, grads.shape[1:], 0)
    extra = jnp.zeros(grads.shape[1:], F32)
    for k in range(R // 2):
        pair = jnp.concatenate([snapshot[2 * k:2 * k + 1], snapshot[2 * k + 1:2 * k + 2]], axis=1)
        extra = jnp.where(line == rows + k, pair, extra)
    for k in range(count):
        grads[k] = jnp.where(line < rows, total[k * rows:k * rows + grads.shape[1], :],
                             extra).astype(BF)


def reduce_pieces(rows, place, stride, received):
    count = received.shape[0]
    total = received[0].astype(F32)
    for k in range(1, count):
        total = total + received[k].astype(F32)
    extra = received[place].astype(F32)
    for k in range(1, count // stride):
        extra = extra + received[place + k * stride].astype(F32)
    line = lax.broadcasted_iota(jnp.int32, total.shape, 0)
    return jnp.where(line < rows, total, extra)


def near_kernel(rows, stride, place, received, out):
    total = reduce_pieces(rows, place[0], stride, received).astype(BF)
    for k in range(out.shape[0]):
        out[k] = total


def far_kernel(rows, stride, step, place, received, out, snapshot):
    total = reduce_pieces(rows, place[0], stride, received)
    for k in range(R // 2):
        snapshot[2 * k:2 * k + 1, :] = step * total[rows + k:rows + k + 1, :W]
        snapshot[2 * k + 1:2 * k + 2, :] = step * total[rows + k:rows + k + 1, W:]
    total = total.astype(BF)
    for k in range(out.shape[0]):
        out[k] = total


def output_kernel(scale, received, first, second, third, total):
    count = received.shape[0]
    rows = 3 * C // count
    for k in range(count):
        total[k * rows:(k + 1) * rows, :] = received[k].astype(F32)[:rows] * scale
    for i in (-1, 0, 1):
        for j in (-1, 0, 1):
            tap = 3 * (i + 1) + (j + 1)
            back = 1 - i
            ahead = 1 + i
            second[tap] = total[back * C:(back + 1) * C, (j + 1) * C:(j + 2) * C]
            at = ahead * Q + j + 1
            first[tap:tap + 1, :] = total[at:at + 1, 3 * C:] + total[at + 3:at + 4, 3 * C:]
            at = 3 * Q + back * Q + j + 1
            third[tap:tap + 1, :] = total[at:at + 1, 3 * C:] + total[at + 3:at + 4, 3 * C:]


def call(kernel, outs, scratch, *operands, specs=None, cost=None, sems=0, limit=40):
    if specs is None:
        specs = [pl.BlockSpec(memory_space=pltpu.VMEM)] * len(operands)
    return pl.pallas_call(
        kernel,
        out_shape=[jax.ShapeDtypeStruct(shape, dtype) for shape, dtype in outs],
        in_specs=specs,
        out_specs=[pl.BlockSpec(memory_space=pltpu.VMEM)] * len(outs),
        scratch_shapes=[pltpu.VMEM(shape, dtype) for shape, dtype in scratch]
        + [pltpu.SemaphoreType.DMA((sems,))] * (sems > 0),
        compiler_params=pltpu.CompilerParams(vmem_limit_bytes=limit * 2**20),
        cost_estimate=cost,
    )(*operands)


def split_parts(field):
    high = field.astype(BF)
    return high, (field - high.astype(F32)).astype(BF)


def exchange(value, axis):
    return lax.all_to_all(value, axis, 0, 0, tiled=True)


def per_device(equilibrium, measurement, coding_masks, upstream, saved_second, conv_first,
               conv_second, conv_third):
    frames = lax.axis_size(TM)
    tiles = lax.axis_size(SPACE)
    total_frames = 2 * frames
    step = 1.0 / total_frames
    scale = 1.0 / math.sqrt(total_frames * R * tiles * W)
    forward = [(i, i + 1) for i in range(tiles - 1)]
    backward = [(i + 1, i) for i in range(tiles - 1)]
    place = lax.axis_index(SPACE)
    inside = jnp.stack([place > 0, place < tiles - 1]).astype(F32)

    hbm = pl.BlockSpec(memory_space=pltpu.HBM)
    edge = ((EDGE * C + FIELDS * R, LANES), BF)
    fields = ((4 * R, LANES), F32)
    frame = ((2, R, W), F32)
    own, top, bottom, own_fields = call(
        pack_kernel, [((R * C, LANES), BF), edge, edge, fields],
        [frame, frame, ((2, R, W), jnp.int32), ((R, W), F32), ((2, C, R, W), BF)],
        upstream, equilibrium, coding_masks, measurement, saved_second,
        specs=[hbm] * 5, sems=5, limit=60)
    low = lax.ppermute(bottom, SPACE, forward)
    high = lax.ppermute(top, SPACE, backward)

    forward_w, third_w, second_w, first_w, gate2_own, hidden2, own_fields = call(
        stage_kernel,
        [((C, 3 * Q), BF), ((C, 3 * Q), BF), ((3 * C, 3 * C), BF), ((Q, C), BF),
         ((R * C, LANES), F32), ((R * C, LANES), BF), fields], [],
        conv_first, conv_second, conv_third, own, own_fields,
        cost=pl.CostEstimate(flops=2 * 10**6, bytes_accessed=10**6, transcendentals=0))

    whole = pl.BlockSpec(memory_space=pltpu.VMEM)
    scalars = pl.BlockSpec(memory_space=pltpu.SMEM)
    ext = ((EXT, LANES), F32)
    part, up, masks, base = call(
        functools.partial(unpack_kernel, step),
        [((frames, 24, W), F32), ext, ext, ext], [ext, ext],
        low, own_fields, high, gate2_own)
    sums = exchange(part, TM)

    narrow = EXT - 6
    weights = (third_w, second_w, first_w)
    copies = ((2, EXT * Q, W), F32)
    d2 = (((EXT - 2) * C, LANES), BF)
    d1 = (((EXT - 4) * C, LANES), BF)
    taps = ((2, (EXT - 4) * Q, W), F32)
    slim_scratch = [((2, narrow * Q, W), F32), (((narrow - 2) * C, LANES), BF),
                    (((narrow - 4) * C, LANES), BF), ((2, (narrow - 4) * Q, W), F32)]
    wide_outs = [((frames, 16, W), F32), ((narrow, LANES), F32)]
    gate2, back = call(
        early_kernel,
        [(((EXT - 2) * C, LANES), F32), (((EXT - 4) * C, LANES), F32)], [copies, d2],
        inside, low, gate2_own, high, up, third_w, second_w,
        specs=[scalars] + [whole] * 6,
        cost=pl.CostEstimate(flops=10**9, bytes_accessed=8 * 10**6, transcendentals=3 * 10**5))
    part, moved, gate1, hidden, inputs = call(
        functools.partial(first_kernel, step),
        wide_outs + [(((EXT - 4) * C, LANES), F32), ((R * C, LANES), BF),
                     (((R + 2) * Q, LANES), BF)],
        [copies, d1, taps],
        inside, sums, up, masks, base, back, first_w, forward_w,
        specs=[scalars] + [whole] * 7)
    sums = exchange(part, TM)

    part, moved = call(
        functools.partial(second_kernel, step),
        [((2 * frames, R + R // 2, LANES), F32), ((R, LANES), F32)], slim_scratch,
        sums, moved, up, masks, gate2, gate1, *weights)
    groups = [[t * tiles + (k + side) % tiles for side in range(2) for t in range(frames)]
              for k in range(1, tiles, 2)]
    received = lax.all_to_all(part, TM + SPACE, 0, 0, axis_index_groups=groups, tiled=True)
    odd = place % 2
    mine = frames * (1 - odd)
    theirs = frames * odd
    pair_place = jnp.stack([mine, theirs, theirs + lax.axis_index(TM), odd])
    field, = call(functools.partial(update_kernel, step), [((R, LANES), F32)], [],
                  pair_place, received, moved, up, masks, specs=[scalars] + [whole] * 4)
    near = lax.ppermute(field, SPACE, [(i, i ^ 1) for i in range(tiles)])
    part, moved = call(
        functools.partial(third_kernel, step), wide_outs, [copies, d2, d1, taps, ext],
        inside, pair_place, received, field, near, up, masks, gate2, gate1, *weights,
        specs=[scalars] * 2 + [whole] * 10)
    sums = exchange(part, TM)

    near_sizes = [lax.axis_size(name) for name in NEAR]
    far_sizes = [lax.axis_size(name) for name in FAR]
    near_count = math.prod(near_sizes)
    far_count = math.prod(far_sizes)
    rows = 3 * C // near_count
    piece = -(-(rows + R // 2) // 16) * 16
    adjoint, grads = call(
        functools.partial(last_kernel, step),
        [((2, R, W), F32), ((near_count, piece, LANES), BF)],
        slim_scratch + [((3 * C + piece, LANES), F32)],
        sums, moved, up, masks, gate2, gate1, hidden2, hidden, inputs, *weights)

    received = exchange(grads, NEAR)
    near_stride = near_count // near_sizes[0]
    near_place = lax.axis_index(NEAR[1:])[None]
    far_stride = far_count // far_sizes[0]
    far_place = lax.axis_index(FAR[1:])[None]
    received, = call(
        functools.partial(near_kernel, rows, near_stride),
        [((far_count, piece, LANES), BF)], [], near_place, received, specs=[scalars, whole])
    received = exchange(received, FAR)
    received, snapshot = call(
        functools.partial(far_kernel, rows, far_stride, step),
        [((near_count, piece, LANES), BF), ((R, W), F32)], [], far_place, received,
        specs=[scalars, whole])
    received = exchange(received, NEAR)
    grad_first, grad_second, grad_third = call(
        functools.partial(output_kernel, scale),
        [((9, C), F32), ((9, C, C), F32), ((9, C), F32)],
        [((3 * C, LANES), F32)], received)
    return adjoint, snapshot, grad_first, grad_second, grad_third


AXES = (("zh", 4), ("core", 2), ("zl", 2), ("y", 8), ("x", 4))


def solution(mesh, axes=AXES):
    names = tuple(name for name, _ in axes)
    sizes = tuple(size for _, size in axes)
    fine = Mesh(mesh.devices.reshape(sizes), names)
    placed = (
        P(TM, SPACE, None),
        P(SPACE, None),
        P(TM, SPACE, None),
        P(TM, SPACE, None),
        P(TM, None, SPACE, None),
        P(),
        P(),
        P(),
    )
    return jax.shard_map(
        per_device,
        mesh=fine,
        in_specs=placed,
        out_specs=(P(TM, SPACE, None), P(SPACE, None), P(), P(), P()),
        check_vma=False,
    )
```

```python
import functools
import math

import jax
import jax.numpy as jnp
from jax import lax
from jax.experimental import pallas as pl
from jax.experimental.pallas import tpu as pltpu
from jax.sharding import Mesh, PartitionSpec as P

ITERS = 3
C = 64
W = 128
LANES = 2 * W
R = 8
HALO = 6
EXT = R + 2 * HALO
EDGE = HALO - 1
FIELDS = 6
Q = 16
PIECE = 32
BF = jnp.bfloat16
F32 = jnp.float32

TM = ("zh", "core")
SPACE = ("zl", "y", "x")
BEFORE, AFTER, ODD, OWN_HALF, THEIR_ENTRY, THEIR_HALF, NEAR_AT, FAR_AT = range(8)
NEAR = ("core", "zl", "x")
FAR = ("zh", "y")


def roll_cols(value, step):
    if step == 0:
        return value
    lane = lax.broadcasted_iota(jnp.int32, (value.shape[0], W), 1)
    edge = 0 if step > 0 else W - 1
    halves = []
    for frame in range(2):
        half = value[:, frame * W:(frame + 1) * W]
        half = pltpu.roll(half, step % W, 1)
        halves.append(jnp.where(lane == edge, 0.0, half))
    return jnp.concatenate(halves, axis=1)


def slope_parts(value):
    logistic = 0.5 * jnp.tanh(0.5 * value) + 0.5
    return logistic, logistic * (1.0 + value * (1.0 - logistic))


def put_slot(ref, at, count, value):
    for frame in range(2):
        ref[frame, pl.ds(at, count, stride=Q), :] = value[:, frame * W:(frame + 1) * W]


def take_slot(ref, at, count):
    return jnp.concatenate(
        [ref[frame, pl.ds(at, count, stride=Q), :] for frame in range(2)], axis=1)


def put_rows(ref, at, value):
    for frame in range(2):
        ref[frame, at:at + value.shape[0], :] = value[:, frame * W:(frame + 1) * W]


def take_rows(ref, first, last):
    return jnp.concatenate([ref[frame, first:last, :] for frame in range(2)], axis=1)


def fill_shifted(field, copies, sign):
    count = field.shape[0]
    for slot, step in enumerate((-1, 0, 1)):
        shifted = roll_cols(field, sign * step)
        high = shifted.astype(BF).astype(F32)
        put_slot(copies, slot, count, high)
        put_slot(copies, 3 + slot, count, shifted - high)


def dot(left, right):
    return jnp.dot(left, right, preferred_element_type=F32)


def dot_nt(left, right):
    return lax.dot_general(left, right, (((1,), (1,)), ((), ())), preferred_element_type=F32)


def back_rows(first, field, gate2, third_w, second_w, copies, d2):
    rows = EXT - 2 * first
    fill_shifted(field, copies, 1)
    for k in range(rows - 2):
        third = dot(third_w, take_rows(copies, k * Q, (k + 3) * Q).astype(BF))
        at = first + k
        d2[k * C:(k + 1) * C, :] = (gate2[at * C:(at + 1) * C, :] * third).astype(BF)
    for k in range(rows - 4):
        parts = dot(second_w, d2[k * C:(k + 3) * C, :])
        total = (
            roll_cols(parts[:C], -1) + parts[C:2 * C] + roll_cols(parts[2 * C:], 1)
        )
        yield k, total


def adjoint_map(first, field, gate2, gate1, third_w, second_w, first_w, copies, d2, d1, taps):
    for k, total in back_rows(first, field, gate2, third_w, second_w, copies, d2):
        at = first + k
        row = (gate1[at * C:(at + 1) * C, :] * total).astype(BF)
        d1[k * C:(k + 1) * C, :] = row
    return map_end(first, field, first_w, d1, taps)


def map_end(first, field, first_w, d1, taps):
    count = EXT - 2 * first - 6
    for k in range(count + 2):
        put_rows(taps, k * Q, dot(first_w, d1[k * C:(k + 1) * C, :]))
    result = field[3:3 + count]
    for j in (-1, 0, 1):
        column = None
        for i in (-1, 0, 1):
            tap = 3 * (i + 1) + (j + 1)
            part = take_slot(taps, (1 - i) * Q + tap, count)
            column = part if column is None else column + part
        result = result + roll_cols(column, j)
    return result


def masked_sum(masks, field):
    product = masks * field
    return product[:, :W] + product[:, W:]


def twice(field):
    return jnp.concatenate([field, field], axis=1)


def gathered_sum(ref):
    total = ref[0]
    for k in range(1, ref.shape[0]):
        total = total + ref[k]
    return total


def pack_kernel(upstream, equilibrium, masks, measurement, saved, out, top, bottom, own_fields,
                up_in, fixed_in, masks_in, snapshot_in, saved_in, sems):
    copies = [
        pltpu.make_async_copy(source, target, sems.at[k])
        for k, (source, target) in enumerate((
            (saved, saved_in), (upstream, up_in), (equilibrium, fixed_in), (masks, masks_in),
            (measurement, snapshot_in)))
    ]
    for copy in copies:
        copy.start()
    for copy in copies[1:]:
        copy.wait()

    def by_frame(ref):
        return jnp.concatenate([ref[0], ref[1]], axis=1)

    up = by_frame(up_in)
    fixed = by_frame(fixed_in)
    mask = by_frame(masks_in).astype(F32)
    snapshot = snapshot_in[...]
    for k, field in enumerate((up, mask, fixed, twice(snapshot))):
        own_fields[k * R:(k + 1) * R, :] = field
    fields = (*split_parts(up), *split_parts(fixed), mask.astype(BF),
              jnp.concatenate(split_parts(snapshot), axis=1))
    for k in range(0, len(fields), 2):
        pair = jnp.concatenate([field.astype(F32) for field in fields[k:k + 2]], axis=0).astype(BF)
        at = EDGE * C + k * R
        top[at:at + 2 * R, :] = pair
        bottom[at:at + 2 * R, :] = pair
    copies[0].wait()
    for frame in range(2):
        lanes = slice(frame * W, (frame + 1) * W)
        rows = jnp.swapaxes(saved_in[frame].astype(F32), 0, 1).astype(BF).reshape(R * C, W)
        out[:, lanes] = rows
        top[:EDGE * C, lanes] = rows[:EDGE * C]
        bottom[:EDGE * C, lanes] = rows[(R - EDGE) * C:]


def stage_kernel(_, first, second, third, saved, own_fields, forward_w, third_w, second_w, first_w,
                 gate2, hidden2, fields):
    fields[...] = own_fields[...]
    for r in range(R):
        value = saved_row(saved, r).astype(F32)
        logistic, slope = slope_parts(value)
        gate2[r * C:(r + 1) * C, :] = slope
        hidden2[r * C:(r + 1) * C, :] = (value * logistic).astype(BF)
    forward = first[...].astype(F32)
    backward = third[...].astype(F32)
    pad = jnp.zeros((Q - 6, C), F32)
    ahead = []
    back = []
    for i in range(3):
        row = forward[3 * i:3 * i + 3]
        ahead += [row, row, pad]
        row = backward[6 - 3 * i:9 - 3 * i]
        back += [row, row, pad]
        for j in range(3):
            tile = second[3 * (2 - i) + j].astype(F32)
            second_w[j * C:(j + 1) * C, i * C:(i + 1) * C] = jnp.transpose(tile).astype(BF)
    forward_w[...] = jnp.transpose(jnp.concatenate(ahead, axis=0)).astype(BF)
    third_w[...] = jnp.transpose(jnp.concatenate(back, axis=0)).astype(BF)
    first_w[...] = jnp.concatenate([forward, jnp.zeros((Q - 9, C), F32)], axis=0).astype(BF)


def unpack_kernel(step, low, own_fields, high, _, part, up, masks, base, fixed, snapshot):
    for k, target in enumerate((up, masks, fixed, snapshot)):
        target[HALO:HALO + R, :] = own_fields[k * R:(k + 1) * R, :]
    for ref, at, first in ((low, 0, R - HALO), (high, HALO + R, 0)):
        fields = ref[EDGE * C:EDGE * C + FIELDS * R, :].astype(F32)

        def field(k):
            return fields[k * R:(k + 1) * R]

        for target, value in ((up, field(0) + field(1)), (fixed, field(2) + field(3)),
                              (masks, field(4)),
                              (snapshot, twice(field(5)[:, :W] + field(5)[:, W:]))):
            target[at:at + HALO, :] = value[first:first + HALO]
    total = masked_sum(masks[...], fixed[...])
    for k in range(part.shape[0]):
        part[k, 0:EXT, :] = total
        part[k, EXT:, :] = jnp.zeros((part.shape[1] - EXT, W), F32)
    base[...] = fixed[...] + step * masks[...] * snapshot[...]


def saved_row(ref, at):
    return ref[at * C:(at + 1) * C, :]


def keep_row(value, at, before, after):
    if at < HALO:
        return value * before
    if at >= HALO + R:
        return value * after
    return value


def ends(places):
    return places[BEFORE].astype(F32), places[AFTER].astype(F32)


def early_kernel(places, low, own, high, up, third_w, second_w, _, gate2, back, copies, d2):
    before, after = ends(places)
    copies[...] = jnp.zeros_like(copies)
    for k in range(EXT - 2):
        at = k + 1
        if HALO <= at < HALO + R:
            gate2[k * C:(k + 1) * C, :] = saved_row(own, at - HALO)
        else:
            value = saved_row(low, k) if at < HALO else saved_row(high, at - HALO - R)
            slope = slope_parts(value.astype(F32))[1]
            gate2[k * C:(k + 1) * C, :] = keep_row(slope, at, before, after)
    for k, total in back_rows(0, up[...], gate2, third_w[...], second_w[...], copies, d2):
        back[k * C:(k + 1) * C, :] = total


def first_kernel(step, places, sums, up, masks, base, back, first_w, forward_w,
                 part, moved, gate1, hidden, inputs, copies, d1, taps):
    before, after = ends(places)
    frame_sum = gathered_sum(sums)[:EXT]
    denoiser_input = base[...] - step * masks[...] * twice(frame_sum)
    copies[...] = jnp.zeros_like(copies)
    fill_shifted(denoiser_input, copies, -1)
    inputs[...] = take_rows(copies, (HALO - 1) * Q, (HALO + R + 1) * Q).astype(BF)
    for k in range(EXT - 4):
        at = k + 2
        value = dot(forward_w[...], take_rows(copies, (at - 1) * Q, (at + 2) * Q).astype(BF))
        logistic, slope = slope_parts(value)
        slope = keep_row(slope, at, before, after)
        gate1[k * C:(k + 1) * C, :] = slope
        if HALO <= at < HALO + R:
            own_at = at - HALO
            hidden[own_at * C:(own_at + 1) * C, :] = (value * logistic).astype(BF)
        d1[k * C:(k + 1) * C, :] = (slope * back[k * C:(k + 1) * C, :]).astype(BF)
    field = map_end(0, up[...], first_w[...], d1, taps)
    finish_wide(field, before, after, masks, part, moved)


def finish_wide(field, before, after, masks, part, moved):
    count = EXT - 6
    row = lax.broadcasted_iota(jnp.int32, field.shape, 0)
    keep = jnp.where(row < HALO - 3, before, jnp.where(row >= HALO - 3 + R, after, 1.0))
    field = field * keep
    moved[...] = field
    total = masked_sum(masks[3:3 + count, :], field)
    for k in range(part.shape[0]):
        part[k, 0:count, :] = total
        part[k, count:, :] = jnp.zeros((part.shape[1] - count, W), F32)


def narrow_field(step, sums, moved, up, masks):
    count = EXT - 6
    totals = gathered_sum(sums)[:count]
    return up[3:3 + count, :] + moved[...] - step * masks[3:3 + count, :] * twice(totals)


def second_kernel(step, sums, moved, up, masks, gate2, gate1, third_w, second_w, first_w,
                  part, out, copies, d2, d1, taps):
    copies[...] = jnp.zeros_like(copies)
    field = narrow_field(step, sums, moved, up, masks)
    result = adjoint_map(3, field, gate2, gate1, third_w[...], second_w[...], first_w[...],
                         copies, d2, d1, taps)
    out[...] = result
    total = masked_sum(masks[HALO:HALO + R, :], result)
    half = jnp.concatenate([total[:R // 2], total[R // 2:]], axis=1)
    for k in range(part.shape[0]):
        part[k, 0:R, :] = result
        part[k, R:, :] = half


def pair_total(received, first):
    count = received.shape[0] // 2
    half = received[first, R:, :]
    for k in range(1, count):
        half = half + received[first + k, R:, :]
    return jnp.concatenate([half[:, :W], half[:, W:]], axis=0)


def update_kernel(step, places, received, moved, up, masks, out):
    totals = pair_total(received, places[OWN_HALF])
    out[...] = (up[HALO:HALO + R, :] + moved[...]
                - step * masks[HALO:HALO + R, :] * twice(totals))


def third_kernel(step, places, received, own, near, up, masks, gate2, gate1, third_w,
                 second_w, first_w, part, moved, copies, d2, d1, taps, whole):
    copies[...] = jnp.zeros_like(copies)
    before, after = ends(places)
    totals = twice(pair_total(received, places[THEIR_HALF]))
    theirs = received[places[THEIR_ENTRY], 0:R, :]
    after_rows = slice(HALO + R, EXT)
    low = (up[0:HALO, :] + theirs[R - HALO:]
           - step * masks[0:HALO, :] * totals[R - HALO:]) * before
    high = (up[after_rows, :] + theirs[:HALO]
            - step * masks[after_rows, :] * totals[:HALO]) * after
    odd = places[ODD] == 1
    whole[0:HALO, :] = jnp.where(odd, near[R - HALO:, :], low)
    whole[HALO:HALO + R, :] = own[...]
    whole[HALO + R:, :] = jnp.where(odd, high, near[:HALO, :])
    field = adjoint_map(0, whole[...], gate2, gate1, third_w[...], second_w[...], first_w[...],
                        copies, d2, d1, taps)
    finish_wide(field, before, after, masks, part, moved)


def last_kernel(step, sums, moved, up, masks, gate2, gate1, hidden2, hidden, inputs, third_w,
                second_w, first_w, adjoint, grads, copies, d2, d1, taps, total):
    copies[...] = jnp.zeros_like(copies)
    field = narrow_field(step, sums, moved, up, masks)
    adjoint[0] = field[3:3 + R, :W]
    adjoint[1] = field[3:3 + R, W:]
    result = adjoint_map(3, field, gate2, gate1, third_w[...], second_w[...], first_w[...],
                         copies, d2, d1, taps)
    snapshot = masked_sum(masks[HALO:HALO + R, :], result)
    left = []
    right = []
    left_first = []
    right_first = []
    left_third = []
    right_third = []
    for r in range(R):
        left.append(d2[(r + 1) * C:(r + 4) * C, :])
        value = hidden[r * C:(r + 1) * C, :].astype(F32)
        right.append(jnp.concatenate(
            [roll_cols(value, 1), value, roll_cols(value, -1)], axis=0).astype(BF))
        left_first.append(inputs[r * Q:(r + 3) * Q, :])
        right_first.append(d1[(r + 1) * C:(r + 2) * C, :])
        left_third.append(take_rows(copies, (r + 2) * Q, (r + 5) * Q).astype(BF))
        right_third.append(saved_row(hidden2, r))
    def join(parts):
        return jnp.concatenate(parts, axis=1)
    second = dot_nt(join(left), join(right))
    first = dot_nt(join(left_first), join(right_first))
    third = dot_nt(join(left_third), join(right_third))
    total[0:3 * C, 0:3 * C] = second
    total[0:3 * Q, 3 * C:] = first
    total[3 * Q:6 * Q, 3 * C:] = third
    total[6 * Q:, 3 * C:] = jnp.zeros((total.shape[0] - 6 * Q, C), F32)
    total[3 * C:, 0:3 * C] = jnp.zeros((total.shape[0] - 3 * C, 3 * C), F32)
    count = grads.shape[0]
    rows = 3 * C // count
    line = lax.broadcasted_iota(jnp.int32, grads.shape[1:], 0)
    extra = jnp.zeros(grads.shape[1:], F32)
    for k in range(R // 2):
        pair = jnp.concatenate([snapshot[2 * k:2 * k + 1], snapshot[2 * k + 1:2 * k + 2]], axis=1)
        extra = jnp.where(line == rows + k, pair, extra)
    for k in range(count):
        grads[k] = jnp.where(line < rows, total[k * rows:k * rows + grads.shape[1], :],
                             extra).astype(BF)


def reduce_pieces(rows, place, stride, received):
    count = received.shape[0]
    total = received[0].astype(F32)
    for k in range(1, count):
        total = total + received[k].astype(F32)
    extra = received[place].astype(F32)
    for k in range(1, count // stride):
        extra = extra + received[place + k * stride].astype(F32)
    line = lax.broadcasted_iota(jnp.int32, total.shape, 0)
    return jnp.where(line < rows, total, extra)


def near_kernel(rows, stride, places, received, out):
    total = reduce_pieces(rows, places[NEAR_AT], stride, received).astype(BF)
    for k in range(out.shape[0]):
        out[k] = total


def far_kernel(rows, stride, step, places, received, out, snapshot):
    total = reduce_pieces(rows, places[FAR_AT], stride, received)
    for k in range(R // 2):
        snapshot[2 * k:2 * k + 1, :] = step * total[rows + k:rows + k + 1, :W]
        snapshot[2 * k + 1:2 * k + 2, :] = step * total[rows + k:rows + k + 1, W:]
    total = total.astype(BF)
    for k in range(out.shape[0]):
        out[k] = total


def output_kernel(scale, received, first, second, third, total):
    count = received.shape[0]
    rows = 3 * C // count
    for k in range(count):
        total[k * rows:(k + 1) * rows, :] = received[k].astype(F32)[:rows] * scale
    for i in (-1, 0, 1):
        for j in (-1, 0, 1):
            tap = 3 * (i + 1) + (j + 1)
            back = 1 - i
            ahead = 1 + i
            second[tap] = total[back * C:(back + 1) * C, (j + 1) * C:(j + 2) * C]
            at = ahead * Q + j + 1
            first[tap:tap + 1, :] = total[at:at + 1, 3 * C:] + total[at + 3:at + 4, 3 * C:]
            at = 3 * Q + back * Q + j + 1
            third[tap:tap + 1, :] = total[at:at + 1, 3 * C:] + total[at + 3:at + 4, 3 * C:]


def call(kernel, outs, scratch, *operands, specs=None, cost=None, sems=0, limit=40):
    if specs is None:
        specs = [pl.BlockSpec(memory_space=pltpu.VMEM)] * len(operands)
    return pl.pallas_call(
        kernel,
        out_shape=[jax.ShapeDtypeStruct(shape, dtype) for shape, dtype in outs],
        in_specs=specs,
        out_specs=[pl.BlockSpec(memory_space=pltpu.VMEM)] * len(outs),
        scratch_shapes=[pltpu.VMEM(shape, dtype) for shape, dtype in scratch]
        + [pltpu.SemaphoreType.DMA((sems,))] * (sems > 0),
        compiler_params=pltpu.CompilerParams(vmem_limit_bytes=limit * 2**20),
        cost_estimate=cost,
    )(*operands)


def split_parts(field):
    high = field.astype(BF)
    return high, (field - high.astype(F32)).astype(BF)


def exchange(value, axis):
    return lax.all_to_all(value, axis, 0, 0, tiled=True)


def per_device(equilibrium, measurement, coding_masks, upstream, saved_second, conv_first,
               conv_second, conv_third):
    frames = lax.axis_size(TM)
    tiles = lax.axis_size(SPACE)
    total_frames = 2 * frames
    step = 1.0 / total_frames
    scale = 1.0 / math.sqrt(total_frames * R * tiles * W)
    forward = [(i, i + 1) for i in range(tiles - 1)]
    backward = [(i + 1, i) for i in range(tiles - 1)]
    place = lax.axis_index(SPACE)
    odd = place % 2
    places = jnp.stack([place > 0, place < tiles - 1, odd, frames * (1 - odd),
                        frames * odd + lax.axis_index(TM), frames * odd,
                        lax.axis_index(NEAR[1:]), lax.axis_index(FAR[1:])]).astype(jnp.int32)

    hbm = pl.BlockSpec(memory_space=pltpu.HBM)
    whole = pl.BlockSpec(memory_space=pltpu.VMEM)
    scalars = pl.BlockSpec(memory_space=pltpu.SMEM)
    edge = ((EDGE * C + FIELDS * R, LANES), BF)
    fields = ((4 * R, LANES), F32)
    frame = ((2, R, W), F32)
    own, top, bottom, own_fields = call(
        pack_kernel, [((R * C, LANES), BF), edge, edge, fields],
        [frame, frame, ((2, R, W), jnp.int32), ((R, W), F32), ((2, C, R, W), BF)],
        upstream, equilibrium, coding_masks, measurement, saved_second,
        specs=[hbm] * 5, sems=5, limit=60)
    low = lax.ppermute(bottom, SPACE, forward)
    high = lax.ppermute(top, SPACE, backward)

    forward_w, third_w, second_w, first_w, gate2_own, hidden2, own_fields = call(
        stage_kernel,
        [((C, 3 * Q), BF), ((C, 3 * Q), BF), ((3 * C, 3 * C), BF), ((Q, C), BF),
         ((R * C, LANES), F32), ((R * C, LANES), BF), fields], [],
        places, conv_first, conv_second, conv_third, own, own_fields,
        specs=[scalars] + [whole] * 5,
        cost=pl.CostEstimate(flops=2 * 10**6, bytes_accessed=10**6, transcendentals=0))

    ext = ((EXT, LANES), F32)
    part, up, masks, base = call(
        functools.partial(unpack_kernel, step),
        [((frames, 24, W), F32), ext, ext, ext], [ext, ext],
        low, own_fields, high, gate2_own)
    sums = exchange(part, TM)

    narrow = EXT - 6
    weights = (third_w, second_w, first_w)
    copies = ((2, EXT * Q, W), F32)
    d2 = (((EXT - 2) * C, LANES), BF)
    d1 = (((EXT - 4) * C, LANES), BF)
    taps = ((2, (EXT - 4) * Q, W), F32)
    slim_scratch = [((2, narrow * Q, W), F32), (((narrow - 2) * C, LANES), BF),
                    (((narrow - 4) * C, LANES), BF), ((2, (narrow - 4) * Q, W), F32)]
    wide_outs = [((frames, 16, W), F32), ((narrow, LANES), F32)]
    gate2, back = call(
        early_kernel,
        [(((EXT - 2) * C, LANES), F32), (((EXT - 4) * C, LANES), F32)], [copies, d2],
        places, low, gate2_own, high, up, third_w, second_w, sums,
        specs=[scalars] + [whole] * 7,
        cost=pl.CostEstimate(flops=10**9, bytes_accessed=8 * 10**6, transcendentals=3 * 10**5))
    part, moved, gate1, hidden, inputs = call(
        functools.partial(first_kernel, step),
        wide_outs + [(((EXT - 4) * C, LANES), F32), ((R * C, LANES), BF),
                     (((R + 2) * Q, LANES), BF)],
        [copies, d1, taps],
        places, sums, up, masks, base, back, first_w, forward_w,
        specs=[scalars] + [whole] * 7)
    sums = exchange(part, TM)

    part, moved = call(
        functools.partial(second_kernel, step),
        [((2 * frames, R + R // 2, LANES), F32), ((R, LANES), F32)], slim_scratch,
        sums, moved, up, masks, gate2, gate1, *weights)
    groups = [[t * tiles + (k + side) % tiles for side in range(2) for t in range(frames)]
              for k in range(1, tiles, 2)]
    received = lax.all_to_all(part, TM + SPACE, 0, 0, axis_index_groups=groups, tiled=True)
    field, = call(functools.partial(update_kernel, step), [((R, LANES), F32)], [],
                  places, received, moved, up, masks, specs=[scalars] + [whole] * 4)
    near = lax.ppermute(field, SPACE, [(i, i ^ 1) for i in range(tiles)])
    part, moved = call(
        functools.partial(third_kernel, step), wide_outs, [copies, d2, d1, taps, ext],
        places, received, field, near, up, masks, gate2, gate1, *weights,
        specs=[scalars] + [whole] * 10)
    sums = exchange(part, TM)

    near_sizes = [lax.axis_size(name) for name in NEAR]
    far_sizes = [lax.axis_size(name) for name in FAR]
    near_count = math.prod(near_sizes)
    far_count = math.prod(far_sizes)
    rows = 3 * C // near_count
    piece = -(-(rows + R // 2) // 16) * 16
    adjoint, grads = call(
        functools.partial(last_kernel, step),
        [((2, R, W), F32), ((near_count, piece, LANES), BF)],
        slim_scratch + [((3 * C + piece, LANES), F32)],
        sums, moved, up, masks, gate2, gate1, hidden2, hidden, inputs, *weights)

    received = exchange(grads, NEAR)
    near_stride = near_count // near_sizes[0]
    far_stride = far_count // far_sizes[0]
    received, = call(
        functools.partial(near_kernel, rows, near_stride),
        [((far_count, piece, LANES), BF)], [], places, received, specs=[scalars, whole])
    received = exchange(received, FAR)
    received, snapshot = call(
        functools.partial(far_kernel, rows, far_stride, step),
        [((near_count, piece, LANES), BF), ((R, W), F32)], [], places, received,
        specs=[scalars, whole])
    received = exchange(received, NEAR)
    grad_first, grad_second, grad_third = call(
        functools.partial(output_kernel, scale),
        [((9, C), F32), ((9, C, C), F32), ((9, C), F32)],
        [((3 * C, LANES), F32)], received)
    return adjoint, snapshot, grad_first, grad_second, grad_third


AXES = (("zh", 4), ("core", 2), ("zl", 2), ("y", 8), ("x", 4))


def solution(mesh, axes=AXES):
    names = tuple(name for name, _ in axes)
    sizes = tuple(size for _, size in axes)
    fine = Mesh(mesh.devices.reshape(sizes), names)
    placed = (
        P(TM, SPACE, None),
        P(SPACE, None),
        P(TM, SPACE, None),
        P(TM, SPACE, None),
        P(TM, None, SPACE, None),
        P(),
        P(),
        P(),
    )
    return jax.shard_map(
        per_device,
        mesh=fine,
        in_specs=placed,
        out_specs=(P(TM, SPACE, None), P(SPACE, None), P(), P(), P()),
        check_vma=False,
    )
```

```python
import functools
import math

import jax
import jax.numpy as jnp
from jax import lax
from jax.experimental import pallas as pl
from jax.experimental.pallas import tpu as pltpu
from jax.sharding import Mesh, PartitionSpec as P

ITERS = 3
C = 64
W = 128
LANES = 2 * W
R = 8
HALO = 6
EXT = R + 2 * HALO
EDGE = HALO - 1
FIELDS = 6
Q = 16
PIECE = 32
BF = jnp.bfloat16
F32 = jnp.float32

TM = ("zh", "core")
SPACE = ("zl", "y", "x")
BEFORE, AFTER, ODD, OWN_HALF, THEIR_ENTRY, THEIR_HALF, NEAR_AT, FAR_AT = range(8)
NEAR = ("core", "zl", "x")
FAR = ("zh", "y")


def roll_cols(value, step):
    if step == 0:
        return value
    lane = lax.broadcasted_iota(jnp.int32, (value.shape[0], W), 1)
    edge = 0 if step > 0 else W - 1
    halves = []
    for frame in range(2):
        half = value[:, frame * W:(frame + 1) * W]
        half = pltpu.roll(half, step % W, 1)
        halves.append(jnp.where(lane == edge, 0.0, half))
    return jnp.concatenate(halves, axis=1)


def slope_parts(value):
    logistic = 0.5 * jnp.tanh(0.5 * value) + 0.5
    return logistic, logistic * (1.0 + value * (1.0 - logistic))


def put_slot(ref, at, count, value):
    for frame in range(2):
        ref[frame, pl.ds(at, count, stride=Q), :] = value[:, frame * W:(frame + 1) * W]


def take_slot(ref, at, count):
    return jnp.concatenate(
        [ref[frame, pl.ds(at, count, stride=Q), :] for frame in range(2)], axis=1)


def put_rows(ref, at, value):
    for frame in range(2):
        ref[frame, at:at + value.shape[0], :] = value[:, frame * W:(frame + 1) * W]


def take_rows(ref, first, last):
    return jnp.concatenate([ref[frame, first:last, :] for frame in range(2)], axis=1)


def fill_shifted(field, copies, sign):
    count = field.shape[0]
    for slot, step in enumerate((-1, 0, 1)):
        shifted = roll_cols(field, sign * step)
        high = shifted.astype(BF).astype(F32)
        put_slot(copies, slot, count, high)
        put_slot(copies, 3 + slot, count, shifted - high)


def dot(left, right):
    return jnp.dot(left, right, preferred_element_type=F32)


def dot_nt(left, right):
    return lax.dot_general(left, right, (((1,), (1,)), ((), ())), preferred_element_type=F32)


def back_rows(first, field, gate2, third_w, second_w, copies, d2):
    rows = EXT - 2 * first
    fill_shifted(field, copies, 1)
    for k in range(rows - 2):
        third = dot(third_w, take_rows(copies, k * Q, (k + 3) * Q).astype(BF))
        at = first + k
        d2[k * C:(k + 1) * C, :] = (gate2[at * C:(at + 1) * C, :] * third).astype(BF)
    for k in range(rows - 4):
        parts = dot(second_w, d2[k * C:(k + 3) * C, :])
        total = (
            roll_cols(parts[:C], -1) + parts[C:2 * C] + roll_cols(parts[2 * C:], 1)
        )
        yield k, total


def adjoint_map(first, field, gate2, gate1, third_w, second_w, first_w, copies, d2, d1, taps):
    for k, total in back_rows(first, field, gate2, third_w, second_w, copies, d2):
        at = first + k
        row = (gate1[at * C:(at + 1) * C, :] * total).astype(BF)
        d1[k * C:(k + 1) * C, :] = row
    return map_end(first, field, first_w, d1, taps)


def map_end(first, field, first_w, d1, taps):
    count = EXT - 2 * first - 6
    for k in range(count + 2):
        put_rows(taps, k * Q, dot(first_w, d1[k * C:(k + 1) * C, :]))
    result = field[3:3 + count]
    for j in (-1, 0, 1):
        column = None
        for i in (-1, 0, 1):
            tap = 3 * (i + 1) + (j + 1)
            part = take_slot(taps, (1 - i) * Q + tap, count)
            column = part if column is None else column + part
        result = result + roll_cols(column, j)
    return result


def masked_sum(masks, field):
    product = masks * field
    return product[:, :W] + product[:, W:]


def twice(field):
    return jnp.concatenate([field, field], axis=1)


def gathered_sum(ref):
    total = ref[0]
    for k in range(1, ref.shape[0]):
        total = total + ref[k]
    return total


def pack_kernel(upstream, equilibrium, masks, measurement, saved, top, bottom, own_fields,
                up_in, fixed_in, masks_in, snapshot_in, saved_in, sems):
    copies = [
        pltpu.make_async_copy(source, target, sems.at[k])
        for k, (source, target) in enumerate((
            (saved, saved_in), (upstream, up_in), (equilibrium, fixed_in), (masks, masks_in),
            (measurement, snapshot_in)))
    ]
    for copy in copies:
        copy.start()
    for copy in copies[1:]:
        copy.wait()

    def by_frame(ref):
        return jnp.concatenate([ref[0], ref[1]], axis=1)

    up = by_frame(up_in)
    fixed = by_frame(fixed_in)
    mask = by_frame(masks_in).astype(F32)
    snapshot = snapshot_in[...]
    for k, field in enumerate((up, mask, fixed, twice(snapshot))):
        own_fields[k * R:(k + 1) * R, :] = field
    fields = (*split_parts(up), *split_parts(fixed), mask.astype(BF),
              jnp.concatenate(split_parts(snapshot), axis=1))
    for k in range(0, len(fields), 2):
        pair = jnp.concatenate([field.astype(F32) for field in fields[k:k + 2]], axis=0).astype(BF)
        at = EDGE * C + k * R
        top[at:at + 2 * R, :] = pair
        bottom[at:at + 2 * R, :] = pair
    copies[0].wait()
    for frame in range(2):
        lanes = slice(frame * W, (frame + 1) * W)
        rows = jnp.swapaxes(saved_in[frame].astype(F32), 0, 1).astype(BF).reshape(R * C, W)
        top[:EDGE * C, lanes] = rows[:EDGE * C]
        bottom[:EDGE * C, lanes] = rows[(R - EDGE) * C:]


def stage_kernel(places, first, second, third, saved, own_fields, forward_w, third_w, second_w,
                 first_w, gate2, hidden2, fields, table):
    fields[...] = own_fields[...]
    for k in range(8):
        table[k:k + 1, :] = jnp.full((1, W), places[k], jnp.int32)
    for frame in range(2):
        lanes = slice(frame * W, (frame + 1) * W)
        value = jnp.swapaxes(saved[frame].astype(F32), 0, 1).reshape(R * C, W)
        logistic, slope = slope_parts(value)
        gate2[:, lanes] = slope
        hidden2[:, lanes] = (value * logistic).astype(BF)
    forward = first[...].astype(F32)
    backward = third[...].astype(F32)
    pad = jnp.zeros((Q - 6, C), F32)
    ahead = []
    back = []
    for i in range(3):
        row = forward[3 * i:3 * i + 3]
        ahead += [row, row, pad]
        row = backward[6 - 3 * i:9 - 3 * i]
        back += [row, row, pad]
        for j in range(3):
            tile = second[3 * (2 - i) + j].astype(F32)
            second_w[j * C:(j + 1) * C, i * C:(i + 1) * C] = jnp.transpose(tile).astype(BF)
    forward_w[...] = jnp.transpose(jnp.concatenate(ahead, axis=0)).astype(BF)
    third_w[...] = jnp.transpose(jnp.concatenate(back, axis=0)).astype(BF)
    first_w[...] = jnp.concatenate([forward, jnp.zeros((Q - 9, C), F32)], axis=0).astype(BF)


def unpack_kernel(step, low, own_fields, high, _, part, up, masks, base, fixed, snapshot):
    for k, target in enumerate((up, masks, fixed, snapshot)):
        target[HALO:HALO + R, :] = own_fields[k * R:(k + 1) * R, :]
    for ref, at, first in ((low, 0, R - HALO), (high, HALO + R, 0)):
        fields = ref[EDGE * C:EDGE * C + FIELDS * R, :].astype(F32)

        def field(k):
            return fields[k * R:(k + 1) * R]

        for target, value in ((up, field(0) + field(1)), (fixed, field(2) + field(3)),
                              (masks, field(4)),
                              (snapshot, twice(field(5)[:, :W] + field(5)[:, W:]))):
            target[at:at + HALO, :] = value[first:first + HALO]
    total = masked_sum(masks[...], fixed[...])
    for k in range(part.shape[0]):
        part[k, 0:EXT, :] = total
        part[k, EXT:, :] = jnp.zeros((part.shape[1] - EXT, W), F32)
    base[...] = fixed[...] + step * masks[...] * snapshot[...]


def saved_row(ref, at):
    return ref[at * C:(at + 1) * C, :]


def keep_row(value, at, before, after):
    if at < HALO:
        return value * before
    if at >= HALO + R:
        return value * after
    return value


def ends(places):
    return tuple(twice(places[k:k + 1, :]).astype(F32) for k in (BEFORE, AFTER))


def first_kernel(step, places, sums, low, own, high, up, masks, base, third_w, second_w, first_w,
                 forward_w, part, moved, gate2, gate1, hidden, inputs, copies, d2, d1, taps):
    before, after = ends(places)
    for k in range(EXT - 2):
        at = k + 1
        if HALO <= at < HALO + R:
            gate2[k * C:(k + 1) * C, :] = saved_row(own, at - HALO)
        else:
            value = saved_row(low, k) if at < HALO else saved_row(high, at - HALO - R)
            slope = slope_parts(value.astype(F32))[1]
            gate2[k * C:(k + 1) * C, :] = keep_row(slope, at, before, after)
    frame_sum = gathered_sum(sums)[:EXT]
    denoiser_input = base[...] - step * masks[...] * twice(frame_sum)
    copies[...] = jnp.zeros_like(copies)
    fill_shifted(denoiser_input, copies, -1)
    inputs[...] = take_rows(copies, (HALO - 1) * Q, (HALO + R + 1) * Q).astype(BF)
    for k in range(EXT - 4):
        at = k + 2
        value = dot(forward_w[...], take_rows(copies, (at - 1) * Q, (at + 2) * Q).astype(BF))
        logistic, slope = slope_parts(value)
        gate1[k * C:(k + 1) * C, :] = keep_row(slope, at, before, after)
        if HALO <= at < HALO + R:
            own_at = at - HALO
            hidden[own_at * C:(own_at + 1) * C, :] = (value * logistic).astype(BF)
    field = adjoint_map(0, up[...], gate2, gate1, third_w[...], second_w[...], first_w[...],
                        copies, d2, d1, taps)
    finish_wide(field, before, after, masks, part, moved)


def finish_wide(field, before, after, masks, part, moved):
    count = EXT - 6
    row = lax.broadcasted_iota(jnp.int32, field.shape, 0)
    keep = jnp.where(row < HALO - 3, before, jnp.where(row >= HALO - 3 + R, after, 1.0))
    field = field * keep
    moved[...] = field
    total = masked_sum(masks[3:3 + count, :], field)
    for k in range(part.shape[0]):
        part[k, 0:count, :] = total
        part[k, count:, :] = jnp.zeros((part.shape[1] - count, W), F32)


def narrow_field(step, sums, moved, up, masks):
    count = EXT - 6
    totals = gathered_sum(sums)[:count]
    return up[3:3 + count, :] + moved[...] - step * masks[3:3 + count, :] * twice(totals)


def second_kernel(step, sums, moved, up, masks, gate2, gate1, third_w, second_w, first_w,
                  part, out, copies, d2, d1, taps):
    copies[...] = jnp.zeros_like(copies)
    field = narrow_field(step, sums, moved, up, masks)
    result = adjoint_map(3, field, gate2, gate1, third_w[...], second_w[...], first_w[...],
                         copies, d2, d1, taps)
    out[...] = result
    total = masked_sum(masks[HALO:HALO + R, :], result)
    half = jnp.concatenate([total[:R // 2], total[R // 2:]], axis=1)
    for k in range(part.shape[0]):
        part[k, 0:R, :] = result
        part[k, R:, :] = half


def pair_total(received, first):
    count = received.shape[0] // 2
    half = received[first, R:, :]
    for k in range(1, count):
        half = half + received[first + k, R:, :]
    return jnp.concatenate([half[:, :W], half[:, W:]], axis=0)


def update_kernel(step, places, received, moved, up, masks, out):
    totals = pair_total(received, places[OWN_HALF, 0])
    out[...] = (up[HALO:HALO + R, :] + moved[...]
                - step * masks[HALO:HALO + R, :] * twice(totals))


def third_kernel(step, places, received, own, near, up, masks, gate2, gate1, third_w,
                 second_w, first_w, part, moved, copies, d2, d1, taps, whole):
    copies[...] = jnp.zeros_like(copies)
    before, after = ends(places)
    totals = twice(pair_total(received, places[THEIR_HALF, 0]))
    theirs = received[places[THEIR_ENTRY, 0], 0:R, :]
    after_rows = slice(HALO + R, EXT)
    low = (up[0:HALO, :] + theirs[R - HALO:]
           - step * masks[0:HALO, :] * totals[R - HALO:]) * before
    high = (up[after_rows, :] + theirs[:HALO]
            - step * masks[after_rows, :] * totals[:HALO]) * after
    odd = twice(places[ODD:ODD + 1, :]) == 1
    whole[0:HALO, :] = jnp.where(odd, near[R - HALO:, :], low)
    whole[HALO:HALO + R, :] = own[...]
    whole[HALO + R:, :] = jnp.where(odd, high, near[:HALO, :])
    field = adjoint_map(0, whole[...], gate2, gate1, third_w[...], second_w[...], first_w[...],
                        copies, d2, d1, taps)
    finish_wide(field, before, after, masks, part, moved)


def last_kernel(step, sums, moved, up, masks, gate2, gate1, hidden2, hidden, inputs, third_w,
                second_w, first_w, adjoint, grads, copies, d2, d1, taps, total):
    copies[...] = jnp.zeros_like(copies)
    field = narrow_field(step, sums, moved, up, masks)
    adjoint[0] = field[3:3 + R, :W]
    adjoint[1] = field[3:3 + R, W:]
    result = adjoint_map(3, field, gate2, gate1, third_w[...], second_w[...], first_w[...],
                         copies, d2, d1, taps)
    snapshot = masked_sum(masks[HALO:HALO + R, :], result)
    left = []
    right = []
    left_first = []
    right_first = []
    left_third = []
    right_third = []
    for r in range(R):
        left.append(d2[(r + 1) * C:(r + 4) * C, :])
        value = hidden[r * C:(r + 1) * C, :].astype(F32)
        right.append(jnp.concatenate(
            [roll_cols(value, 1), value, roll_cols(value, -1)], axis=0).astype(BF))
        left_first.append(inputs[r * Q:(r + 3) * Q, :])
        right_first.append(d1[(r + 1) * C:(r + 2) * C, :])
        left_third.append(take_rows(copies, (r + 2) * Q, (r + 5) * Q).astype(BF))
        right_third.append(saved_row(hidden2, r))
    def join(parts):
        return jnp.concatenate(parts, axis=1)
    second = dot_nt(join(left), join(right))
    first = dot_nt(join(left_first), join(right_first))
    third = dot_nt(join(left_third), join(right_third))
    total[0:3 * C, 0:3 * C] = second
    total[0:3 * Q, 3 * C:] = first
    total[3 * Q:6 * Q, 3 * C:] = third
    total[6 * Q:, 3 * C:] = jnp.zeros((total.shape[0] - 6 * Q, C), F32)
    total[3 * C:, 0:3 * C] = jnp.zeros((total.shape[0] - 3 * C, 3 * C), F32)
    count = grads.shape[0]
    rows = 3 * C // count
    line = lax.broadcasted_iota(jnp.int32, grads.shape[1:], 0)
    extra = jnp.zeros(grads.shape[1:], F32)
    for k in range(R // 2):
        pair = jnp.concatenate([snapshot[2 * k:2 * k + 1], snapshot[2 * k + 1:2 * k + 2]], axis=1)
        extra = jnp.where(line == rows + k, pair, extra)
    for k in range(count):
        grads[k] = jnp.where(line < rows, total[k * rows:k * rows + grads.shape[1], :],
                             extra).astype(BF)


def reduce_pieces(rows, place, stride, received):
    count = received.shape[0]
    total = received[0].astype(F32)
    for k in range(1, count):
        total = total + received[k].astype(F32)
    extra = received[place].astype(F32)
    for k in range(1, count // stride):
        extra = extra + received[place + k * stride].astype(F32)
    line = lax.broadcasted_iota(jnp.int32, total.shape, 0)
    return jnp.where(line < rows, total, extra)


def near_kernel(rows, stride, places, received, out):
    total = reduce_pieces(rows, places[NEAR_AT, 0], stride, received).astype(BF)
    for k in range(out.shape[0]):
        out[k] = total


def far_kernel(rows, stride, step, places, received, out, snapshot):
    total = reduce_pieces(rows, places[FAR_AT, 0], stride, received)
    for k in range(R // 2):
        snapshot[2 * k:2 * k + 1, :] = step * total[rows + k:rows + k + 1, :W]
        snapshot[2 * k + 1:2 * k + 2, :] = step * total[rows + k:rows + k + 1, W:]
    total = total.astype(BF)
    for k in range(out.shape[0]):
        out[k] = total


def output_kernel(scale, received, first, second, third, total):
    count = received.shape[0]
    rows = 3 * C // count
    for k in range(count):
        total[k * rows:(k + 1) * rows, :] = received[k].astype(F32)[:rows] * scale
    for i in (-1, 0, 1):
        for j in (-1, 0, 1):
            tap = 3 * (i + 1) + (j + 1)
            back = 1 - i
            ahead = 1 + i
            second[tap] = total[back * C:(back + 1) * C, (j + 1) * C:(j + 2) * C]
            at = ahead * Q + j + 1
            first[tap:tap + 1, :] = total[at:at + 1, 3 * C:] + total[at + 3:at + 4, 3 * C:]
            at = 3 * Q + back * Q + j + 1
            third[tap:tap + 1, :] = total[at:at + 1, 3 * C:] + total[at + 3:at + 4, 3 * C:]


def call(kernel, outs, scratch, *operands, specs=None, cost=None, sems=0, limit=40):
    if specs is None:
        specs = [pl.BlockSpec(memory_space=pltpu.VMEM)] * len(operands)
    return pl.pallas_call(
        kernel,
        out_shape=[jax.ShapeDtypeStruct(shape, dtype) for shape, dtype in outs],
        in_specs=specs,
        out_specs=[pl.BlockSpec(memory_space=pltpu.VMEM)] * len(outs),
        scratch_shapes=[pltpu.VMEM(shape, dtype) for shape, dtype in scratch]
        + [pltpu.SemaphoreType.DMA((sems,))] * (sems > 0),
        compiler_params=pltpu.CompilerParams(vmem_limit_bytes=limit * 2**20),
        cost_estimate=cost,
    )(*operands)


def split_parts(field):
    high = field.astype(BF)
    return high, (field - high.astype(F32)).astype(BF)


def exchange(value, axis):
    return lax.all_to_all(value, axis, 0, 0, tiled=True)


def per_device(equilibrium, measurement, coding_masks, upstream, saved_second, conv_first,
               conv_second, conv_third):
    frames = lax.axis_size(TM)
    tiles = lax.axis_size(SPACE)
    total_frames = 2 * frames
    step = 1.0 / total_frames
    scale = 1.0 / math.sqrt(total_frames * R * tiles * W)
    forward = [(i, i + 1) for i in range(tiles - 1)]
    backward = [(i + 1, i) for i in range(tiles - 1)]
    place = lax.axis_index(SPACE)
    odd = place % 2
    places = jnp.stack([place > 0, place < tiles - 1, odd, frames * (1 - odd),
                        frames * odd + lax.axis_index(TM), frames * odd,
                        lax.axis_index(NEAR[1:]), lax.axis_index(FAR[1:])]).astype(jnp.int32)

    hbm = pl.BlockSpec(memory_space=pltpu.HBM)
    whole = pl.BlockSpec(memory_space=pltpu.VMEM)
    scalars = pl.BlockSpec(memory_space=pltpu.SMEM)
    edge = ((EDGE * C + FIELDS * R, LANES), BF)
    fields = ((4 * R, LANES), F32)
    frame = ((2, R, W), F32)
    top, bottom, own_fields = call(
        pack_kernel, [edge, edge, fields],
        [frame, frame, ((2, R, W), jnp.int32), ((R, W), F32), ((2, C, R, W), BF)],
        upstream, equilibrium, coding_masks, measurement, saved_second,
        specs=[hbm] * 5, sems=5, limit=60)
    low = lax.ppermute(bottom, SPACE, forward)
    high = lax.ppermute(top, SPACE, backward)

    forward_w, third_w, second_w, first_w, gate2_own, hidden2, own_fields, table = call(
        stage_kernel,
        [((C, 3 * Q), BF), ((C, 3 * Q), BF), ((3 * C, 3 * C), BF), ((Q, C), BF),
         ((R * C, LANES), F32), ((R * C, LANES), BF), fields, ((8, W), jnp.int32)], [],
        places, conv_first, conv_second, conv_third, saved_second, own_fields,
        specs=[scalars] + [whole] * 5,
        cost=pl.CostEstimate(flops=2 * 10**6, bytes_accessed=10**6, transcendentals=0))

    ext = ((EXT, LANES), F32)
    part, up, masks, base = call(
        functools.partial(unpack_kernel, step),
        [((frames, 24, W), F32), ext, ext, ext], [ext, ext],
        low, own_fields, high, gate2_own)
    sums = exchange(part, TM)

    narrow = EXT - 6
    weights = (third_w, second_w, first_w)
    copies = ((2, EXT * Q, W), F32)
    d2 = (((EXT - 2) * C, LANES), BF)
    d1 = (((EXT - 4) * C, LANES), BF)
    taps = ((2, (EXT - 4) * Q, W), F32)
    slim_scratch = [((2, narrow * Q, W), F32), (((narrow - 2) * C, LANES), BF),
                    (((narrow - 4) * C, LANES), BF), ((2, (narrow - 4) * Q, W), F32)]
    wide_outs = [((frames, 16, W), F32), ((narrow, LANES), F32)]
    part, moved, gate2, gate1, hidden, inputs = call(
        functools.partial(first_kernel, step),
        wide_outs + [(((EXT - 2) * C, LANES), F32), (((EXT - 4) * C, LANES), F32),
                     ((R * C, LANES), BF), (((R + 2) * Q, LANES), BF)],
        [copies, d2, d1, taps],
        table, sums, low, gate2_own, high, up, masks, base, *weights, forward_w)
    sums = exchange(part, TM)

    part, moved = call(
        functools.partial(second_kernel, step),
        [((2 * frames, R + R // 2, LANES), F32), ((R, LANES), F32)], slim_scratch,
        sums, moved, up, masks, gate2, gate1, *weights)
    groups = [[t * tiles + (k + side) % tiles for side in range(2) for t in range(frames)]
              for k in range(1, tiles, 2)]
    received = lax.all_to_all(part, TM + SPACE, 0, 0, axis_index_groups=groups, tiled=True)
    field, = call(functools.partial(update_kernel, step), [((R, LANES), F32)], [],
                  table, received, moved, up, masks)
    near = lax.ppermute(field, SPACE, [(i, i ^ 1) for i in range(tiles)])
    part, moved = call(
        functools.partial(third_kernel, step), wide_outs, [copies, d2, d1, taps, ext],
        table, received, field, near, up, masks, gate2, gate1, *weights)
    sums = exchange(part, TM)

    near_sizes = [lax.axis_size(name) for name in NEAR]
    far_sizes = [lax.axis_size(name) for name in FAR]
    near_count = math.prod(near_sizes)
    far_count = math.prod(far_sizes)
    rows = 3 * C // near_count
    piece = -(-(rows + R // 2) // 16) * 16
    adjoint, grads = call(
        functools.partial(last_kernel, step),
        [((2, R, W), F32), ((near_count, piece, LANES), BF)],
        slim_scratch + [((3 * C + piece, LANES), F32)],
        sums, moved, up, masks, gate2, gate1, hidden2, hidden, inputs, *weights)

    received = exchange(grads, NEAR)
    near_stride = near_count // near_sizes[0]
    far_stride = far_count // far_sizes[0]
    received, = call(
        functools.partial(near_kernel, rows, near_stride),
        [((far_count, piece, LANES), BF)], [], table, received)
    received = exchange(received, FAR)
    received, snapshot = call(
        functools.partial(far_kernel, rows, far_stride, step),
        [((near_count, piece, LANES), BF), ((R, W), F32)], [], table, received)
    received = exchange(received, NEAR)
    grad_first, grad_second, grad_third = call(
        functools.partial(output_kernel, scale),
        [((9, C), F32), ((9, C, C), F32), ((9, C), F32)],
        [((3 * C, LANES), F32)], received)
    return adjoint, snapshot, grad_first, grad_second, grad_third


AXES = (("zh", 4), ("core", 2), ("zl", 2), ("y", 8), ("x", 4))


def solution(mesh, axes=AXES):
    names = tuple(name for name, _ in axes)
    sizes = tuple(size for _, size in axes)
    fine = Mesh(mesh.devices.reshape(sizes), names)
    placed = (
        P(TM, SPACE, None),
        P(SPACE, None),
        P(TM, SPACE, None),
        P(TM, SPACE, None),
        P(TM, None, SPACE, None),
        P(),
        P(),
        P(),
    )
    return jax.shard_map(
        per_device,
        mesh=fine,
        in_specs=placed,
        out_specs=(P(TM, SPACE, None), P(SPACE, None), P(), P(), P()),
        check_vma=False,
    )
```

```python
import functools
import math

import jax
import jax.numpy as jnp
from jax import lax
from jax.experimental import pallas as pl
from jax.experimental.pallas import tpu as pltpu
from jax.sharding import Mesh, PartitionSpec as P

ITERS = 3
C = 64
W = 128
LANES = 2 * W
R = 8
HALO = 6
EXT = R + 2 * HALO
EDGE = HALO - 1
FIELDS = 6
Q = 16
PIECE = 32
BF = jnp.bfloat16
F32 = jnp.float32

TM = ("zh", "core")
SPACE = ("zl", "y", "x")
BEFORE, AFTER, ODD, OWN_HALF, THEIR_ENTRY, THEIR_HALF, NEAR_AT, FAR_AT = range(8)
NEAR = ("core", "zl", "x")
FAR = ("zh", "y")


def roll_cols(value, step):
    if step == 0:
        return value
    lane = lax.broadcasted_iota(jnp.int32, (value.shape[0], W), 1)
    edge = 0 if step > 0 else W - 1
    halves = []
    for frame in range(2):
        half = value[:, frame * W:(frame + 1) * W]
        half = pltpu.roll(half, step % W, 1)
        halves.append(jnp.where(lane == edge, 0.0, half))
    return jnp.concatenate(halves, axis=1)


def slope_parts(value):
    logistic = 0.5 * jnp.tanh(0.5 * value) + 0.5
    return logistic, logistic * (1.0 + value * (1.0 - logistic))


def put_slot(ref, at, count, value):
    for frame in range(2):
        ref[frame, pl.ds(at, count, stride=Q), :] = value[:, frame * W:(frame + 1) * W]


def take_slot(ref, at, count):
    return jnp.concatenate(
        [ref[frame, pl.ds(at, count, stride=Q), :] for frame in range(2)], axis=1)


def put_rows(ref, at, value):
    for frame in range(2):
        ref[frame, at:at + value.shape[0], :] = value[:, frame * W:(frame + 1) * W]


def take_rows(ref, first, last):
    return jnp.concatenate([ref[frame, first:last, :] for frame in range(2)], axis=1)


def fill_shifted(field, copies, sign):
    count = field.shape[0]
    for slot, step in enumerate((-1, 0, 1)):
        shifted = roll_cols(field, sign * step)
        high = shifted.astype(BF).astype(F32)
        put_slot(copies, slot, count, high)
        put_slot(copies, 3 + slot, count, shifted - high)


def dot(left, right):
    return jnp.dot(left, right, preferred_element_type=F32)


def dot_nt(left, right):
    return lax.dot_general(left, right, (((1,), (1,)), ((), ())), preferred_element_type=F32)


def back_rows(first, field, gate2, third_w, second_w, copies, d2):
    rows = EXT - 2 * first
    fill_shifted(field, copies, 1)
    for k in range(rows - 2):
        third = dot(third_w, take_rows(copies, k * Q, (k + 3) * Q).astype(BF))
        at = first + k
        d2[k * C:(k + 1) * C, :] = (gate2[at * C:(at + 1) * C, :] * third).astype(BF)
    for k in range(rows - 4):
        parts = dot(second_w, d2[k * C:(k + 3) * C, :])
        total = (
            roll_cols(parts[:C], -1) + parts[C:2 * C] + roll_cols(parts[2 * C:], 1)
        )
        yield k, total


def adjoint_map(first, field, gate2, gate1, third_w, second_w, first_w, copies, d2, d1, taps):
    for k, total in back_rows(first, field, gate2, third_w, second_w, copies, d2):
        at = first + k
        row = (gate1[at * C:(at + 1) * C, :] * total).astype(BF)
        d1[k * C:(k + 1) * C, :] = row
    return map_end(first, field, first_w, d1, taps)


def map_end(first, field, first_w, d1, taps):
    count = EXT - 2 * first - 6
    for k in range(count + 2):
        put_rows(taps, k * Q, dot(first_w, d1[k * C:(k + 1) * C, :]))
    result = field[3:3 + count]
    for j in (-1, 0, 1):
        column = None
        for i in (-1, 0, 1):
            tap = 3 * (i + 1) + (j + 1)
            part = take_slot(taps, (1 - i) * Q + tap, count)
            column = part if column is None else column + part
        result = result + roll_cols(column, j)
    return result


def masked_sum(masks, field):
    product = masks * field
    return product[:, :W] + product[:, W:]


def twice(field):
    return jnp.concatenate([field, field], axis=1)


def gathered_sum(ref):
    total = ref[0].astype(F32)
    for k in range(1, ref.shape[0]):
        total = total + ref[k].astype(F32)
    return total


def send_all(part, value):
    fill = jnp.zeros((part.shape[1] - value.shape[0], value.shape[1]), F32)
    value = jnp.concatenate([value, fill], axis=0).astype(part.dtype)
    for k in range(part.shape[0]):
        part[k] = value


def pack_kernel(upstream, equilibrium, masks, measurement, saved, top, bottom, own_fields,
                up_in, fixed_in, masks_in, snapshot_in, saved_in, top_out, bottom_out, sems):
    arrivals = [
        pltpu.make_async_copy(source, target, sems.at[k])
        for k, (source, target) in enumerate((
            (saved.at[0], saved_in.at[0]), (saved.at[1], saved_in.at[1]), (upstream, up_in),
            (equilibrium, fixed_in), (masks, masks_in), (measurement, snapshot_in)))
    ]
    for copy in arrivals:
        copy.start()
    for copy in arrivals[2:]:
        copy.wait()

    def by_frame(ref):
        return jnp.concatenate([ref[0], ref[1]], axis=1)

    up = by_frame(up_in)
    fixed = by_frame(fixed_in)
    mask = by_frame(masks_in).astype(F32)
    snapshot = snapshot_in[...]
    for k, field in enumerate((up, mask, fixed, twice(snapshot))):
        own_fields[k * R:(k + 1) * R, :] = field
    fields = (*split_parts(up), *split_parts(fixed), mask.astype(BF),
              jnp.concatenate(split_parts(snapshot), axis=1))
    for k in range(0, len(fields), 2):
        pair = jnp.concatenate([field.astype(F32) for field in fields[k:k + 2]], axis=0).astype(BF)
        at = EDGE * C + k * R
        top_out[at:at + 2 * R, :] = pair
        bottom_out[at:at + 2 * R, :] = pair
    departures = []
    for frame in range(2):
        lanes = slice(frame * W, (frame + 1) * W)
        arrivals[frame].wait()
        rows = jnp.swapaxes(saved_in[frame].astype(F32), 0, 1).astype(BF).reshape(R * C, W)
        for value, here, there in ((rows[:EDGE * C], top_out, top),
                                   (rows[(R - EDGE) * C:], bottom_out, bottom)):
            here[:EDGE * C, lanes] = value
            copy = pltpu.make_async_copy(here.at[:, lanes], there.at[:, lanes],
                                         sems.at[len(arrivals) + len(departures)])
            copy.start()
            departures.append(copy)
    for copy in departures:
        copy.wait()


def stage_kernel(places, first, second, third, saved, own_fields, forward_w, third_w, second_w,
                 first_w, gate2, hidden2, fields, table):
    fields[...] = own_fields[...]
    for k in range(8):
        table[k:k + 1, :] = jnp.full((1, W), places[k], jnp.int32)
    for frame in range(2):
        lanes = slice(frame * W, (frame + 1) * W)
        value = jnp.swapaxes(saved[frame].astype(F32), 0, 1).reshape(R * C, W)
        logistic, slope = slope_parts(value)
        gate2[:, lanes] = slope
        hidden2[:, lanes] = (value * logistic).astype(BF)
    forward = first[...].astype(F32)
    backward = third[...].astype(F32)
    pad = jnp.zeros((Q - 6, C), F32)
    ahead = []
    back = []
    for i in range(3):
        row = forward[3 * i:3 * i + 3]
        ahead += [row, row, pad]
        row = backward[6 - 3 * i:9 - 3 * i]
        back += [row, row, pad]
        for j in range(3):
            tile = second[3 * (2 - i) + j].astype(F32)
            second_w[j * C:(j + 1) * C, i * C:(i + 1) * C] = jnp.transpose(tile).astype(BF)
    forward_w[...] = jnp.transpose(jnp.concatenate(ahead, axis=0)).astype(BF)
    third_w[...] = jnp.transpose(jnp.concatenate(back, axis=0)).astype(BF)
    first_w[...] = jnp.concatenate([forward, jnp.zeros((Q - 9, C), F32)], axis=0).astype(BF)


def unpack_kernel(step, low, own_fields, high, _, part, up, masks, base, fixed, snapshot):
    for k, target in enumerate((up, masks, fixed, snapshot)):
        target[HALO:HALO + R, :] = own_fields[k * R:(k + 1) * R, :]
    for ref, at, first in ((low, 0, R - HALO), (high, HALO + R, 0)):
        fields = ref[EDGE * C:EDGE * C + FIELDS * R, :].astype(F32)

        def field(k):
            return fields[k * R:(k + 1) * R]

        for target, value in ((up, field(0) + field(1)), (fixed, field(2) + field(3)),
                              (masks, field(4)),
                              (snapshot, twice(field(5)[:, :W] + field(5)[:, W:]))):
            target[at:at + HALO, :] = value[first:first + HALO]
    send_all(part, masked_sum(masks[...], fixed[...]))
    base[...] = fixed[...] + step * masks[...] * snapshot[...]


def saved_row(ref, at):
    return ref[at * C:(at + 1) * C, :]


def keep_row(value, at, before, after):
    if at < HALO:
        return value * before
    if at >= HALO + R:
        return value * after
    return value


def ends(places):
    return tuple(twice(places[k:k + 1, :]).astype(F32) for k in (BEFORE, AFTER))


def first_kernel(step, places, sums, low, own, high, up, masks, base, third_w, second_w, first_w,
                 forward_w, part, moved, gate2, gate1, hidden, inputs, copies, d2, d1, taps):
    before, after = ends(places)
    for k in range(EXT - 2):
        at = k + 1
        if HALO <= at < HALO + R:
            gate2[k * C:(k + 1) * C, :] = saved_row(own, at - HALO)
        else:
            value = saved_row(low, k) if at < HALO else saved_row(high, at - HALO - R)
            slope = slope_parts(value.astype(F32))[1]
            gate2[k * C:(k + 1) * C, :] = keep_row(slope, at, before, after)
    frame_sum = gathered_sum(sums)[:EXT]
    denoiser_input = base[...] - step * masks[...] * twice(frame_sum)
    copies[...] = jnp.zeros_like(copies)
    fill_shifted(denoiser_input, copies, -1)
    inputs[...] = take_rows(copies, (HALO - 1) * Q, (HALO + R + 1) * Q).astype(BF)
    for k in range(EXT - 4):
        at = k + 2
        value = dot(forward_w[...], take_rows(copies, (at - 1) * Q, (at + 2) * Q).astype(BF))
        logistic, slope = slope_parts(value)
        gate1[k * C:(k + 1) * C, :] = keep_row(slope, at, before, after)
        if HALO <= at < HALO + R:
            own_at = at - HALO
            hidden[own_at * C:(own_at + 1) * C, :] = (value * logistic).astype(BF)
    field = adjoint_map(0, up[...], gate2, gate1, third_w[...], second_w[...], first_w[...],
                        copies, d2, d1, taps)
    finish_wide(field, before, after, masks, part, moved)


def finish_wide(field, before, after, masks, part, moved):
    count = EXT - 6
    row = lax.broadcasted_iota(jnp.int32, field.shape, 0)
    keep = jnp.where(row < HALO - 3, before, jnp.where(row >= HALO - 3 + R, after, 1.0))
    field = field * keep
    moved[...] = field
    send_all(part, masked_sum(masks[3:3 + count, :], field))


def narrow_field(step, sums, moved, up, masks):
    count = EXT - 6
    totals = gathered_sum(sums)[:count]
    return up[3:3 + count, :] + moved[...] - step * masks[3:3 + count, :] * twice(totals)


def second_kernel(step, sums, moved, up, masks, gate2, gate1, third_w, second_w, first_w,
                  part, out, copies, d2, d1, taps):
    copies[...] = jnp.zeros_like(copies)
    field = narrow_field(step, sums, moved, up, masks)
    result = adjoint_map(3, field, gate2, gate1, third_w[...], second_w[...], first_w[...],
                         copies, d2, d1, taps)
    out[...] = result
    total = masked_sum(masks[HALO:HALO + R, :], result)
    half = jnp.concatenate([total[:R // 2], total[R // 2:]], axis=1)
    send_all(part, jnp.concatenate([result, half], axis=0))


def pair_total(received, first):
    count = received.shape[0] // 2
    half = received[first].astype(F32)
    for k in range(1, count):
        half = half + received[first + k].astype(F32)
    half = half[R:R + R // 2]
    return jnp.concatenate([half[:, :W], half[:, W:]], axis=0)


def update_kernel(step, places, received, moved, up, masks, out):
    totals = pair_total(received, places[OWN_HALF, 0])
    out[...] = (up[HALO:HALO + R, :] + moved[...]
                - step * masks[HALO:HALO + R, :] * twice(totals))


def third_kernel(step, places, received, own, near, up, masks, gate2, gate1, third_w,
                 second_w, first_w, part, moved, copies, d2, d1, taps, whole):
    copies[...] = jnp.zeros_like(copies)
    before, after = ends(places)
    totals = twice(pair_total(received, places[THEIR_HALF, 0]))
    theirs = received[places[THEIR_ENTRY, 0]].astype(F32)[:R]
    after_rows = slice(HALO + R, EXT)
    low = (up[0:HALO, :] + theirs[R - HALO:]
           - step * masks[0:HALO, :] * totals[R - HALO:]) * before
    high = (up[after_rows, :] + theirs[:HALO]
            - step * masks[after_rows, :] * totals[:HALO]) * after
    odd = twice(places[ODD:ODD + 1, :]) == 1
    whole[0:HALO, :] = jnp.where(odd, near[R - HALO:, :], low)
    whole[HALO:HALO + R, :] = own[...]
    whole[HALO + R:, :] = jnp.where(odd, high, near[:HALO, :])
    field = adjoint_map(0, whole[...], gate2, gate1, third_w[...], second_w[...], first_w[...],
                        copies, d2, d1, taps)
    finish_wide(field, before, after, masks, part, moved)


def last_kernel(step, sums, moved, up, masks, gate2, gate1, hidden2, hidden, inputs, third_w,
                second_w, first_w, adjoint, grads, copies, d2, d1, taps, total):
    copies[...] = jnp.zeros_like(copies)
    field = narrow_field(step, sums, moved, up, masks)
    adjoint[...] = field[3:3 + R]
    result = adjoint_map(3, field, gate2, gate1, third_w[...], second_w[...], first_w[...],
                         copies, d2, d1, taps)
    snapshot = masked_sum(masks[HALO:HALO + R, :], result)
    left = []
    right = []
    left_first = []
    right_first = []
    left_third = []
    right_third = []
    for r in range(R):
        left.append(d2[(r + 1) * C:(r + 4) * C, :])
        value = hidden[r * C:(r + 1) * C, :].astype(F32)
        right.append(jnp.concatenate(
            [roll_cols(value, 1), value, roll_cols(value, -1)], axis=0).astype(BF))
        left_first.append(inputs[r * Q:(r + 3) * Q, :])
        right_first.append(d1[(r + 1) * C:(r + 2) * C, :])
        left_third.append(take_rows(copies, (r + 2) * Q, (r + 5) * Q).astype(BF))
        right_third.append(saved_row(hidden2, r))
    def join(parts):
        return jnp.concatenate(parts, axis=1)
    second = dot_nt(join(left), join(right))
    first = dot_nt(join(left_first), join(right_first))
    third = dot_nt(join(left_third), join(right_third))
    total[0:3 * C, 0:3 * C] = second
    total[0:3 * Q, 3 * C:] = first
    total[3 * Q:6 * Q, 3 * C:] = third
    total[6 * Q:, 3 * C:] = jnp.zeros((total.shape[0] - 6 * Q, C), F32)
    total[3 * C:, 0:3 * C] = jnp.zeros((total.shape[0] - 3 * C, 3 * C), F32)
    count = grads.shape[0]
    rows = 3 * C // count
    line = lax.broadcasted_iota(jnp.int32, grads.shape[1:], 0)
    extra = jnp.zeros(grads.shape[1:], F32)
    for k in range(R // 2):
        pair = jnp.concatenate([snapshot[2 * k:2 * k + 1], snapshot[2 * k + 1:2 * k + 2]], axis=1)
        extra = jnp.where(line == rows + k, pair, extra)
    for k in range(count):
        grads[k] = jnp.where(line < rows, total[k * rows:k * rows + grads.shape[1], :],
                             extra).astype(BF)


def reduce_pieces(rows, place, stride, received):
    count = received.shape[0]
    total = received[0].astype(F32)
    for k in range(1, count):
        total = total + received[k].astype(F32)
    extra = received[place].astype(F32)
    for k in range(1, count // stride):
        extra = extra + received[place + k * stride].astype(F32)
    line = lax.broadcasted_iota(jnp.int32, total.shape, 0)
    return jnp.where(line < rows, total, extra)


def near_kernel(rows, stride, places, received, out):
    total = reduce_pieces(rows, places[NEAR_AT, 0], stride, received).astype(BF)
    for k in range(out.shape[0]):
        out[k] = total


def far_kernel(rows, stride, step, places, received, out, snapshot):
    total = reduce_pieces(rows, places[FAR_AT, 0], stride, received)
    for k in range(R // 2):
        snapshot[2 * k:2 * k + 1, :] = step * total[rows + k:rows + k + 1, :W]
        snapshot[2 * k + 1:2 * k + 2, :] = step * total[rows + k:rows + k + 1, W:]
    total = total.astype(BF)
    for k in range(out.shape[0]):
        out[k] = total


def output_kernel(scale, received, field, sums, adjoint, snapshot, first, second, third, total):
    adjoint[0] = field[:, :W]
    adjoint[1] = field[:, W:]
    snapshot[...] = sums[...]
    count = received.shape[0]
    rows = 3 * C // count
    for k in range(count):
        total[k * rows:(k + 1) * rows, :] = received[k].astype(F32)[:rows] * scale
    for i in (-1, 0, 1):
        for j in (-1, 0, 1):
            tap = 3 * (i + 1) + (j + 1)
            back = 1 - i
            ahead = 1 + i
            second[tap] = total[back * C:(back + 1) * C, (j + 1) * C:(j + 2) * C]
            at = ahead * Q + j + 1
            first[tap:tap + 1, :] = total[at:at + 1, 3 * C:] + total[at + 3:at + 4, 3 * C:]
            at = 3 * Q + back * Q + j + 1
            third[tap:tap + 1, :] = total[at:at + 1, 3 * C:] + total[at + 3:at + 4, 3 * C:]


def call(kernel, outs, scratch, *operands, specs=None, cost=None, sems=0, limit=40,
         out_specs=None):
    if specs is None:
        specs = [pl.BlockSpec(memory_space=pltpu.VMEM)] * len(operands)
    return pl.pallas_call(
        kernel,
        out_shape=[jax.ShapeDtypeStruct(shape, dtype) for shape, dtype in outs],
        in_specs=specs,
        out_specs=out_specs or [pl.BlockSpec(memory_space=pltpu.VMEM)] * len(outs),
        scratch_shapes=[pltpu.VMEM(shape, dtype) for shape, dtype in scratch]
        + [pltpu.SemaphoreType.DMA((sems,))] * (sems > 0),
        compiler_params=pltpu.CompilerParams(vmem_limit_bytes=limit * 2**20),
        cost_estimate=cost,
    )(*operands)


def split_parts(field):
    high = field.astype(BF)
    return high, (field - high.astype(F32)).astype(BF)


def exchange(value, axis):
    return lax.all_to_all(value, axis, 0, 0, tiled=True)


def per_device(equilibrium, measurement, coding_masks, upstream, saved_second, conv_first,
               conv_second, conv_third):
    frames = lax.axis_size(TM)
    tiles = lax.axis_size(SPACE)
    total_frames = 2 * frames
    step = 1.0 / total_frames
    scale = 1.0 / math.sqrt(total_frames * R * tiles * W)
    forward = [(i, i + 1) for i in range(tiles - 1)]
    backward = [(i + 1, i) for i in range(tiles - 1)]
    place = lax.axis_index(SPACE)
    odd = place % 2
    places = jnp.stack([place > 0, place < tiles - 1, odd, frames * (1 - odd),
                        frames * odd + lax.axis_index(TM), frames * odd,
                        lax.axis_index(NEAR[1:]), lax.axis_index(FAR[1:])]).astype(jnp.int32)

    hbm = pl.BlockSpec(memory_space=pltpu.HBM)
    whole = pl.BlockSpec(memory_space=pltpu.VMEM)
    scalars = pl.BlockSpec(memory_space=pltpu.SMEM)
    edge = ((EDGE * C + FIELDS * R, LANES), BF)
    fields = ((4 * R, LANES), F32)
    frame = ((2, R, W), F32)
    top, bottom, own_fields = call(
        pack_kernel, [edge, edge, fields],
        [frame, frame, ((2, R, W), jnp.int32), ((R, W), F32), ((2, C, R, W), BF), edge, edge],
        upstream, equilibrium, coding_masks, measurement, saved_second,
        specs=[hbm] * 5, out_specs=[hbm, hbm, whole], sems=10, limit=60)
    low = lax.ppermute(bottom, SPACE, forward)
    high = lax.ppermute(top, SPACE, backward)

    forward_w, third_w, second_w, first_w, gate2_own, hidden2, own_fields, table = call(
        stage_kernel,
        [((C, 3 * Q), BF), ((C, 3 * Q), BF), ((3 * C, 3 * C), BF), ((Q, C), BF),
         ((R * C, LANES), F32), ((R * C, LANES), BF), fields, ((8, W), jnp.int32)], [],
        places, conv_first, conv_second, conv_third, saved_second, own_fields,
        specs=[scalars] + [whole] * 5,
        cost=pl.CostEstimate(flops=2 * 10**6, bytes_accessed=10**6, transcendentals=0))

    ext = ((EXT, LANES), F32)
    part, up, masks, base = call(
        functools.partial(unpack_kernel, step),
        [((frames, 32, W), BF), ext, ext, ext], [ext, ext],
        low, own_fields, high, gate2_own)
    sums = exchange(part, TM)

    narrow = EXT - 6
    weights = (third_w, second_w, first_w)
    copies = ((2, EXT * Q, W), F32)
    d2 = (((EXT - 2) * C, LANES), BF)
    d1 = (((EXT - 4) * C, LANES), BF)
    taps = ((2, (EXT - 4) * Q, W), F32)
    slim_scratch = [((2, narrow * Q, W), F32), (((narrow - 2) * C, LANES), BF),
                    (((narrow - 4) * C, LANES), BF), ((2, (narrow - 4) * Q, W), F32)]
    wide_outs = [((frames, 16, W), BF), ((narrow, LANES), F32)]
    part, moved, gate2, gate1, hidden, inputs = call(
        functools.partial(first_kernel, step),
        wide_outs + [(((EXT - 2) * C, LANES), F32), (((EXT - 4) * C, LANES), F32),
                     ((R * C, LANES), BF), (((R + 2) * Q, LANES), BF)],
        [copies, d2, d1, taps],
        table, sums, low, gate2_own, high, up, masks, base, *weights, forward_w)
    sums = exchange(part, TM)

    part, moved = call(
        functools.partial(second_kernel, step),
        [((2 * frames, 2 * R, LANES), BF), ((R, LANES), F32)], slim_scratch,
        sums, moved, up, masks, gate2, gate1, *weights)
    groups = [[t * tiles + (k + side) % tiles for side in range(2) for t in range(frames)]
              for k in range(1, tiles, 2)]
    received = lax.all_to_all(part, TM + SPACE, 0, 0, axis_index_groups=groups, tiled=True)
    field, = call(functools.partial(update_kernel, step), [((R, LANES), F32)], [],
                  table, received, moved, up, masks)
    near = lax.ppermute(field, SPACE, [(i, i ^ 1) for i in range(tiles)])
    part, moved = call(
        functools.partial(third_kernel, step), wide_outs, [copies, d2, d1, taps, ext],
        table, received, field, near, up, masks, gate2, gate1, *weights)
    sums = exchange(part, TM)

    near_sizes = [lax.axis_size(name) for name in NEAR]
    far_sizes = [lax.axis_size(name) for name in FAR]
    near_count = math.prod(near_sizes)
    far_count = math.prod(far_sizes)
    rows = 3 * C // near_count
    piece = -(-(rows + R // 2) // 16) * 16
    adjoint, grads = call(
        functools.partial(last_kernel, step),
        [((R, LANES), F32), ((near_count, piece, LANES), BF)],
        slim_scratch + [((3 * C + piece, LANES), F32)],
        sums, moved, up, masks, gate2, gate1, hidden2, hidden, inputs, *weights)

    received = exchange(grads, NEAR)
    near_stride = near_count // near_sizes[0]
    far_stride = far_count // far_sizes[0]
    received, = call(
        functools.partial(near_kernel, rows, near_stride),
        [((far_count, piece, LANES), BF)], [], table, received)
    received = exchange(received, FAR)
    received, snapshot = call(
        functools.partial(far_kernel, rows, far_stride, step),
        [((near_count, piece, LANES), BF), ((R, W), F32)], [], table, received)
    received = exchange(received, NEAR)
    return call(
        functools.partial(output_kernel, scale),
        [((2, R, W), F32), ((R, W), F32), ((9, C), F32), ((9, C, C), F32), ((9, C), F32)],
        [((3 * C, LANES), F32)], received, adjoint, snapshot)


AXES = (("zh", 4), ("core", 2), ("zl", 2), ("y", 8), ("x", 4))


def solution(mesh, axes=AXES):
    names = tuple(name for name, _ in axes)
    sizes = tuple(size for _, size in axes)
    fine = Mesh(mesh.devices.reshape(sizes), names)
    placed = (
        P(TM, SPACE, None),
        P(SPACE, None),
        P(TM, SPACE, None),
        P(TM, SPACE, None),
        P(TM, None, SPACE, None),
        P(),
        P(),
        P(),
    )
    return jax.shard_map(
        per_device,
        mesh=fine,
        in_specs=placed,
        out_specs=(P(TM, SPACE, None), P(SPACE, None), P(), P(), P()),
        check_vma=False,
    )
```

```python
import functools
import math

import jax
import jax.numpy as jnp
from jax import lax
from jax.experimental import pallas as pl
from jax.experimental.pallas import tpu as pltpu
from jax.sharding import Mesh, PartitionSpec as P

ITERS = 3
C = 64
W = 128
LANES = 2 * W
R = 8
HALO = 6
EXT = R + 2 * HALO
EDGE = HALO - 1
FIELDS = 6
Q = 16
PIECE = 32
BF = jnp.bfloat16
F32 = jnp.float32

TM = ("zh", "core")
SPACE = ("zl", "yh", "yl", "x")
BEFORE, AFTER, ODD, OWN_HALF, THEIR_ENTRY, THEIR_HALF, NEAR_AT, FAR_AT = range(8)
NEAR = ("core", "zl", "yl", "x")
FAR = ("zh", "yh")


def roll_cols(value, step):
    if step == 0:
        return value
    lane = lax.broadcasted_iota(jnp.int32, (value.shape[0], W), 1)
    edge = 0 if step > 0 else W - 1
    halves = []
    for frame in range(2):
        half = value[:, frame * W:(frame + 1) * W]
        half = pltpu.roll(half, step % W, 1)
        halves.append(jnp.where(lane == edge, 0.0, half))
    return jnp.concatenate(halves, axis=1)


def slope_parts(value):
    logistic = 0.5 * jnp.tanh(0.5 * value) + 0.5
    return logistic, logistic * (1.0 + value * (1.0 - logistic))


def put_slot(ref, at, count, value):
    for frame in range(2):
        ref[frame, pl.ds(at, count, stride=Q), :] = value[:, frame * W:(frame + 1) * W]


def take_slot(ref, at, count):
    return jnp.concatenate(
        [ref[frame, pl.ds(at, count, stride=Q), :] for frame in range(2)], axis=1)


def put_rows(ref, at, value):
    for frame in range(2):
        ref[frame, at:at + value.shape[0], :] = value[:, frame * W:(frame + 1) * W]


def take_rows(ref, first, last):
    return jnp.concatenate([ref[frame, first:last, :] for frame in range(2)], axis=1)


def fill_shifted(field, copies, sign):
    count = field.shape[0]
    for slot, step in enumerate((-1, 0, 1)):
        shifted = roll_cols(field, sign * step)
        high = shifted.astype(BF).astype(F32)
        put_slot(copies, slot, count, high)
        put_slot(copies, 3 + slot, count, shifted - high)


def dot(left, right):
    return jnp.dot(left, right, preferred_element_type=F32)


def dot_nt(left, right):
    return lax.dot_general(left, right, (((1,), (1,)), ((), ())), preferred_element_type=F32)


def back_rows(first, field, gate2, third_w, second_w, copies, d2):
    rows = EXT - 2 * first
    fill_shifted(field, copies, 1)
    for k in range(rows - 2):
        third = dot(third_w, take_rows(copies, k * Q, (k + 3) * Q).astype(BF))
        at = first + k
        d2[k * C:(k + 1) * C, :] = (gate2[at * C:(at + 1) * C, :] * third).astype(BF)
    for k in range(rows - 4):
        parts = dot(second_w, d2[k * C:(k + 3) * C, :])
        total = (
            roll_cols(parts[:C], -1) + parts[C:2 * C] + roll_cols(parts[2 * C:], 1)
        )
        yield k, total


def adjoint_map(first, field, gate2, gate1, third_w, second_w, first_w, copies, d2, d1, taps):
    for k, total in back_rows(first, field, gate2, third_w, second_w, copies, d2):
        at = first + k
        row = (gate1[at * C:(at + 1) * C, :] * total).astype(BF)
        d1[k * C:(k + 1) * C, :] = row
    return map_end(first, field, first_w, d1, taps)


def map_end(first, field, first_w, d1, taps):
    count = EXT - 2 * first - 6
    for k in range(count + 2):
        put_rows(taps, k * Q, dot(first_w, d1[k * C:(k + 1) * C, :]))
    result = field[3:3 + count]
    for j in (-1, 0, 1):
        column = None
        for i in (-1, 0, 1):
            tap = 3 * (i + 1) + (j + 1)
            part = take_slot(taps, (1 - i) * Q + tap, count)
            column = part if column is None else column + part
        result = result + roll_cols(column, j)
    return result


def masked_sum(masks, field):
    product = masks * field
    return product[:, :W] + product[:, W:]


def twice(field):
    return jnp.concatenate([field, field], axis=1)


def gathered_sum(ref):
    total = ref[0].astype(F32)
    for k in range(1, ref.shape[0]):
        total = total + ref[k].astype(F32)
    return total


def send_all(part, value):
    fill = jnp.zeros((part.shape[1] - value.shape[0], value.shape[1]), F32)
    value = jnp.concatenate([value, fill], axis=0).astype(part.dtype)
    for k in range(part.shape[0]):
        part[k] = value


def pack_kernel(upstream, equilibrium, masks, measurement, saved, top, bottom, own_fields,
                up_in, fixed_in, masks_in, snapshot_in, saved_in, sems):
    copies = [
        pltpu.make_async_copy(source, target, sems.at[k])
        for k, (source, target) in enumerate((
            (saved, saved_in), (upstream, up_in), (equilibrium, fixed_in), (masks, masks_in),
            (measurement, snapshot_in)))
    ]
    for copy in copies:
        copy.start()
    for copy in copies[1:]:
        copy.wait()

    def by_frame(ref):
        return jnp.concatenate([ref[0], ref[1]], axis=1)

    up = by_frame(up_in)
    fixed = by_frame(fixed_in)
    mask = by_frame(masks_in).astype(F32)
    snapshot = snapshot_in[...]
    for k, field in enumerate((up, mask, fixed, twice(snapshot))):
        own_fields[k * R:(k + 1) * R, :] = field
    fields = (*split_parts(up), *split_parts(fixed), mask.astype(BF),
              jnp.concatenate(split_parts(snapshot), axis=1))
    for k in range(0, len(fields), 2):
        pair = jnp.concatenate([field.astype(F32) for field in fields[k:k + 2]], axis=0).astype(BF)
        at = EDGE * C + k * R
        top[at:at + 2 * R, :] = pair
        bottom[at:at + 2 * R, :] = pair
    copies[0].wait()
    for frame in range(2):
        lanes = slice(frame * W, (frame + 1) * W)
        rows = jnp.swapaxes(saved_in[frame].astype(F32), 0, 1).astype(BF).reshape(R * C, W)
        top[:EDGE * C, lanes] = rows[:EDGE * C]
        bottom[:EDGE * C, lanes] = rows[(R - EDGE) * C:]


def stage_kernel(places, first, second, third, saved, own_fields, forward_w, third_w, second_w,
                 first_w, gate2, hidden2, fields, table):
    fields[...] = own_fields[...]
    for k in range(8):
        table[k:k + 1, :] = jnp.full((1, W), places[k], jnp.int32)
    for frame in range(2):
        lanes = slice(frame * W, (frame + 1) * W)
        value = jnp.swapaxes(saved[frame].astype(F32), 0, 1).reshape(R * C, W)
        logistic, slope = slope_parts(value)
        gate2[:, lanes] = slope
        hidden2[:, lanes] = (value * logistic).astype(BF)
    forward = first[...].astype(F32)
    backward = third[...].astype(F32)
    pad = jnp.zeros((Q - 6, C), F32)
    ahead = []
    back = []
    for i in range(3):
        row = forward[3 * i:3 * i + 3]
        ahead += [row, row, pad]
        row = backward[6 - 3 * i:9 - 3 * i]
        back += [row, row, pad]
        for j in range(3):
            tile = second[3 * (2 - i) + j].astype(F32)
            second_w[j * C:(j + 1) * C, i * C:(i + 1) * C] = jnp.transpose(tile).astype(BF)
    forward_w[...] = jnp.transpose(jnp.concatenate(ahead, axis=0)).astype(BF)
    third_w[...] = jnp.transpose(jnp.concatenate(back, axis=0)).astype(BF)
    first_w[...] = jnp.concatenate([forward, jnp.zeros((Q - 9, C), F32)], axis=0).astype(BF)


def unpack_kernel(step, low, own_fields, high, _, part, up, masks, base, fixed, snapshot):
    for k, target in enumerate((up, masks, fixed, snapshot)):
        target[HALO:HALO + R, :] = own_fields[k * R:(k + 1) * R, :]
    for ref, at, first in ((low, 0, R - HALO), (high, HALO + R, 0)):
        fields = ref[EDGE * C:EDGE * C + FIELDS * R, :].astype(F32)

        def field(k):
            return fields[k * R:(k + 1) * R]

        for target, value in ((up, field(0) + field(1)), (fixed, field(2) + field(3)),
                              (masks, field(4)),
                              (snapshot, twice(field(5)[:, :W] + field(5)[:, W:]))):
            target[at:at + HALO, :] = value[first:first + HALO]
    send_all(part, masked_sum(masks[...], fixed[...]))
    base[...] = fixed[...] + step * masks[...] * snapshot[...]


def saved_row(ref, at):
    return ref[at * C:(at + 1) * C, :]


def keep_row(value, at, before, after):
    if at < HALO:
        return value * before
    if at >= HALO + R:
        return value * after
    return value


def ends(places):
    return tuple(twice(places[k:k + 1, :]).astype(F32) for k in (BEFORE, AFTER))


def first_kernel(step, places, sums, low, own, high, up, masks, base, third_w, second_w, first_w,
                 forward_w, part, moved, gate2, gate1, hidden, inputs, copies, d2, d1, taps):
    before, after = ends(places)
    for k in range(EXT - 2):
        at = k + 1
        if HALO <= at < HALO + R:
            gate2[k * C:(k + 1) * C, :] = saved_row(own, at - HALO)
        else:
            value = saved_row(low, k) if at < HALO else saved_row(high, at - HALO - R)
            slope = slope_parts(value.astype(F32))[1]
            gate2[k * C:(k + 1) * C, :] = keep_row(slope, at, before, after)
    frame_sum = gathered_sum(sums)[:EXT]
    denoiser_input = base[...] - step * masks[...] * twice(frame_sum)
    copies[...] = jnp.zeros_like(copies)
    fill_shifted(denoiser_input, copies, -1)
    inputs[...] = take_rows(copies, (HALO - 1) * Q, (HALO + R + 1) * Q).astype(BF)
    for k in range(EXT - 4):
        at = k + 2
        value = dot(forward_w[...], take_rows(copies, (at - 1) * Q, (at + 2) * Q).astype(BF))
        logistic, slope = slope_parts(value)
        gate1[k * C:(k + 1) * C, :] = keep_row(slope, at, before, after)
        if HALO <= at < HALO + R:
            own_at = at - HALO
            hidden[own_at * C:(own_at + 1) * C, :] = (value * logistic).astype(BF)
    field = adjoint_map(0, up[...], gate2, gate1, third_w[...], second_w[...], first_w[...],
                        copies, d2, d1, taps)
    finish_wide(field, before, after, masks, part, moved)


def finish_wide(field, before, after, masks, part, moved):
    count = EXT - 6
    row = lax.broadcasted_iota(jnp.int32, field.shape, 0)
    keep = jnp.where(row < HALO - 3, before, jnp.where(row >= HALO - 3 + R, after, 1.0))
    field = field * keep
    moved[...] = field
    send_all(part, masked_sum(masks[3:3 + count, :], field))


def narrow_field(step, sums, moved, up, masks):
    count = EXT - 6
    totals = gathered_sum(sums)[:count]
    return up[3:3 + count, :] + moved[...] - step * masks[3:3 + count, :] * twice(totals)


def second_kernel(step, sums, moved, up, masks, gate2, gate1, third_w, second_w, first_w,
                  part, out, copies, d2, d1, taps):
    copies[...] = jnp.zeros_like(copies)
    field = narrow_field(step, sums, moved, up, masks)
    result = adjoint_map(3, field, gate2, gate1, third_w[...], second_w[...], first_w[...],
                         copies, d2, d1, taps)
    out[...] = result
    total = masked_sum(masks[HALO:HALO + R, :], result)
    half = jnp.concatenate([total[:R // 2], total[R // 2:]], axis=1)
    send_all(part, jnp.concatenate([result, half], axis=0))


def pair_total(received, first):
    count = received.shape[0] // 2
    half = received[first].astype(F32)
    for k in range(1, count):
        half = half + received[first + k].astype(F32)
    half = half[R:R + R // 2]
    return jnp.concatenate([half[:, :W], half[:, W:]], axis=0)


def update_kernel(step, places, received, moved, up, masks, out):
    totals = pair_total(received, places[OWN_HALF, 0])
    out[...] = (up[HALO:HALO + R, :] + moved[...]
                - step * masks[HALO:HALO + R, :] * twice(totals))


def third_kernel(step, places, received, own, near, up, masks, gate2, gate1, third_w,
                 second_w, first_w, part, moved, copies, d2, d1, taps, whole):
    copies[...] = jnp.zeros_like(copies)
    before, after = ends(places)
    totals = twice(pair_total(received, places[THEIR_HALF, 0]))
    theirs = received[places[THEIR_ENTRY, 0]].astype(F32)[:R]
    after_rows = slice(HALO + R, EXT)
    low = (up[0:HALO, :] + theirs[R - HALO:]
           - step * masks[0:HALO, :] * totals[R - HALO:]) * before
    high = (up[after_rows, :] + theirs[:HALO]
            - step * masks[after_rows, :] * totals[:HALO]) * after
    odd = twice(places[ODD:ODD + 1, :]) == 1
    whole[0:HALO, :] = jnp.where(odd, near[R - HALO:, :], low)
    whole[HALO:HALO + R, :] = own[...]
    whole[HALO + R:, :] = jnp.where(odd, high, near[:HALO, :])
    field = adjoint_map(0, whole[...], gate2, gate1, third_w[...], second_w[...], first_w[...],
                        copies, d2, d1, taps)
    finish_wide(field, before, after, masks, part, moved)


def last_kernel(step, cores, sums, moved, up, masks, gate2, gate1, hidden2, hidden, inputs, third_w,
                second_w, first_w, adjoint, grads, copies, d2, d1, taps, total):
    copies[...] = jnp.zeros_like(copies)
    field = narrow_field(step, sums, moved, up, masks)
    adjoint[...] = field[3:3 + R]
    result = adjoint_map(3, field, gate2, gate1, third_w[...], second_w[...], first_w[...],
                         copies, d2, d1, taps)
    snapshot = masked_sum(masks[HALO:HALO + R, :], result)
    left = []
    right = []
    left_first = []
    right_first = []
    left_third = []
    right_third = []
    for r in range(R):
        left.append(d2[(r + 1) * C:(r + 4) * C, :])
        value = hidden[r * C:(r + 1) * C, :].astype(F32)
        right.append(jnp.concatenate(
            [roll_cols(value, 1), value, roll_cols(value, -1)], axis=0).astype(BF))
        left_first.append(inputs[r * Q:(r + 3) * Q, :])
        right_first.append(d1[(r + 1) * C:(r + 2) * C, :])
        left_third.append(take_rows(copies, (r + 2) * Q, (r + 5) * Q).astype(BF))
        right_third.append(saved_row(hidden2, r))
    def join(parts):
        return jnp.concatenate(parts, axis=1)
    second = dot_nt(join(left), join(right))
    first = dot_nt(join(left_first), join(right_first))
    third = dot_nt(join(left_third), join(right_third))
    total[0:3 * C, 0:3 * C] = second
    total[0:3 * Q, 3 * C:] = first
    total[3 * Q:6 * Q, 3 * C:] = third
    total[6 * Q:, 3 * C:] = jnp.zeros((total.shape[0] - 6 * Q, C), F32)
    total[3 * C:, 0:3 * C] = jnp.zeros((total.shape[0] - 3 * C, 3 * C), F32)
    count = grads.shape[0]
    rows = 3 * C // count
    line = lax.broadcasted_iota(jnp.int32, grads.shape[1:], 0)
    extras = []
    for core in range(cores):
        extra = jnp.zeros(grads.shape[1:], F32)
        for k in range(R // 2 // cores):
            at = 2 * (core * (R // 2 // cores) + k)
            pair = jnp.concatenate([snapshot[at:at + 1], snapshot[at + 1:at + 2]], axis=1)
            extra = jnp.where(line == rows + k, pair, extra)
        extras.append(extra)
    for k in range(count):
        grads[k] = jnp.where(line < rows, total[k * rows:k * rows + grads.shape[1], :],
                             extras[k * cores // count]).astype(BF)


def reduce_pieces(rows, place, stride, received):
    count = received.shape[0]
    total = received[0].astype(F32)
    for k in range(1, count):
        total = total + received[k].astype(F32)
    extra = received[place].astype(F32)
    for k in range(1, count // stride):
        extra = extra + received[place + k * stride].astype(F32)
    line = lax.broadcasted_iota(jnp.int32, total.shape, 0)
    return jnp.where(line < rows, total, extra)


def sum_kernel(rows, stride, at, places, received, out):
    total = reduce_pieces(rows, places[at, 0], stride, received).astype(BF)
    for k in range(out.shape[0]):
        out[k] = total


def output_kernel(step, scale, cores, places, received, field, adjoint, snapshot, first, second,
                  third, total):
    adjoint[0] = field[:, :W]
    adjoint[1] = field[:, W:]
    count = received.shape[0]
    rows = 3 * C // count
    for core in range(cores):
        piece = received[places[NEAR_AT, 0] + core * (count // cores)].astype(F32) * step
        for k in range(R // 2 // cores):
            at = 2 * (core * (R // 2 // cores) + k)
            snapshot[at:at + 1, :] = piece[rows + k:rows + k + 1, :W]
            snapshot[at + 1:at + 2, :] = piece[rows + k:rows + k + 1, W:]
    for k in range(count):
        total[k * rows:(k + 1) * rows, :] = received[k].astype(F32)[:rows] * scale
    for i in (-1, 0, 1):
        for j in (-1, 0, 1):
            tap = 3 * (i + 1) + (j + 1)
            back = 1 - i
            ahead = 1 + i
            second[tap] = total[back * C:(back + 1) * C, (j + 1) * C:(j + 2) * C]
            at = ahead * Q + j + 1
            first[tap:tap + 1, :] = total[at:at + 1, 3 * C:] + total[at + 3:at + 4, 3 * C:]
            at = 3 * Q + back * Q + j + 1
            third[tap:tap + 1, :] = total[at:at + 1, 3 * C:] + total[at + 3:at + 4, 3 * C:]


def call(kernel, outs, scratch, *operands, specs=None, cost=None, sems=0, limit=40):
    if specs is None:
        specs = [pl.BlockSpec(memory_space=pltpu.VMEM)] * len(operands)
    return pl.pallas_call(
        kernel,
        out_shape=[jax.ShapeDtypeStruct(shape, dtype) for shape, dtype in outs],
        in_specs=specs,
        out_specs=[pl.BlockSpec(memory_space=pltpu.VMEM)] * len(outs),
        scratch_shapes=[pltpu.VMEM(shape, dtype) for shape, dtype in scratch]
        + [pltpu.SemaphoreType.DMA((sems,))] * (sems > 0),
        compiler_params=pltpu.CompilerParams(vmem_limit_bytes=limit * 2**20),
        cost_estimate=cost,
    )(*operands)


def split_parts(field):
    high = field.astype(BF)
    return high, (field - high.astype(F32)).astype(BF)


def exchange(value, axis):
    return lax.all_to_all(value, axis, 0, 0, tiled=True)


def per_device(equilibrium, measurement, coding_masks, upstream, saved_second, conv_first,
               conv_second, conv_third):
    frames = lax.axis_size(TM)
    tiles = lax.axis_size(SPACE)
    total_frames = 2 * frames
    step = 1.0 / total_frames
    scale = 1.0 / math.sqrt(total_frames * R * tiles * W)
    forward = [(i, i + 1) for i in range(tiles - 1)]
    backward = [(i + 1, i) for i in range(tiles - 1)]
    place = lax.axis_index(SPACE)
    odd = place % 2
    places = jnp.stack([place > 0, place < tiles - 1, odd, frames * (1 - odd),
                        frames * odd + lax.axis_index(TM), frames * odd,
                        lax.axis_index(NEAR[1:]), lax.axis_index(FAR[1:])]).astype(jnp.int32)

    hbm = pl.BlockSpec(memory_space=pltpu.HBM)
    whole = pl.BlockSpec(memory_space=pltpu.VMEM)
    scalars = pl.BlockSpec(memory_space=pltpu.SMEM)
    edge = ((EDGE * C + FIELDS * R, LANES), BF)
    fields = ((4 * R, LANES), F32)
    frame = ((2, R, W), F32)
    top, bottom, own_fields = call(
        pack_kernel, [edge, edge, fields],
        [frame, frame, ((2, R, W), jnp.int32), ((R, W), F32), ((2, C, R, W), BF)],
        upstream, equilibrium, coding_masks, measurement, saved_second,
        specs=[hbm] * 5, sems=5, limit=60)
    low = lax.ppermute(bottom, SPACE, forward)
    high = lax.ppermute(top, SPACE, backward)

    forward_w, third_w, second_w, first_w, gate2_own, hidden2, own_fields, table = call(
        stage_kernel,
        [((C, 3 * Q), BF), ((C, 3 * Q), BF), ((3 * C, 3 * C), BF), ((Q, C), BF),
         ((R * C, LANES), F32), ((R * C, LANES), BF), fields, ((8, W), jnp.int32)], [],
        places, conv_first, conv_second, conv_third, saved_second, own_fields,
        specs=[scalars] + [whole] * 5,
        cost=pl.CostEstimate(flops=2 * 10**6, bytes_accessed=10**6, transcendentals=0))

    ext = ((EXT, LANES), F32)
    part, up, masks, base = call(
        functools.partial(unpack_kernel, step),
        [((frames, 32, W), BF), ext, ext, ext], [ext, ext],
        low, own_fields, high, gate2_own)
    sums = exchange(part, TM)

    narrow = EXT - 6
    weights = (third_w, second_w, first_w)
    copies = ((2, EXT * Q, W), F32)
    d2 = (((EXT - 2) * C, LANES), BF)
    d1 = (((EXT - 4) * C, LANES), BF)
    taps = ((2, (EXT - 4) * Q, W), F32)
    slim_scratch = [((2, narrow * Q, W), F32), (((narrow - 2) * C, LANES), BF),
                    (((narrow - 4) * C, LANES), BF), ((2, (narrow - 4) * Q, W), F32)]
    wide_outs = [((frames, 16, W), BF), ((narrow, LANES), F32)]
    part, moved, gate2, gate1, hidden, inputs = call(
        functools.partial(first_kernel, step),
        wide_outs + [(((EXT - 2) * C, LANES), F32), (((EXT - 4) * C, LANES), F32),
                     ((R * C, LANES), BF), (((R + 2) * Q, LANES), BF)],
        [copies, d2, d1, taps],
        table, sums, low, gate2_own, high, up, masks, base, *weights, forward_w)
    sums = exchange(part, TM)

    part, moved = call(
        functools.partial(second_kernel, step),
        [((2 * frames, 2 * R, LANES), BF), ((R, LANES), F32)], slim_scratch,
        sums, moved, up, masks, gate2, gate1, *weights)
    groups = [[t * tiles + (k + side) % tiles for side in range(2) for t in range(frames)]
              for k in range(1, tiles, 2)]
    received = lax.all_to_all(part, TM + SPACE, 0, 0, axis_index_groups=groups, tiled=True)
    field, = call(functools.partial(update_kernel, step), [((R, LANES), F32)], [],
                  table, received, moved, up, masks)
    near = lax.ppermute(field, SPACE, [(i, i ^ 1) for i in range(tiles)])
    part, moved = call(
        functools.partial(third_kernel, step), wide_outs, [copies, d2, d1, taps, ext],
        table, received, field, near, up, masks, gate2, gate1, *weights)
    sums = exchange(part, TM)

    near_sizes = [lax.axis_size(name) for name in NEAR]
    far_sizes = [lax.axis_size(name) for name in FAR]
    near_count = math.prod(near_sizes)
    far_count = math.prod(far_sizes)
    rows = 3 * C // near_count
    piece = -(-(rows + R // 2 // near_sizes[0]) // 8) * 8
    adjoint, grads = call(
        functools.partial(last_kernel, step, near_sizes[0]),
        [((R, LANES), F32), ((near_count, piece, LANES), BF)],
        slim_scratch + [((3 * C + piece, LANES), F32)],
        sums, moved, up, masks, gate2, gate1, hidden2, hidden, inputs, *weights)

    received = exchange(grads, NEAR)
    near_stride = near_count // near_sizes[0]
    far_stride = far_count // far_sizes[0]
    received, = call(
        functools.partial(sum_kernel, rows, near_stride, NEAR_AT),
        [((far_count, piece, LANES), BF)], [], table, received)
    received = exchange(received, FAR)
    received, = call(
        functools.partial(sum_kernel, rows, far_stride, FAR_AT),
        [((near_count, piece, LANES), BF)], [], table, received)
    received = exchange(received, NEAR)
    return call(
        functools.partial(output_kernel, step, scale, near_sizes[0]),
        [((2, R, W), F32), ((R, W), F32), ((9, C), F32), ((9, C, C), F32), ((9, C), F32)],
        [((3 * C, LANES), F32)], table, received, adjoint)


AXES = (("zh", 4), ("core", 2), ("zl", 2), ("yh", 4), ("yl", 2), ("x", 4))


def solution(mesh, axes=AXES):
    names = tuple(name for name, _ in axes)
    sizes = tuple(size for _, size in axes)
    fine = Mesh(mesh.devices.reshape(sizes), names)
    placed = (
        P(TM, SPACE, None),
        P(SPACE, None),
        P(TM, SPACE, None),
        P(TM, SPACE, None),
        P(TM, None, SPACE, None),
        P(),
        P(),
        P(),
    )
    return jax.shard_map(
        per_device,
        mesh=fine,
        in_specs=placed,
        out_specs=(P(TM, SPACE, None), P(SPACE, None), P(), P(), P()),
        check_vma=False,
    )
```

```python
import functools
import math

import jax
import jax.numpy as jnp
from jax import lax
from jax.experimental import pallas as pl
from jax.experimental.pallas import tpu as pltpu
from jax.sharding import Mesh, PartitionSpec as P

ITERS = 3
C = 64
W = 128
LANES = 2 * W
R = 8
HALO = 6
EXT = R + 2 * HALO
EDGE = HALO - 1
FIELDS = 6
Q = 16
PIECE = 32
BF = jnp.bfloat16
F32 = jnp.float32

TM = ("zh", "core")
SPACE = ("zl", "yh", "yl", "xh", "xl")
BEFORE, AFTER, ODD, OWN_HALF, THEIR_ENTRY, THEIR_HALF, NEAR_AT, FAR_AT = range(8)
NEAR = ("core", "zl", "yl", "xh", "xl")
FAR = ("zh", "yh")


def roll_cols(value, step):
    if step == 0:
        return value
    lane = lax.broadcasted_iota(jnp.int32, (value.shape[0], W), 1)
    edge = 0 if step > 0 else W - 1
    halves = []
    for frame in range(2):
        half = value[:, frame * W:(frame + 1) * W]
        half = pltpu.roll(half, step % W, 1)
        halves.append(jnp.where(lane == edge, 0.0, half))
    return jnp.concatenate(halves, axis=1)


def slope_parts(value):
    logistic = 0.5 * jnp.tanh(0.5 * value) + 0.5
    return logistic, logistic * (1.0 + value * (1.0 - logistic))


def put_slot(ref, at, count, value):
    for frame in range(2):
        ref[frame, pl.ds(at, count, stride=Q), :] = value[:, frame * W:(frame + 1) * W]


def take_slot(ref, at, count):
    return jnp.concatenate(
        [ref[frame, pl.ds(at, count, stride=Q), :] for frame in range(2)], axis=1)


def put_rows(ref, at, value):
    for frame in range(2):
        ref[frame, at:at + value.shape[0], :] = value[:, frame * W:(frame + 1) * W]


def take_rows(ref, first, last):
    return jnp.concatenate([ref[frame, first:last, :] for frame in range(2)], axis=1)


def fill_shifted(field, copies, sign):
    count = field.shape[0]
    for slot, step in enumerate((-1, 0, 1)):
        shifted = roll_cols(field, sign * step)
        high = shifted.astype(BF).astype(F32)
        put_slot(copies, slot, count, high)
        put_slot(copies, 3 + slot, count, shifted - high)


def dot(left, right):
    return jnp.dot(left, right, preferred_element_type=F32)


def dot_nt(left, right):
    return lax.dot_general(left, right, (((1,), (1,)), ((), ())), preferred_element_type=F32)


def back_rows(first, field, gate2, third_w, second_w, copies, d2):
    rows = EXT - 2 * first
    fill_shifted(field, copies, 1)
    for k in range(rows - 2):
        third = dot(third_w, take_rows(copies, k * Q, (k + 3) * Q).astype(BF))
        at = first + k
        d2[k * C:(k + 1) * C, :] = (gate2[at * C:(at + 1) * C, :] * third).astype(BF)
    for k in range(rows - 4):
        parts = dot(second_w, d2[k * C:(k + 3) * C, :])
        total = (
            roll_cols(parts[:C], -1) + parts[C:2 * C] + roll_cols(parts[2 * C:], 1)
        )
        yield k, total


def adjoint_map(first, field, gate2, gate1, third_w, second_w, first_w, copies, d2, d1, taps):
    for k, total in back_rows(first, field, gate2, third_w, second_w, copies, d2):
        at = first + k
        row = (gate1[at * C:(at + 1) * C, :] * total).astype(BF)
        d1[k * C:(k + 1) * C, :] = row
    return map_end(first, field, first_w, d1, taps)


def map_end(first, field, first_w, d1, taps):
    count = EXT - 2 * first - 6
    for k in range(count + 2):
        put_rows(taps, k * Q, dot(first_w, d1[k * C:(k + 1) * C, :]))
    result = field[3:3 + count]
    for j in (-1, 0, 1):
        column = None
        for i in (-1, 0, 1):
            tap = 3 * (i + 1) + (j + 1)
            part = take_slot(taps, (1 - i) * Q + tap, count)
            column = part if column is None else column + part
        result = result + roll_cols(column, j)
    return result


def masked_sum(masks, field):
    product = masks * field
    return product[:, :W] + product[:, W:]


def twice(field):
    return jnp.concatenate([field, field], axis=1)


def gathered_sum(ref):
    total = ref[0].astype(F32)
    for k in range(1, ref.shape[0]):
        total = total + ref[k].astype(F32)
    return total


def send_all(part, value):
    fill = jnp.zeros((part.shape[1] - value.shape[0], value.shape[1]), F32)
    value = jnp.concatenate([value, fill], axis=0).astype(part.dtype)
    for k in range(part.shape[0]):
        part[k] = value


def pack_kernel(upstream, equilibrium, masks, measurement, saved, top, bottom, own_fields,
                up_in, fixed_in, masks_in, snapshot_in, saved_in, sems):
    copies = [
        pltpu.make_async_copy(source, target, sems.at[k])
        for k, (source, target) in enumerate((
            (saved, saved_in), (upstream, up_in), (equilibrium, fixed_in), (masks, masks_in),
            (measurement, snapshot_in)))
    ]
    for copy in copies:
        copy.start()
    for copy in copies[1:]:
        copy.wait()

    def by_frame(ref):
        return jnp.concatenate([ref[0], ref[1]], axis=1)

    up = by_frame(up_in)
    fixed = by_frame(fixed_in)
    mask = by_frame(masks_in).astype(F32)
    snapshot = snapshot_in[...]
    for k, field in enumerate((up, mask, fixed, twice(snapshot))):
        own_fields[k * R:(k + 1) * R, :] = field
    fields = (*split_parts(up), *split_parts(fixed), mask.astype(BF),
              jnp.concatenate(split_parts(snapshot), axis=1))
    for k in range(0, len(fields), 2):
        pair = jnp.concatenate([field.astype(F32) for field in fields[k:k + 2]], axis=0).astype(BF)
        at = EDGE * C + k * R
        top[at:at + 2 * R, :] = pair
        bottom[at:at + 2 * R, :] = pair
    copies[0].wait()
    for frame in range(2):
        lanes = slice(frame * W, (frame + 1) * W)
        rows = jnp.swapaxes(saved_in[frame].astype(F32), 0, 1).astype(BF).reshape(R * C, W)
        top[:EDGE * C, lanes] = rows[:EDGE * C]
        bottom[:EDGE * C, lanes] = rows[(R - EDGE) * C:]


def stage_kernel(places, first, second, third, saved, own_fields, forward_w, third_w, second_w,
                 first_w, gate2, hidden2, fields, table):
    fields[...] = own_fields[...]
    for k in range(8):
        table[k:k + 1, :] = jnp.full((1, W), places[k], jnp.int32)
    for frame in range(2):
        lanes = slice(frame * W, (frame + 1) * W)
        value = jnp.swapaxes(saved[frame].astype(F32), 0, 1).reshape(R * C, W)
        logistic, slope = slope_parts(value)
        gate2[:, lanes] = slope
        hidden2[:, lanes] = (value * logistic).astype(BF)
    forward = first[...].astype(F32)
    backward = third[...].astype(F32)
    pad = jnp.zeros((Q - 6, C), F32)
    ahead = []
    back = []
    for i in range(3):
        row = forward[3 * i:3 * i + 3]
        ahead += [row, row, pad]
        row = backward[6 - 3 * i:9 - 3 * i]
        back += [row, row, pad]
        for j in range(3):
            tile = second[3 * (2 - i) + j].astype(F32)
            second_w[j * C:(j + 1) * C, i * C:(i + 1) * C] = jnp.transpose(tile).astype(BF)
    forward_w[...] = jnp.transpose(jnp.concatenate(ahead, axis=0)).astype(BF)
    third_w[...] = jnp.transpose(jnp.concatenate(back, axis=0)).astype(BF)
    first_w[...] = jnp.concatenate([forward, jnp.zeros((Q - 9, C), F32)], axis=0).astype(BF)


def unpack_kernel(step, low, own_fields, high, _, part, up, masks, base, fixed, snapshot):
    for k, target in enumerate((up, masks, fixed, snapshot)):
        target[HALO:HALO + R, :] = own_fields[k * R:(k + 1) * R, :]
    for ref, at, first in ((low, 0, R - HALO), (high, HALO + R, 0)):
        fields = ref[EDGE * C:EDGE * C + FIELDS * R, :].astype(F32)

        def field(k):
            return fields[k * R:(k + 1) * R]

        for target, value in ((up, field(0) + field(1)), (fixed, field(2) + field(3)),
                              (masks, field(4)),
                              (snapshot, twice(field(5)[:, :W] + field(5)[:, W:]))):
            target[at:at + HALO, :] = value[first:first + HALO]
    send_all(part, masked_sum(masks[...], fixed[...]))
    base[...] = fixed[...] + step * masks[...] * snapshot[...]


def saved_row(ref, at):
    return ref[at * C:(at + 1) * C, :]


def keep_row(value, at, before, after):
    if at < HALO:
        return value * before
    if at >= HALO + R:
        return value * after
    return value


def ends(places):
    return tuple(twice(places[k:k + 1, :]).astype(F32) for k in (BEFORE, AFTER))


def first_kernel(step, places, sums, low, own, high, up, masks, base, third_w, second_w, first_w,
                 forward_w, part, moved, gate2, gate1, hidden, inputs, copies, d2, d1, taps):
    before, after = ends(places)
    for k in range(EXT - 2):
        at = k + 1
        if HALO <= at < HALO + R:
            gate2[k * C:(k + 1) * C, :] = saved_row(own, at - HALO)
        else:
            value = saved_row(low, k) if at < HALO else saved_row(high, at - HALO - R)
            slope = slope_parts(value.astype(F32))[1]
            gate2[k * C:(k + 1) * C, :] = keep_row(slope, at, before, after)
    frame_sum = gathered_sum(sums)[:EXT]
    denoiser_input = base[...] - step * masks[...] * twice(frame_sum)
    copies[...] = jnp.zeros_like(copies)
    fill_shifted(denoiser_input, copies, -1)
    inputs[...] = take_rows(copies, (HALO - 1) * Q, (HALO + R + 1) * Q).astype(BF)
    for k in range(EXT - 4):
        at = k + 2
        value = dot(forward_w[...], take_rows(copies, (at - 1) * Q, (at + 2) * Q).astype(BF))
        logistic, slope = slope_parts(value)
        gate1[k * C:(k + 1) * C, :] = keep_row(slope, at, before, after)
        if HALO <= at < HALO + R:
            own_at = at - HALO
            hidden[own_at * C:(own_at + 1) * C, :] = (value * logistic).astype(BF)
    field = adjoint_map(0, up[...], gate2, gate1, third_w[...], second_w[...], first_w[...],
                        copies, d2, d1, taps)
    finish_wide(field, before, after, masks, part, moved)


def finish_wide(field, before, after, masks, part, moved):
    count = EXT - 6
    row = lax.broadcasted_iota(jnp.int32, field.shape, 0)
    keep = jnp.where(row < HALO - 3, before, jnp.where(row >= HALO - 3 + R, after, 1.0))
    field = field * keep
    moved[...] = field
    send_all(part, masked_sum(masks[3:3 + count, :], field))


def narrow_field(step, sums, moved, up, masks):
    count = EXT - 6
    totals = gathered_sum(sums)[:count]
    return up[3:3 + count, :] + moved[...] - step * masks[3:3 + count, :] * twice(totals)


def second_kernel(step, sums, moved, up, masks, gate2, gate1, third_w, second_w, first_w,
                  part, out, copies, d2, d1, taps):
    copies[...] = jnp.zeros_like(copies)
    field = narrow_field(step, sums, moved, up, masks)
    result = adjoint_map(3, field, gate2, gate1, third_w[...], second_w[...], first_w[...],
                         copies, d2, d1, taps)
    out[...] = result
    total = masked_sum(masks[HALO:HALO + R, :], result)
    half = jnp.concatenate([total[:R // 2], total[R // 2:]], axis=1)
    send_all(part, jnp.concatenate([result, half], axis=0))


def pair_total(received, first):
    count = received.shape[0] // 2
    half = received[first].astype(F32)
    for k in range(1, count):
        half = half + received[first + k].astype(F32)
    half = half[R:R + R // 2]
    return jnp.concatenate([half[:, :W], half[:, W:]], axis=0)


def update_kernel(step, places, received, moved, up, masks, out):
    totals = pair_total(received, places[OWN_HALF, 0])
    out[...] = (up[HALO:HALO + R, :] + moved[...]
                - step * masks[HALO:HALO + R, :] * twice(totals))


def third_kernel(step, places, received, own, near, up, masks, gate2, gate1, third_w,
                 second_w, first_w, part, moved, copies, d2, d1, taps, whole):
    copies[...] = jnp.zeros_like(copies)
    before, after = ends(places)
    totals = twice(pair_total(received, places[THEIR_HALF, 0]))
    theirs = received[places[THEIR_ENTRY, 0]].astype(F32)[:R]
    after_rows = slice(HALO + R, EXT)
    low = (up[0:HALO, :] + theirs[R - HALO:]
           - step * masks[0:HALO, :] * totals[R - HALO:]) * before
    high = (up[after_rows, :] + theirs[:HALO]
            - step * masks[after_rows, :] * totals[:HALO]) * after
    odd = twice(places[ODD:ODD + 1, :]) == 1
    whole[0:HALO, :] = jnp.where(odd, near[0, R - HALO:, :], low)
    whole[HALO:HALO + R, :] = own[...]
    whole[HALO + R:, :] = jnp.where(odd, high, near[1, :HALO, :])
    field = adjoint_map(0, whole[...], gate2, gate1, third_w[...], second_w[...], first_w[...],
                        copies, d2, d1, taps)
    finish_wide(field, before, after, masks, part, moved)


def last_kernel(step, cores, sums, moved, up, masks, gate2, gate1, hidden2, hidden, inputs, third_w,
                second_w, first_w, adjoint, grads, copies, d2, d1, taps, total):
    copies[...] = jnp.zeros_like(copies)
    field = narrow_field(step, sums, moved, up, masks)
    adjoint[...] = field[3:3 + R]
    result = adjoint_map(3, field, gate2, gate1, third_w[...], second_w[...], first_w[...],
                         copies, d2, d1, taps)
    snapshot = masked_sum(masks[HALO:HALO + R, :], result)
    left = []
    right = []
    left_first = []
    right_first = []
    left_third = []
    right_third = []
    for r in range(R):
        left.append(d2[(r + 1) * C:(r + 4) * C, :])
        value = hidden[r * C:(r + 1) * C, :].astype(F32)
        right.append(jnp.concatenate(
            [roll_cols(value, 1), value, roll_cols(value, -1)], axis=0).astype(BF))
        left_first.append(inputs[r * Q:(r + 3) * Q, :])
        right_first.append(d1[(r + 1) * C:(r + 2) * C, :])
        left_third.append(take_rows(copies, (r + 2) * Q, (r + 5) * Q).astype(BF))
        right_third.append(saved_row(hidden2, r))
    def join(parts):
        return jnp.concatenate(parts, axis=1)
    second = dot_nt(join(left), join(right))
    first = dot_nt(join(left_first), join(right_first))
    third = dot_nt(join(left_third), join(right_third))
    total[0:3 * C, 0:3 * C] = second
    total[0:3 * Q, 3 * C:] = first
    total[3 * Q:6 * Q, 3 * C:] = third
    total[6 * Q:, 3 * C:] = jnp.zeros((total.shape[0] - 6 * Q, C), F32)
    total[3 * C:, 0:3 * C] = jnp.zeros((total.shape[0] - 3 * C, 3 * C), F32)
    count = grads.shape[0]
    rows = 3 * C // count
    line = lax.broadcasted_iota(jnp.int32, grads.shape[1:], 0)
    extras = []
    for core in range(cores):
        extra = jnp.zeros(grads.shape[1:], F32)
        for k in range(R // 2 // cores):
            at = 2 * (core * (R // 2 // cores) + k)
            pair = jnp.concatenate([snapshot[at:at + 1], snapshot[at + 1:at + 2]], axis=1)
            extra = jnp.where(line == rows + k, pair, extra)
        extras.append(extra)
    for k in range(count):
        grads[k] = jnp.where(line < rows, total[k * rows:k * rows + grads.shape[1], :],
                             extras[k * cores // count]).astype(BF)


def reduce_pieces(rows, place, stride, received):
    count = received.shape[0]
    total = received[0].astype(F32)
    for k in range(1, count):
        total = total + received[k].astype(F32)
    extra = received[place].astype(F32)
    for k in range(1, count // stride):
        extra = extra + received[place + k * stride].astype(F32)
    line = lax.broadcasted_iota(jnp.int32, total.shape, 0)
    return jnp.where(line < rows, total, extra)


def sum_kernel(rows, stride, at, places, received, out):
    total = reduce_pieces(rows, places[at, 0], stride, received).astype(BF)
    for k in range(out.shape[0]):
        out[k] = total


def output_kernel(step, scale, cores, places, received, field, adjoint, snapshot, first, second,
                  third, total):
    adjoint[0] = field[:, :W]
    adjoint[1] = field[:, W:]
    count = received.shape[0]
    rows = 3 * C // count
    for core in range(cores):
        piece = received[places[NEAR_AT, 0] + core * (count // cores)].astype(F32) * step
        for k in range(R // 2 // cores):
            at = 2 * (core * (R // 2 // cores) + k)
            snapshot[at:at + 1, :] = piece[rows + k:rows + k + 1, :W]
            snapshot[at + 1:at + 2, :] = piece[rows + k:rows + k + 1, W:]
    for k in range(count):
        total[k * rows:(k + 1) * rows, :] = received[k].astype(F32)[:rows] * scale
    for i in (-1, 0, 1):
        for j in (-1, 0, 1):
            tap = 3 * (i + 1) + (j + 1)
            back = 1 - i
            ahead = 1 + i
            second[tap] = total[back * C:(back + 1) * C, (j + 1) * C:(j + 2) * C]
            at = ahead * Q + j + 1
            first[tap:tap + 1, :] = total[at:at + 1, 3 * C:] + total[at + 3:at + 4, 3 * C:]
            at = 3 * Q + back * Q + j + 1
            third[tap:tap + 1, :] = total[at:at + 1, 3 * C:] + total[at + 3:at + 4, 3 * C:]


def call(kernel, outs, scratch, *operands, specs=None, cost=None, sems=0, limit=40):
    if specs is None:
        specs = [pl.BlockSpec(memory_space=pltpu.VMEM)] * len(operands)
    return pl.pallas_call(
        kernel,
        out_shape=[jax.ShapeDtypeStruct(shape, dtype) for shape, dtype in outs],
        in_specs=specs,
        out_specs=[pl.BlockSpec(memory_space=pltpu.VMEM)] * len(outs),
        scratch_shapes=[pltpu.VMEM(shape, dtype) for shape, dtype in scratch]
        + [pltpu.SemaphoreType.DMA((sems,))] * (sems > 0),
        compiler_params=pltpu.CompilerParams(vmem_limit_bytes=limit * 2**20),
        cost_estimate=cost,
    )(*operands)


def split_parts(field):
    high = field.astype(BF)
    return high, (field - high.astype(F32)).astype(BF)


def exchange(value, axis):
    return lax.all_to_all(value, axis, 0, 0, tiled=True)


def per_device(equilibrium, measurement, coding_masks, upstream, saved_second, conv_first,
               conv_second, conv_third):
    frames = lax.axis_size(TM)
    tiles = lax.axis_size(SPACE)
    total_frames = 2 * frames
    step = 1.0 / total_frames
    scale = 1.0 / math.sqrt(total_frames * R * tiles * W)
    forward = [(i, i + 1) for i in range(tiles - 1)]
    backward = [(i + 1, i) for i in range(tiles - 1)]
    place = lax.axis_index(SPACE)
    odd = place % 2
    places = jnp.stack([place > 0, place < tiles - 1, odd, frames * (1 - odd),
                        frames * odd + lax.axis_index(TM), frames * odd,
                        lax.axis_index(NEAR[1:]), lax.axis_index(FAR[1:])]).astype(jnp.int32)

    hbm = pl.BlockSpec(memory_space=pltpu.HBM)
    whole = pl.BlockSpec(memory_space=pltpu.VMEM)
    scalars = pl.BlockSpec(memory_space=pltpu.SMEM)
    edge = ((EDGE * C + FIELDS * R, LANES), BF)
    fields = ((4 * R, LANES), F32)
    frame = ((2, R, W), F32)
    top, bottom, own_fields = call(
        pack_kernel, [edge, edge, fields],
        [frame, frame, ((2, R, W), jnp.int32), ((R, W), F32), ((2, C, R, W), BF)],
        upstream, equilibrium, coding_masks, measurement, saved_second,
        specs=[hbm] * 5, sems=5, limit=60)
    low = lax.ppermute(bottom, SPACE, forward)
    high = lax.ppermute(top, SPACE, backward)

    forward_w, third_w, second_w, first_w, gate2_own, hidden2, own_fields, table = call(
        stage_kernel,
        [((C, 3 * Q), BF), ((C, 3 * Q), BF), ((3 * C, 3 * C), BF), ((Q, C), BF),
         ((R * C, LANES), F32), ((R * C, LANES), BF), fields, ((8, W), jnp.int32)], [],
        places, conv_first, conv_second, conv_third, saved_second, own_fields,
        specs=[scalars] + [whole] * 5,
        cost=pl.CostEstimate(flops=2 * 10**6, bytes_accessed=10**6, transcendentals=0))

    ext = ((EXT, LANES), F32)
    part, up, masks, base = call(
        functools.partial(unpack_kernel, step),
        [((frames, 32, W), BF), ext, ext, ext], [ext, ext],
        low, own_fields, high, gate2_own)
    sums = exchange(part, TM)

    narrow = EXT - 6
    weights = (third_w, second_w, first_w)
    copies = ((2, EXT * Q, W), F32)
    d2 = (((EXT - 2) * C, LANES), BF)
    d1 = (((EXT - 4) * C, LANES), BF)
    taps = ((2, (EXT - 4) * Q, W), F32)
    slim_scratch = [((2, narrow * Q, W), F32), (((narrow - 2) * C, LANES), BF),
                    (((narrow - 4) * C, LANES), BF), ((2, (narrow - 4) * Q, W), F32)]
    wide_outs = [((frames, 16, W), BF), ((narrow, LANES), F32)]
    part, moved, gate2, gate1, hidden, inputs = call(
        functools.partial(first_kernel, step),
        wide_outs + [(((EXT - 2) * C, LANES), F32), (((EXT - 4) * C, LANES), F32),
                     ((R * C, LANES), BF), (((R + 2) * Q, LANES), BF)],
        [copies, d2, d1, taps],
        table, sums, low, gate2_own, high, up, masks, base, *weights, forward_w)
    sums = exchange(part, TM)

    part, moved = call(
        functools.partial(second_kernel, step),
        [((2 * frames, 2 * R, LANES), BF), ((R, LANES), F32)], slim_scratch,
        sums, moved, up, masks, gate2, gate1, *weights)
    groups = [[t * tiles + (k + side) % tiles for side in range(2) for t in range(frames)]
              for k in range(1, tiles, 2)]
    received = lax.all_to_all(part, TM + SPACE, 0, 0, axis_index_groups=groups, tiled=True)
    field, = call(functools.partial(update_kernel, step), [((R, LANES), F32)], [],
                  table, received, moved, up, masks)
    near = lax.all_gather(field, SPACE[-1])
    part, moved = call(
        functools.partial(third_kernel, step), wide_outs, [copies, d2, d1, taps, ext],
        table, received, field, near, up, masks, gate2, gate1, *weights)
    sums = exchange(part, TM)

    near_sizes = [lax.axis_size(name) for name in NEAR]
    far_sizes = [lax.axis_size(name) for name in FAR]
    near_count = math.prod(near_sizes)
    far_count = math.prod(far_sizes)
    rows = 3 * C // near_count
    piece = -(-(rows + R // 2 // near_sizes[0]) // 8) * 8
    adjoint, grads = call(
        functools.partial(last_kernel, step, near_sizes[0]),
        [((R, LANES), F32), ((near_count, piece, LANES), BF)],
        slim_scratch + [((3 * C + piece, LANES), F32)],
        sums, moved, up, masks, gate2, gate1, hidden2, hidden, inputs, *weights)

    received = exchange(grads, NEAR)
    near_stride = near_count // near_sizes[0]
    far_stride = far_count // far_sizes[0]
    received, = call(
        functools.partial(sum_kernel, rows, near_stride, NEAR_AT),
        [((far_count, piece, LANES), BF)], [], table, received)
    received = exchange(received, FAR)
    received, = call(
        functools.partial(sum_kernel, rows, far_stride, FAR_AT),
        [((near_count, piece, LANES), BF)], [], table, received)
    received = exchange(received, NEAR)
    return call(
        functools.partial(output_kernel, step, scale, near_sizes[0]),
        [((2, R, W), F32), ((R, W), F32), ((9, C), F32), ((9, C, C), F32), ((9, C), F32)],
        [((3 * C, LANES), F32)], table, received, adjoint)


AXES = (("zh", 4), ("core", 2), ("zl", 2), ("yh", 4), ("yl", 2), ("xh", 2), ("xl", 2))


def solution(mesh, axes=AXES):
    names = tuple(name for name, _ in axes)
    sizes = tuple(size for _, size in axes)
    fine = Mesh(mesh.devices.reshape(sizes), names)
    placed = (
        P(TM, SPACE, None),
        P(SPACE, None),
        P(TM, SPACE, None),
        P(TM, SPACE, None),
        P(TM, None, SPACE, None),
        P(),
        P(),
        P(),
    )
    return jax.shard_map(
        per_device,
        mesh=fine,
        in_specs=placed,
        out_specs=(P(TM, SPACE, None), P(SPACE, None), P(), P(), P()),
        check_vma=False,
    )
```

```python
import functools
import math

import jax
import jax.numpy as jnp
from jax import lax
from jax.experimental import pallas as pl
from jax.experimental.pallas import tpu as pltpu
from jax.sharding import Mesh, PartitionSpec as P

ITERS = 3
C = 64
W = 128
LANES = 2 * W
R = 8
HALO = 6
EXT = R + 2 * HALO
EDGE = HALO - 1
FIELDS = 6
Q = 16
PIECE = 32
BF = jnp.bfloat16
F32 = jnp.float32

TM = ("zh", "core")
SPACE = ("zl", "yh", "yl", "xh", "xl")
BEFORE, AFTER, ODD, OWN_HALF, THEIR_ENTRY, THEIR_HALF, NEAR_AT, FAR_AT = range(8)
NEAR = ("core", "zl", "yl", "xh", "xl")
FAR = ("zh", "yh")


def roll_cols(value, step):
    if step == 0:
        return value
    lane = lax.broadcasted_iota(jnp.int32, (value.shape[0], W), 1)
    edge = 0 if step > 0 else W - 1
    halves = []
    for frame in range(2):
        half = value[:, frame * W:(frame + 1) * W]
        half = pltpu.roll(half, step % W, 1)
        halves.append(jnp.where(lane == edge, 0.0, half))
    return jnp.concatenate(halves, axis=1)


def slope_parts(value):
    logistic = 0.5 * jnp.tanh(0.5 * value) + 0.5
    return logistic, logistic * (1.0 + value * (1.0 - logistic))


def put_slot(ref, at, count, value):
    for frame in range(2):
        ref[frame, pl.ds(at, count, stride=Q), :] = value[:, frame * W:(frame + 1) * W]


def take_slot(ref, at, count):
    return jnp.concatenate(
        [ref[frame, pl.ds(at, count, stride=Q), :] for frame in range(2)], axis=1)


def put_rows(ref, at, value):
    for frame in range(2):
        ref[frame, at:at + value.shape[0], :] = value[:, frame * W:(frame + 1) * W]


def take_rows(ref, first, last):
    return jnp.concatenate([ref[frame, first:last, :] for frame in range(2)], axis=1)


def fill_shifted(field, copies, sign):
    count = field.shape[0]
    for slot, step in enumerate((-1, 0, 1)):
        shifted = roll_cols(field, sign * step)
        high = shifted.astype(BF).astype(F32)
        put_slot(copies, slot, count, high)
        put_slot(copies, 3 + slot, count, shifted - high)


def dot(left, right):
    return jnp.dot(left, right, preferred_element_type=F32)


def dot_nt(left, right):
    return lax.dot_general(left, right, (((1,), (1,)), ((), ())), preferred_element_type=F32)


def back_rows(first, field, gate2, third_w, second_w, copies, d2):
    rows = EXT - 2 * first
    fill_shifted(field, copies, 1)
    for k in range(rows - 2):
        third = dot(third_w, take_rows(copies, k * Q, (k + 3) * Q).astype(BF))
        at = first + k
        d2[k * C:(k + 1) * C, :] = (gate2[at * C:(at + 1) * C, :] * third).astype(BF)
    for k in range(rows - 4):
        parts = dot(second_w, d2[k * C:(k + 3) * C, :])
        total = (
            roll_cols(parts[:C], -1) + parts[C:2 * C] + roll_cols(parts[2 * C:], 1)
        )
        yield k, total


def adjoint_map(first, field, gate2, gate1, third_w, second_w, first_w, copies, d2, d1, taps):
    for k, total in back_rows(first, field, gate2, third_w, second_w, copies, d2):
        at = first + k
        row = (gate1[at * C:(at + 1) * C, :] * total).astype(BF)
        d1[k * C:(k + 1) * C, :] = row
    return map_end(first, field, first_w, d1, taps)


def map_end(first, field, first_w, d1, taps):
    count = EXT - 2 * first - 6
    for k in range(count + 2):
        put_rows(taps, k * Q, dot(first_w, d1[k * C:(k + 1) * C, :]))
    result = field[3:3 + count]
    for j in (-1, 0, 1):
        column = None
        for i in (-1, 0, 1):
            tap = 3 * (i + 1) + (j + 1)
            part = take_slot(taps, (1 - i) * Q + tap, count)
            column = part if column is None else column + part
        result = result + roll_cols(column, j)
    return result


def masked_sum(masks, field):
    product = masks * field
    return product[:, :W] + product[:, W:]


def twice(field):
    return jnp.concatenate([field, field], axis=1)


def gathered_sum(ref):
    total = ref[0].astype(F32)
    for k in range(1, ref.shape[0]):
        total = total + ref[k].astype(F32)
    return total


def send_all(part, value):
    fill = jnp.zeros((part.shape[1] - value.shape[0], value.shape[1]), F32)
    value = jnp.concatenate([value, fill], axis=0).astype(part.dtype)
    for k in range(part.shape[0]):
        part[k] = value


def pack_kernel(upstream, equilibrium, masks, measurement, saved, conv_first, conv_second,
                conv_third, to_near, to_far, bundle, narrow, up_in, fixed_in, masks_in,
                snapshot_in, saved_in, first_in, second_in, third_in, sems):
    odd = lax.broadcast_in_dim(lax.axis_index(SPACE[-1]), (1, W), ()) == 1
    copies = [
        pltpu.make_async_copy(source, target, sems.at[k])
        for k, (source, target) in enumerate((
            (saved, saved_in), (upstream, up_in), (equilibrium, fixed_in), (masks, masks_in),
            (measurement, snapshot_in), (conv_first, first_in), (conv_second, second_in),
            (conv_third, third_in)))
    ]
    for copy in copies:
        copy.start()
    for copy in copies[1:]:
        copy.wait()

    def by_frame(ref):
        return jnp.concatenate([ref[0], ref[1]], axis=1)

    up = by_frame(up_in)
    fixed = by_frame(fixed_in)
    mask = by_frame(masks_in).astype(F32)
    snapshot = snapshot_in[...]
    for k, field in enumerate((up, mask, fixed, twice(snapshot))):
        narrow[k * R:(k + 1) * R, :] = field
    narrow[4 * R:, :] = jnp.zeros((4 * R, LANES), F32)
    narrow[4 * R:4 * R + 9, :C] = first_in[...].astype(F32)
    narrow[6 * R:6 * R + 9, :C] = third_in[...].astype(F32)
    for k in range(9):
        at = R * C + (k // 4) * C
        bundle[at:at + C, (k % 4) * C:(k % 4 + 1) * C] = second_in[k]
    bundle[(R + 2) * C:, C:] = jnp.zeros((C, 3 * C), BF)
    fields = (*split_parts(up), *split_parts(fixed), mask.astype(BF),
              jnp.concatenate(split_parts(snapshot), axis=1))
    for k in range(0, len(fields), 2):
        pair = jnp.concatenate([field.astype(F32) for field in fields[k:k + 2]], axis=0).astype(BF)
        at = EDGE * C + k * R
        to_near[at:at + 2 * R, :] = pair
        to_far[at:at + 2 * R, :] = pair
    copies[0].wait()
    for frame in range(2):
        lanes = slice(frame * W, (frame + 1) * W)
        rows = jnp.swapaxes(saved_in[frame].astype(F32), 0, 1).reshape(R * C, W)
        bundle[:R * C, lanes] = rows.astype(BF)
        top = rows[:EDGE * C]
        bottom = rows[(R - EDGE) * C:]
        to_near[:EDGE * C, lanes] = jnp.where(odd, top, bottom).astype(BF)
        to_far[:EDGE * C, lanes] = jnp.where(odd, bottom, top).astype(BF)


def stage_kernel(places, bundle, narrow, forward_w, third_w, second_w, first_w, gate2, hidden2,
                 fields, table):
    fields[...] = narrow[:4 * R, :]
    for k in range(8):
        table[k:k + 1, :] = jnp.full((1, W), places[k], jnp.int32)
    for r in range(R):
        value = saved_row(bundle, r).astype(F32)
        logistic, slope = slope_parts(value)
        gate2[r * C:(r + 1) * C, :] = slope
        hidden2[r * C:(r + 1) * C, :] = (value * logistic).astype(BF)
    forward = narrow[4 * R:4 * R + 9, :C]
    backward = narrow[6 * R:6 * R + 9, :C]
    pad = jnp.zeros((Q - 6, C), F32)
    ahead = []
    back = []
    for i in range(3):
        row = forward[3 * i:3 * i + 3]
        ahead += [row, row, pad]
        row = backward[6 - 3 * i:9 - 3 * i]
        back += [row, row, pad]
        for j in range(3):
            tap = 3 * (2 - i) + j
            at = R * C + (tap // 4) * C
            tile = bundle[at:at + C, (tap % 4) * C:(tap % 4 + 1) * C].astype(F32)
            second_w[j * C:(j + 1) * C, i * C:(i + 1) * C] = jnp.transpose(tile).astype(BF)
    forward_w[...] = jnp.transpose(jnp.concatenate(ahead, axis=0)).astype(BF)
    third_w[...] = jnp.transpose(jnp.concatenate(back, axis=0)).astype(BF)
    first_w[...] = jnp.concatenate([forward, jnp.zeros((Q - 9, C), F32)], axis=0).astype(BF)


def unpack_kernel(step, places, near, far, own_fields, _, part, up, masks, base, fixed, snapshot):
    for k, target in enumerate((up, masks, fixed, snapshot)):
        target[HALO:HALO + R, :] = own_fields[k * R:(k + 1) * R, :]
    for side, at, first in ((0, 0, R - HALO), (1, HALO + R, 0)):
        fields = edge_rows(places, near, far, side, EDGE * C, FIELDS * R)

        def field(k):
            return fields[k * R:(k + 1) * R]

        for target, value in ((up, field(0) + field(1)), (fixed, field(2) + field(3)),
                              (masks, field(4)),
                              (snapshot, twice(field(5)[:, :W] + field(5)[:, W:]))):
            target[at:at + HALO, :] = value[first:first + HALO]
    send_all(part, masked_sum(masks[...], fixed[...]))
    base[...] = fixed[...] + step * masks[...] * snapshot[...]


def edge_rows(places, near, far, side, at, count):
    from_pair = twice(places[ODD:ODD + 1, :]) == 1 - side
    return jnp.where(from_pair, near[side, at:at + count, :].astype(F32),
                     far[at:at + count, :].astype(F32))


def saved_row(ref, at):
    return ref[at * C:(at + 1) * C, :]


def keep_row(value, at, before, after):
    if at < HALO:
        return value * before
    if at >= HALO + R:
        return value * after
    return value


def ends(places):
    return tuple(twice(places[k:k + 1, :]).astype(F32) for k in (BEFORE, AFTER))


def first_kernel(step, places, sums, near, far, own, up, masks, base, third_w, second_w, first_w,
                 forward_w, part, moved, gate2, gate1, hidden, inputs, copies, d2, d1, taps):
    before, after = ends(places)
    for k in range(EXT - 2):
        at = k + 1
        if HALO <= at < HALO + R:
            gate2[k * C:(k + 1) * C, :] = saved_row(own, at - HALO)
        else:
            side, row = (0, k) if at < HALO else (1, at - HALO - R)
            slope = slope_parts(edge_rows(places, near, far, side, row * C, C))[1]
            gate2[k * C:(k + 1) * C, :] = keep_row(slope, at, before, after)
    frame_sum = gathered_sum(sums)[:EXT]
    denoiser_input = base[...] - step * masks[...] * twice(frame_sum)
    copies[...] = jnp.zeros_like(copies)
    fill_shifted(denoiser_input, copies, -1)
    inputs[...] = take_rows(copies, (HALO - 1) * Q, (HALO + R + 1) * Q).astype(BF)
    for k in range(EXT - 4):
        at = k + 2
        value = dot(forward_w[...], take_rows(copies, (at - 1) * Q, (at + 2) * Q).astype(BF))
        logistic, slope = slope_parts(value)
        gate1[k * C:(k + 1) * C, :] = keep_row(slope, at, before, after)
        if HALO <= at < HALO + R:
            own_at = at - HALO
            hidden[own_at * C:(own_at + 1) * C, :] = (value * logistic).astype(BF)
    field = adjoint_map(0, up[...], gate2, gate1, third_w[...], second_w[...], first_w[...],
                        copies, d2, d1, taps)
    finish_wide(field, before, after, masks, part, moved)


def finish_wide(field, before, after, masks, part, moved):
    count = EXT - 6
    row = lax.broadcasted_iota(jnp.int32, field.shape, 0)
    keep = jnp.where(row < HALO - 3, before, jnp.where(row >= HALO - 3 + R, after, 1.0))
    field = field * keep
    moved[...] = field
    send_all(part, masked_sum(masks[3:3 + count, :], field))


def narrow_field(step, sums, moved, up, masks):
    count = EXT - 6
    totals = gathered_sum(sums)[:count]
    return up[3:3 + count, :] + moved[...] - step * masks[3:3 + count, :] * twice(totals)


def second_kernel(step, sums, moved, up, masks, gate2, gate1, third_w, second_w, first_w,
                  part, out, copies, d2, d1, taps):
    copies[...] = jnp.zeros_like(copies)
    field = narrow_field(step, sums, moved, up, masks)
    result = adjoint_map(3, field, gate2, gate1, third_w[...], second_w[...], first_w[...],
                         copies, d2, d1, taps)
    out[...] = result
    total = masked_sum(masks[HALO:HALO + R, :], result)
    half = jnp.concatenate([total[:R // 2], total[R // 2:]], axis=1)
    send_all(part, jnp.concatenate([result, half], axis=0))


def pair_total(received, first):
    count = received.shape[0] // 2
    half = received[first].astype(F32)
    for k in range(1, count):
        half = half + received[first + k].astype(F32)
    half = half[R:R + R // 2]
    return jnp.concatenate([half[:, :W], half[:, W:]], axis=0)


def update_kernel(step, places, received, moved, up, masks, out):
    totals = pair_total(received, places[OWN_HALF, 0])
    out[...] = (up[HALO:HALO + R, :] + moved[...]
                - step * masks[HALO:HALO + R, :] * twice(totals))


def third_kernel(step, places, received, own, near, up, masks, gate2, gate1, third_w,
                 second_w, first_w, part, moved, copies, d2, d1, taps, whole):
    copies[...] = jnp.zeros_like(copies)
    before, after = ends(places)
    totals = twice(pair_total(received, places[THEIR_HALF, 0]))
    theirs = received[places[THEIR_ENTRY, 0]].astype(F32)[:R]
    after_rows = slice(HALO + R, EXT)
    low = (up[0:HALO, :] + theirs[R - HALO:]
           - step * masks[0:HALO, :] * totals[R - HALO:]) * before
    high = (up[after_rows, :] + theirs[:HALO]
            - step * masks[after_rows, :] * totals[:HALO]) * after
    odd = twice(places[ODD:ODD + 1, :]) == 1
    whole[0:HALO, :] = jnp.where(odd, near[0, R - HALO:, :], low)
    whole[HALO:HALO + R, :] = own[...]
    whole[HALO + R:, :] = jnp.where(odd, high, near[1, :HALO, :])
    field = adjoint_map(0, whole[...], gate2, gate1, third_w[...], second_w[...], first_w[...],
                        copies, d2, d1, taps)
    finish_wide(field, before, after, masks, part, moved)


def last_kernel(step, cores, sums, moved, up, masks, gate2, gate1, hidden2, hidden, inputs, third_w,
                second_w, first_w, adjoint, grads, copies, d2, d1, taps, total):
    copies[...] = jnp.zeros_like(copies)
    field = narrow_field(step, sums, moved, up, masks)
    adjoint[...] = field[3:3 + R]
    result = adjoint_map(3, field, gate2, gate1, third_w[...], second_w[...], first_w[...],
                         copies, d2, d1, taps)
    snapshot = masked_sum(masks[HALO:HALO + R, :], result)
    left = []
    right = []
    left_first = []
    right_first = []
    left_third = []
    right_third = []
    for r in range(R):
        left.append(d2[(r + 1) * C:(r + 4) * C, :])
        value = hidden[r * C:(r + 1) * C, :].astype(F32)
        right.append(jnp.concatenate(
            [roll_cols(value, 1), value, roll_cols(value, -1)], axis=0).astype(BF))
        left_first.append(inputs[r * Q:(r + 3) * Q, :])
        right_first.append(d1[(r + 1) * C:(r + 2) * C, :])
        left_third.append(take_rows(copies, (r + 2) * Q, (r + 5) * Q).astype(BF))
        right_third.append(saved_row(hidden2, r))
    def join(parts):
        return jnp.concatenate(parts, axis=1)
    second = dot_nt(join(left), join(right))
    first = dot_nt(join(left_first), join(right_first))
    third = dot_nt(join(left_third), join(right_third))
    total[0:3 * C, 0:3 * C] = second
    total[0:3 * Q, 3 * C:] = first
    total[3 * Q:6 * Q, 3 * C:] = third
    total[6 * Q:, 3 * C:] = jnp.zeros((total.shape[0] - 6 * Q, C), F32)
    total[3 * C:, 0:3 * C] = jnp.zeros((total.shape[0] - 3 * C, 3 * C), F32)
    count = grads.shape[0]
    rows = 3 * C // count
    line = lax.broadcasted_iota(jnp.int32, grads.shape[1:], 0)
    extras = []
    for core in range(cores):
        extra = jnp.zeros(grads.shape[1:], F32)
        for k in range(R // 2 // cores):
            at = 2 * (core * (R // 2 // cores) + k)
            pair = jnp.concatenate([snapshot[at:at + 1], snapshot[at + 1:at + 2]], axis=1)
            extra = jnp.where(line == rows + k, pair, extra)
        extras.append(extra)
    for k in range(count):
        grads[k] = jnp.where(line < rows, total[k * rows:k * rows + grads.shape[1], :],
                             extras[k * cores // count]).astype(BF)


def reduce_pieces(rows, place, stride, received):
    count = received.shape[0]
    total = received[0].astype(F32)
    for k in range(1, count):
        total = total + received[k].astype(F32)
    extra = received[place].astype(F32)
    for k in range(1, count // stride):
        extra = extra + received[place + k * stride].astype(F32)
    line = lax.broadcasted_iota(jnp.int32, total.shape, 0)
    return jnp.where(line < rows, total, extra)


def sum_kernel(rows, stride, at, places, received, out):
    total = reduce_pieces(rows, places[at, 0], stride, received).astype(BF)
    for k in range(out.shape[0]):
        out[k] = total


def output_kernel(step, scale, cores, places, received, field, adjoint, snapshot, first, second,
                  third, total):
    adjoint[0] = field[:, :W]
    adjoint[1] = field[:, W:]
    count = received.shape[0]
    rows = 3 * C // count
    for core in range(cores):
        piece = received[places[NEAR_AT, 0] + core * (count // cores)].astype(F32) * step
        for k in range(R // 2 // cores):
            at = 2 * (core * (R // 2 // cores) + k)
            snapshot[at:at + 1, :] = piece[rows + k:rows + k + 1, :W]
            snapshot[at + 1:at + 2, :] = piece[rows + k:rows + k + 1, W:]
    for k in range(count):
        total[k * rows:(k + 1) * rows, :] = received[k].astype(F32)[:rows] * scale
    for i in (-1, 0, 1):
        for j in (-1, 0, 1):
            tap = 3 * (i + 1) + (j + 1)
            back = 1 - i
            ahead = 1 + i
            second[tap] = total[back * C:(back + 1) * C, (j + 1) * C:(j + 2) * C]
            at = ahead * Q + j + 1
            first[tap:tap + 1, :] = total[at:at + 1, 3 * C:] + total[at + 3:at + 4, 3 * C:]
            at = 3 * Q + back * Q + j + 1
            third[tap:tap + 1, :] = total[at:at + 1, 3 * C:] + total[at + 3:at + 4, 3 * C:]


def call(kernel, outs, scratch, *operands, specs=None, cost=None, sems=0, limit=40):
    if specs is None:
        specs = [pl.BlockSpec(memory_space=pltpu.VMEM)] * len(operands)
    return pl.pallas_call(
        kernel,
        out_shape=[jax.ShapeDtypeStruct(shape, dtype) for shape, dtype in outs],
        in_specs=specs,
        out_specs=[pl.BlockSpec(memory_space=pltpu.VMEM)] * len(outs),
        scratch_shapes=[pltpu.VMEM(shape, dtype) for shape, dtype in scratch]
        + [pltpu.SemaphoreType.DMA((sems,))] * (sems > 0),
        compiler_params=pltpu.CompilerParams(vmem_limit_bytes=limit * 2**20),
        cost_estimate=cost,
    )(*operands)


def split_parts(field):
    high = field.astype(BF)
    return high, (field - high.astype(F32)).astype(BF)


def exchange(value, axis):
    return lax.all_to_all(value, axis, 0, 0, tiled=True)


def per_device(equilibrium, measurement, coding_masks, upstream, saved_second, conv_first,
               conv_second, conv_third):
    frames = lax.axis_size(TM)
    tiles = lax.axis_size(SPACE)
    total_frames = 2 * frames
    step = 1.0 / total_frames
    scale = 1.0 / math.sqrt(total_frames * R * tiles * W)
    place = lax.axis_index(SPACE)
    odd = place % 2
    places = jnp.stack([place > 0, place < tiles - 1, odd, frames * (1 - odd),
                        frames * odd + lax.axis_index(TM), frames * odd,
                        lax.axis_index(NEAR[1:]), lax.axis_index(FAR[1:])]).astype(jnp.int32)

    hbm = pl.BlockSpec(memory_space=pltpu.HBM)
    whole = pl.BlockSpec(memory_space=pltpu.VMEM)
    scalars = pl.BlockSpec(memory_space=pltpu.SMEM)
    edge = ((EDGE * C + FIELDS * R, LANES), BF)
    fields = ((4 * R, LANES), F32)
    frame = ((2, R, W), F32)
    to_near, to_far, bundle, narrow_bundle = call(
        pack_kernel, [edge, edge, (((R + 3) * C, LANES), BF), ((8 * R, LANES), F32)],
        [frame, frame, ((2, R, W), jnp.int32), ((R, W), F32), ((2, C, R, W), BF), ((9, C), BF),
         ((9, C, C), BF), ((9, C), BF)],
        upstream, equilibrium, coding_masks, measurement, saved_second, conv_first, conv_second,
        conv_third, specs=[hbm] * 8, sems=8, limit=60)
    far = lax.ppermute(to_far, SPACE, [(k + side, k + 1 - side) for k in range(1, tiles - 1, 2)
                                       for side in range(2)])
    near = lax.all_gather(to_near, SPACE[-1])

    forward_w, third_w, second_w, first_w, gate2_own, hidden2, own_fields, table = call(
        stage_kernel,
        [((C, 3 * Q), BF), ((C, 3 * Q), BF), ((3 * C, 3 * C), BF), ((Q, C), BF),
         ((R * C, LANES), F32), ((R * C, LANES), BF), fields, ((8, W), jnp.int32)], [],
        places, bundle, narrow_bundle, specs=[scalars] + [whole] * 2,
        cost=pl.CostEstimate(flops=2 * 10**6, bytes_accessed=10**6, transcendentals=0))

    ext = ((EXT, LANES), F32)
    part, up, masks, base = call(
        functools.partial(unpack_kernel, step),
        [((frames, 32, W), BF), ext, ext, ext], [ext, ext],
        table, near, far, own_fields, gate2_own)
    sums = exchange(part, TM)

    narrow = EXT - 6
    weights = (third_w, second_w, first_w)
    copies = ((2, EXT * Q, W), F32)
    d2 = (((EXT - 2) * C, LANES), BF)
    d1 = (((EXT - 4) * C, LANES), BF)
    taps = ((2, (EXT - 4) * Q, W), F32)
    slim_scratch = [((2, narrow * Q, W), F32), (((narrow - 2) * C, LANES), BF),
                    (((narrow - 4) * C, LANES), BF), ((2, (narrow - 4) * Q, W), F32)]
    wide_outs = [((frames, 16, W), BF), ((narrow, LANES), F32)]
    part, moved, gate2, gate1, hidden, inputs = call(
        functools.partial(first_kernel, step),
        wide_outs + [(((EXT - 2) * C, LANES), F32), (((EXT - 4) * C, LANES), F32),
                     ((R * C, LANES), BF), (((R + 2) * Q, LANES), BF)],
        [copies, d2, d1, taps],
        table, sums, near, far, gate2_own, up, masks, base, *weights, forward_w)
    sums = exchange(part, TM)

    part, moved = call(
        functools.partial(second_kernel, step),
        [((2 * frames, 2 * R, LANES), BF), ((R, LANES), F32)], slim_scratch,
        sums, moved, up, masks, gate2, gate1, *weights)
    groups = [[t * tiles + (k + side) % tiles for side in range(2) for t in range(frames)]
              for k in range(1, tiles, 2)]
    received = lax.all_to_all(part, TM + SPACE, 0, 0, axis_index_groups=groups, tiled=True)
    field, = call(functools.partial(update_kernel, step), [((R, LANES), F32)], [],
                  table, received, moved, up, masks)
    near = lax.all_gather(field, SPACE[-1])
    part, moved = call(
        functools.partial(third_kernel, step), wide_outs, [copies, d2, d1, taps, ext],
        table, received, field, near, up, masks, gate2, gate1, *weights)
    sums = exchange(part, TM)

    near_sizes = [lax.axis_size(name) for name in NEAR]
    far_sizes = [lax.axis_size(name) for name in FAR]
    near_count = math.prod(near_sizes)
    far_count = math.prod(far_sizes)
    rows = 3 * C // near_count
    piece = -(-(rows + R // 2 // near_sizes[0]) // 8) * 8
    adjoint, grads = call(
        functools.partial(last_kernel, step, near_sizes[0]),
        [((R, LANES), F32), ((near_count, piece, LANES), BF)],
        slim_scratch + [((3 * C + piece, LANES), F32)],
        sums, moved, up, masks, gate2, gate1, hidden2, hidden, inputs, *weights)

    received = exchange(grads, NEAR)
    near_stride = near_count // near_sizes[0]
    far_stride = far_count // far_sizes[0]
    received, = call(
        functools.partial(sum_kernel, rows, near_stride, NEAR_AT),
        [((far_count, piece, LANES), BF)], [], table, received)
    received = exchange(received, FAR)
    received, = call(
        functools.partial(sum_kernel, rows, far_stride, FAR_AT),
        [((near_count, piece, LANES), BF)], [], table, received)
    received = exchange(received, NEAR)
    return call(
        functools.partial(output_kernel, step, scale, near_sizes[0]),
        [((2, R, W), F32), ((R, W), F32), ((9, C), F32), ((9, C, C), F32), ((9, C), F32)],
        [((3 * C, LANES), F32)], table, received, adjoint)


AXES = (("zh", 4), ("core", 2), ("zl", 2), ("yh", 4), ("yl", 2), ("xh", 2), ("xl", 2))


def solution(mesh, axes=AXES):
    names = tuple(name for name, _ in axes)
    sizes = tuple(size for _, size in axes)
    fine = Mesh(mesh.devices.reshape(sizes), names)
    placed = (
        P(TM, SPACE, None),
        P(SPACE, None),
        P(TM, SPACE, None),
        P(TM, SPACE, None),
        P(TM, None, SPACE, None),
        P(),
        P(),
        P(),
    )
    return jax.shard_map(
        per_device,
        mesh=fine,
        in_specs=placed,
        out_specs=(P(TM, SPACE, None), P(SPACE, None), P(), P(), P()),
        check_vma=False,
    )
```

```python
import functools
import math

import jax
import jax.numpy as jnp
from jax import lax
from jax.experimental import pallas as pl
from jax.experimental.pallas import tpu as pltpu
from jax.sharding import Mesh, PartitionSpec as P

ITERS = 3
C = 64
W = 128
LANES = 2 * W
R = 8
HALO = 6
EXT = R + 2 * HALO
EDGE = HALO - 1
FIELDS_AT = (R + 3) * C
FIRST_AT = FIELDS_AT + 6 * R
THIRD_AT = FIRST_AT + 16
FIELDS = 6
Q = 16
PIECE = 32
BF = jnp.bfloat16
F32 = jnp.float32

TM = ("zh", "core")
SPACE = ("zl", "yh", "yl", "xh", "xl")
BEFORE, AFTER, ODD, OWN_HALF, THEIR_ENTRY, THEIR_HALF, NEAR_AT, FAR_AT = range(8)
NEAR = ("core", "zl", "yl", "xh", "xl")
FAR = ("zh", "yh")


def roll_cols(value, step):
    if step == 0:
        return value
    lane = lax.broadcasted_iota(jnp.int32, (value.shape[0], W), 1)
    edge = 0 if step > 0 else W - 1
    halves = []
    for frame in range(2):
        half = value[:, frame * W:(frame + 1) * W]
        half = pltpu.roll(half, step % W, 1)
        halves.append(jnp.where(lane == edge, 0.0, half))
    return jnp.concatenate(halves, axis=1)


def slope_parts(value):
    logistic = 0.5 * jnp.tanh(0.5 * value) + 0.5
    return logistic, logistic * (1.0 + value * (1.0 - logistic))


def put_slot(ref, at, count, value):
    for frame in range(2):
        ref[frame, pl.ds(at, count, stride=Q), :] = value[:, frame * W:(frame + 1) * W]


def take_slot(ref, at, count):
    return jnp.concatenate(
        [ref[frame, pl.ds(at, count, stride=Q), :] for frame in range(2)], axis=1)


def put_rows(ref, at, value):
    for frame in range(2):
        ref[frame, at:at + value.shape[0], :] = value[:, frame * W:(frame + 1) * W]


def take_rows(ref, first, last):
    return jnp.concatenate([ref[frame, first:last, :] for frame in range(2)], axis=1)


def fill_shifted(field, copies, sign):
    count = field.shape[0]
    for slot, step in enumerate((-1, 0, 1)):
        shifted = roll_cols(field, sign * step)
        high = shifted.astype(BF).astype(F32)
        put_slot(copies, slot, count, high)
        put_slot(copies, 3 + slot, count, shifted - high)


def dot(left, right):
    return jnp.dot(left, right, preferred_element_type=F32)


def dot_nt(left, right):
    return lax.dot_general(left, right, (((1,), (1,)), ((), ())), preferred_element_type=F32)


def back_rows(first, field, gate2, third_w, second_w, copies, d2):
    rows = EXT - 2 * first
    fill_shifted(field, copies, 1)
    for k in range(rows - 2):
        third = dot(third_w, take_rows(copies, k * Q, (k + 3) * Q).astype(BF))
        at = first + k
        d2[k * C:(k + 1) * C, :] = (gate2[at * C:(at + 1) * C, :] * third).astype(BF)
    for k in range(rows - 4):
        parts = dot(second_w, d2[k * C:(k + 3) * C, :])
        total = (
            roll_cols(parts[:C], -1) + parts[C:2 * C] + roll_cols(parts[2 * C:], 1)
        )
        yield k, total


def adjoint_map(first, field, gate2, gate1, third_w, second_w, first_w, copies, d2, d1, taps):
    for k, total in back_rows(first, field, gate2, third_w, second_w, copies, d2):
        at = first + k
        row = (gate1[at * C:(at + 1) * C, :] * total).astype(BF)
        d1[k * C:(k + 1) * C, :] = row
    return map_end(first, field, first_w, d1, taps)


def map_end(first, field, first_w, d1, taps):
    count = EXT - 2 * first - 6
    for k in range(count + 2):
        put_rows(taps, k * Q, dot(first_w, d1[k * C:(k + 1) * C, :]))
    result = field[3:3 + count]
    for j in (-1, 0, 1):
        column = None
        for i in (-1, 0, 1):
            tap = 3 * (i + 1) + (j + 1)
            part = take_slot(taps, (1 - i) * Q + tap, count)
            column = part if column is None else column + part
        result = result + roll_cols(column, j)
    return result


def masked_sum(masks, field):
    product = masks * field
    return product[:, :W] + product[:, W:]


def twice(field):
    return jnp.concatenate([field, field], axis=1)


def gathered_sum(ref):
    total = ref[0].astype(F32)
    for k in range(1, ref.shape[0]):
        total = total + ref[k].astype(F32)
    return total


def send_all(part, value):
    fill = jnp.zeros((part.shape[1] - value.shape[0], value.shape[1]), F32)
    value = jnp.concatenate([value, fill], axis=0).astype(part.dtype)
    for k in range(part.shape[0]):
        part[k] = value


def pack_kernel(upstream, equilibrium, masks, measurement, saved, conv_first, conv_second,
                conv_third, to_near, to_far, bundle, up_in, fixed_in, masks_in,
                snapshot_in, saved_in, first_in, second_in, third_in, sems):
    odd = lax.broadcast_in_dim(lax.axis_index(SPACE[-1]), (1, W), ()) == 1
    copies = [
        pltpu.make_async_copy(source, target, sems.at[k])
        for k, (source, target) in enumerate((
            (saved, saved_in), (upstream, up_in), (equilibrium, fixed_in), (masks, masks_in),
            (measurement, snapshot_in), (conv_first, first_in), (conv_second, second_in),
            (conv_third, third_in)))
    ]
    for copy in copies:
        copy.start()
    for copy in copies[1:]:
        copy.wait()

    def by_frame(ref):
        return jnp.concatenate([ref[0], ref[1]], axis=1)

    up = by_frame(up_in)
    fixed = by_frame(fixed_in)
    mask = by_frame(masks_in).astype(F32)
    snapshot = snapshot_in[...]
    for at, ref in ((FIRST_AT, first_in), (THIRD_AT, third_in)):
        taps = jnp.concatenate([ref[...].astype(F32), jnp.zeros((Q - 9, C), F32)], axis=0)
        taps = jnp.concatenate([taps, jnp.zeros((Q, 3 * C), F32)], axis=1)
        bundle[at:at + Q, :] = taps.astype(BF)
    for k in range(9):
        at = R * C + (k // 4) * C
        bundle[at:at + C, (k % 4) * C:(k % 4 + 1) * C] = second_in[k]
    bundle[(R + 2) * C:FIELDS_AT, C:] = jnp.zeros((C, 3 * C), BF)
    fields = (*split_parts(up), *split_parts(fixed), mask.astype(BF),
              jnp.concatenate(split_parts(snapshot), axis=1))
    for k in range(0, len(fields), 2):
        pair = jnp.concatenate([field.astype(F32) for field in fields[k:k + 2]], axis=0).astype(BF)
        at = EDGE * C + k * R
        to_near[at:at + 2 * R, :] = pair
        to_far[at:at + 2 * R, :] = pair
        bundle[FIELDS_AT + k * R:FIELDS_AT + (k + 2) * R, :] = pair
    copies[0].wait()
    for frame in range(2):
        lanes = slice(frame * W, (frame + 1) * W)
        rows = jnp.swapaxes(saved_in[frame].astype(F32), 0, 1).reshape(R * C, W)
        bundle[:R * C, lanes] = rows.astype(BF)
        top = rows[:EDGE * C]
        bottom = rows[(R - EDGE) * C:]
        to_near[:EDGE * C, lanes] = jnp.where(odd, top, bottom).astype(BF)
        to_far[:EDGE * C, lanes] = jnp.where(odd, bottom, top).astype(BF)


def stage_kernel(frames, tiles, bundle, forward_w, third_w, second_w, first_w, gate2, hidden2,
                 fields, table):
    place = lax.axis_index(SPACE)
    odd = lax.axis_index(SPACE[-1])
    entries = {BEFORE: jnp.minimum(place, 1), AFTER: jnp.minimum(tiles - 1 - place, 1), ODD: odd,
               OWN_HALF: frames * (1 - odd), THEIR_ENTRY: frames * odd + lax.axis_index(TM),
               THEIR_HALF: frames * odd, NEAR_AT: lax.axis_index(NEAR[1:]),
               FAR_AT: lax.axis_index(FAR[1:])}
    for k, entry in entries.items():
        table[k:k + 1, :] = lax.broadcast_in_dim(entry.astype(jnp.int32), (1, W), ())
    rows = bundle[FIELDS_AT:FIRST_AT, :].astype(F32)
    pair = rows[5 * R:]
    for k, field in enumerate((rows[:R] + rows[R:2 * R], rows[4 * R:5 * R],
                               rows[2 * R:3 * R] + rows[3 * R:4 * R],
                               twice(pair[:, :W] + pair[:, W:]))):
        fields[k * R:(k + 1) * R, :] = field
    for r in range(R):
        value = saved_row(bundle, r).astype(F32)
        logistic, slope = slope_parts(value)
        gate2[r * C:(r + 1) * C, :] = slope
        hidden2[r * C:(r + 1) * C, :] = (value * logistic).astype(BF)
    forward = bundle[FIRST_AT:FIRST_AT + Q, :].astype(F32)[:9, :C]
    backward = bundle[THIRD_AT:THIRD_AT + Q, :].astype(F32)[:9, :C]
    pad = jnp.zeros((Q - 6, C), F32)
    ahead = []
    back = []
    for i in range(3):
        row = forward[3 * i:3 * i + 3]
        ahead += [row, row, pad]
        row = backward[6 - 3 * i:9 - 3 * i]
        back += [row, row, pad]
        for j in range(3):
            tap = 3 * (2 - i) + j
            at = R * C + (tap // 4) * C
            tile = bundle[at:at + C, (tap % 4) * C:(tap % 4 + 1) * C].astype(F32)
            second_w[j * C:(j + 1) * C, i * C:(i + 1) * C] = jnp.transpose(tile).astype(BF)
    forward_w[...] = jnp.transpose(jnp.concatenate(ahead, axis=0)).astype(BF)
    third_w[...] = jnp.transpose(jnp.concatenate(back, axis=0)).astype(BF)
    first_w[...] = jnp.concatenate([forward, jnp.zeros((Q - 9, C), F32)], axis=0).astype(BF)


def unpack_kernel(step, places, near, far, own_fields, _, part, up, masks, base, fixed, snapshot):
    for k, target in enumerate((up, masks, fixed, snapshot)):
        target[HALO:HALO + R, :] = own_fields[k * R:(k + 1) * R, :]
    for side, at, first in ((0, 0, R - HALO), (1, HALO + R, 0)):
        fields = edge_rows(places, near, far, side, EDGE * C, FIELDS * R)

        def field(k):
            return fields[k * R:(k + 1) * R]

        for target, value in ((up, field(0) + field(1)), (fixed, field(2) + field(3)),
                              (masks, field(4)),
                              (snapshot, twice(field(5)[:, :W] + field(5)[:, W:]))):
            target[at:at + HALO, :] = value[first:first + HALO]
    send_all(part, masked_sum(masks[...], fixed[...]))
    base[...] = fixed[...] + step * masks[...] * snapshot[...]


def edge_rows(places, near, far, side, at, count):
    from_pair = twice(places[ODD:ODD + 1, :]) == 1 - side
    return jnp.where(from_pair, near[side, at:at + count, :].astype(F32),
                     far[at:at + count, :].astype(F32))


def saved_row(ref, at):
    return ref[at * C:(at + 1) * C, :]


def keep_row(value, at, before, after):
    if at < HALO:
        return value * before
    if at >= HALO + R:
        return value * after
    return value


def ends(places):
    return tuple(twice(places[k:k + 1, :]).astype(F32) for k in (BEFORE, AFTER))


def first_kernel(step, places, sums, near, far, own, up, masks, base, third_w, second_w, first_w,
                 forward_w, part, moved, gate2, gate1, hidden, inputs, copies, d2, d1, taps):
    before, after = ends(places)
    for k in range(EXT - 2):
        at = k + 1
        if HALO <= at < HALO + R:
            gate2[k * C:(k + 1) * C, :] = saved_row(own, at - HALO)
        else:
            side, row = (0, k) if at < HALO else (1, at - HALO - R)
            slope = slope_parts(edge_rows(places, near, far, side, row * C, C))[1]
            gate2[k * C:(k + 1) * C, :] = keep_row(slope, at, before, after)
    frame_sum = gathered_sum(sums)[:EXT]
    denoiser_input = base[...] - step * masks[...] * twice(frame_sum)
    copies[...] = jnp.zeros_like(copies)
    fill_shifted(denoiser_input, copies, -1)
    inputs[...] = take_rows(copies, (HALO - 1) * Q, (HALO + R + 1) * Q).astype(BF)
    for k in range(EXT - 4):
        at = k + 2
        value = dot(forward_w[...], take_rows(copies, (at - 1) * Q, (at + 2) * Q).astype(BF))
        logistic, slope = slope_parts(value)
        gate1[k * C:(k + 1) * C, :] = keep_row(slope, at, before, after)
        if HALO <= at < HALO + R:
            own_at = at - HALO
            hidden[own_at * C:(own_at + 1) * C, :] = (value * logistic).astype(BF)
    field = adjoint_map(0, up[...], gate2, gate1, third_w[...], second_w[...], first_w[...],
                        copies, d2, d1, taps)
    finish_wide(field, before, after, masks, part, moved)


def finish_wide(field, before, after, masks, part, moved):
    count = EXT - 6
    row = lax.broadcasted_iota(jnp.int32, field.shape, 0)
    keep = jnp.where(row < HALO - 3, before, jnp.where(row >= HALO - 3 + R, after, 1.0))
    field = field * keep
    moved[...] = field
    send_all(part, masked_sum(masks[3:3 + count, :], field))


def narrow_field(step, sums, moved, up, masks):
    count = EXT - 6
    totals = gathered_sum(sums)[:count]
    return up[3:3 + count, :] + moved[...] - step * masks[3:3 + count, :] * twice(totals)


def second_kernel(step, sums, moved, up, masks, gate2, gate1, third_w, second_w, first_w,
                  part, out, copies, d2, d1, taps):
    copies[...] = jnp.zeros_like(copies)
    field = narrow_field(step, sums, moved, up, masks)
    result = adjoint_map(3, field, gate2, gate1, third_w[...], second_w[...], first_w[...],
                         copies, d2, d1, taps)
    out[...] = result
    total = masked_sum(masks[HALO:HALO + R, :], result)
    half = jnp.concatenate([total[:R // 2], total[R // 2:]], axis=1)
    send_all(part, jnp.concatenate([result, half], axis=0))


def pair_total(received, first):
    count = received.shape[0] // 2
    half = received[first].astype(F32)
    for k in range(1, count):
        half = half + received[first + k].astype(F32)
    half = half[R:R + R // 2]
    return jnp.concatenate([half[:, :W], half[:, W:]], axis=0)


def update_kernel(step, places, received, moved, up, masks, out):
    totals = pair_total(received, places[OWN_HALF, 0])
    out[...] = (up[HALO:HALO + R, :] + moved[...]
                - step * masks[HALO:HALO + R, :] * twice(totals))


def third_kernel(step, places, received, own, near, up, masks, gate2, gate1, third_w,
                 second_w, first_w, part, moved, copies, d2, d1, taps, whole):
    copies[...] = jnp.zeros_like(copies)
    before, after = ends(places)
    totals = twice(pair_total(received, places[THEIR_HALF, 0]))
    theirs = received[places[THEIR_ENTRY, 0]].astype(F32)[:R]
    after_rows = slice(HALO + R, EXT)
    low = (up[0:HALO, :] + theirs[R - HALO:]
           - step * masks[0:HALO, :] * totals[R - HALO:]) * before
    high = (up[after_rows, :] + theirs[:HALO]
            - step * masks[after_rows, :] * totals[:HALO]) * after
    odd = twice(places[ODD:ODD + 1, :]) == 1
    whole[0:HALO, :] = jnp.where(odd, near[0, R - HALO:, :], low)
    whole[HALO:HALO + R, :] = own[...]
    whole[HALO + R:, :] = jnp.where(odd, high, near[1, :HALO, :])
    field = adjoint_map(0, whole[...], gate2, gate1, third_w[...], second_w[...], first_w[...],
                        copies, d2, d1, taps)
    finish_wide(field, before, after, masks, part, moved)


def last_kernel(step, cores, sums, moved, up, masks, gate2, gate1, hidden2, hidden, inputs, third_w,
                second_w, first_w, adjoint, grads, copies, d2, d1, taps, total):
    copies[...] = jnp.zeros_like(copies)
    field = narrow_field(step, sums, moved, up, masks)
    adjoint[...] = field[3:3 + R]
    result = adjoint_map(3, field, gate2, gate1, third_w[...], second_w[...], first_w[...],
                         copies, d2, d1, taps)
    snapshot = masked_sum(masks[HALO:HALO + R, :], result)
    left = []
    right = []
    left_first = []
    right_first = []
    left_third = []
    right_third = []
    for r in range(R):
        left.append(d2[(r + 1) * C:(r + 4) * C, :])
        value = hidden[r * C:(r + 1) * C, :].astype(F32)
        right.append(jnp.concatenate(
            [roll_cols(value, 1), value, roll_cols(value, -1)], axis=0).astype(BF))
        left_first.append(inputs[r * Q:(r + 3) * Q, :])
        right_first.append(d1[(r + 1) * C:(r + 2) * C, :])
        left_third.append(take_rows(copies, (r + 2) * Q, (r + 5) * Q).astype(BF))
        right_third.append(saved_row(hidden2, r))
    def join(parts):
        return jnp.concatenate(parts, axis=1)
    second = dot_nt(join(left), join(right))
    first = dot_nt(join(left_first), join(right_first))
    third = dot_nt(join(left_third), join(right_third))
    total[0:3 * C, 0:3 * C] = second
    total[0:3 * Q, 3 * C:] = first
    total[3 * Q:6 * Q, 3 * C:] = third
    total[6 * Q:, 3 * C:] = jnp.zeros((total.shape[0] - 6 * Q, C), F32)
    total[3 * C:, 0:3 * C] = jnp.zeros((total.shape[0] - 3 * C, 3 * C), F32)
    count = grads.shape[0]
    rows = 3 * C // count
    line = lax.broadcasted_iota(jnp.int32, grads.shape[1:], 0)
    extras = []
    for core in range(cores):
        extra = jnp.zeros(grads.shape[1:], F32)
        for k in range(R // 2 // cores):
            at = 2 * (core * (R // 2 // cores) + k)
            pair = jnp.concatenate([snapshot[at:at + 1], snapshot[at + 1:at + 2]], axis=1)
            extra = jnp.where(line == rows + k, pair, extra)
        extras.append(extra)
    for k in range(count):
        grads[k] = jnp.where(line < rows, total[k * rows:k * rows + grads.shape[1], :],
                             extras[k * cores // count]).astype(BF)


def reduce_pieces(rows, place, stride, received):
    count = received.shape[0]
    total = received[0].astype(F32)
    for k in range(1, count):
        total = total + received[k].astype(F32)
    extra = received[place].astype(F32)
    for k in range(1, count // stride):
        extra = extra + received[place + k * stride].astype(F32)
    line = lax.broadcasted_iota(jnp.int32, total.shape, 0)
    return jnp.where(line < rows, total, extra)


def sum_kernel(rows, stride, at, places, received, out):
    total = reduce_pieces(rows, places[at, 0], stride, received).astype(BF)
    for k in range(out.shape[0]):
        out[k] = total


def output_kernel(step, scale, cores, places, received, field, adjoint, snapshot, first, second,
                  third, total):
    adjoint[0] = field[:, :W]
    adjoint[1] = field[:, W:]
    count = received.shape[0]
    rows = 3 * C // count
    for core in range(cores):
        piece = received[places[NEAR_AT, 0] + core * (count // cores)].astype(F32) * step
        for k in range(R // 2 // cores):
            at = 2 * (core * (R // 2 // cores) + k)
            snapshot[at:at + 1, :] = piece[rows + k:rows + k + 1, :W]
            snapshot[at + 1:at + 2, :] = piece[rows + k:rows + k + 1, W:]
    for k in range(count):
        total[k * rows:(k + 1) * rows, :] = received[k].astype(F32)[:rows] * scale
    for i in (-1, 0, 1):
        for j in (-1, 0, 1):
            tap = 3 * (i + 1) + (j + 1)
            back = 1 - i
            ahead = 1 + i
            second[tap] = total[back * C:(back + 1) * C, (j + 1) * C:(j + 2) * C]
            at = ahead * Q + j + 1
            first[tap:tap + 1, :] = total[at:at + 1, 3 * C:] + total[at + 3:at + 4, 3 * C:]
            at = 3 * Q + back * Q + j + 1
            third[tap:tap + 1, :] = total[at:at + 1, 3 * C:] + total[at + 3:at + 4, 3 * C:]


def call(kernel, outs, scratch, *operands, specs=None, cost=None, sems=0, limit=40):
    if specs is None:
        specs = [pl.BlockSpec(memory_space=pltpu.VMEM)] * len(operands)
    return pl.pallas_call(
        kernel,
        out_shape=[jax.ShapeDtypeStruct(shape, dtype) for shape, dtype in outs],
        in_specs=specs,
        out_specs=[pl.BlockSpec(memory_space=pltpu.VMEM)] * len(outs),
        scratch_shapes=[pltpu.VMEM(shape, dtype) for shape, dtype in scratch]
        + [pltpu.SemaphoreType.DMA((sems,))] * (sems > 0),
        compiler_params=pltpu.CompilerParams(vmem_limit_bytes=limit * 2**20),
        cost_estimate=cost,
    )(*operands)


def split_parts(field):
    high = field.astype(BF)
    return high, (field - high.astype(F32)).astype(BF)


def exchange(value, axis):
    return lax.all_to_all(value, axis, 0, 0, tiled=True)


def per_device(equilibrium, measurement, coding_masks, upstream, saved_second, conv_first,
               conv_second, conv_third):
    frames = lax.axis_size(TM)
    tiles = lax.axis_size(SPACE)
    total_frames = 2 * frames
    step = 1.0 / total_frames
    scale = 1.0 / math.sqrt(total_frames * R * tiles * W)
    hbm = pl.BlockSpec(memory_space=pltpu.HBM)
    whole = pl.BlockSpec(memory_space=pltpu.VMEM)
    edge = ((EDGE * C + FIELDS * R, LANES), BF)
    fields = ((4 * R, LANES), F32)
    frame = ((2, R, W), F32)
    to_near, to_far, bundle = call(
        pack_kernel, [edge, edge, ((THIRD_AT + Q, LANES), BF)],
        [frame, frame, ((2, R, W), jnp.int32), ((R, W), F32), ((2, C, R, W), BF), ((9, C), BF),
         ((9, C, C), BF), ((9, C), BF)],
        upstream, equilibrium, coding_masks, measurement, saved_second, conv_first, conv_second,
        conv_third, specs=[hbm] * 8, sems=8, limit=60)
    far = lax.ppermute(to_far, SPACE, [(k + side, k + 1 - side) for k in range(1, tiles - 1, 2)
                                       for side in range(2)])
    near = lax.all_gather(to_near, SPACE[-1])

    forward_w, third_w, second_w, first_w, gate2_own, hidden2, own_fields, table = call(
        functools.partial(stage_kernel, frames, tiles),
        [((C, 3 * Q), BF), ((C, 3 * Q), BF), ((3 * C, 3 * C), BF), ((Q, C), BF),
         ((R * C, LANES), F32), ((R * C, LANES), BF), fields, ((8, W), jnp.int32)], [],
        bundle,
        cost=pl.CostEstimate(flops=2 * 10**6, bytes_accessed=10**6, transcendentals=0))

    ext = ((EXT, LANES), F32)
    part, up, masks, base = call(
        functools.partial(unpack_kernel, step),
        [((frames, 32, W), BF), ext, ext, ext], [ext, ext],
        table, near, far, own_fields, gate2_own)
    sums = exchange(part, TM)

    narrow = EXT - 6
    weights = (third_w, second_w, first_w)
    copies = ((2, EXT * Q, W), F32)
    d2 = (((EXT - 2) * C, LANES), BF)
    d1 = (((EXT - 4) * C, LANES), BF)
    taps = ((2, (EXT - 4) * Q, W), F32)
    slim_scratch = [((2, narrow * Q, W), F32), (((narrow - 2) * C, LANES), BF),
                    (((narrow - 4) * C, LANES), BF), ((2, (narrow - 4) * Q, W), F32)]
    wide_outs = [((frames, 16, W), BF), ((narrow, LANES), F32)]
    part, moved, gate2, gate1, hidden, inputs = call(
        functools.partial(first_kernel, step),
        wide_outs + [(((EXT - 2) * C, LANES), F32), (((EXT - 4) * C, LANES), F32),
                     ((R * C, LANES), BF), (((R + 2) * Q, LANES), BF)],
        [copies, d2, d1, taps],
        table, sums, near, far, gate2_own, up, masks, base, *weights, forward_w)
    sums = exchange(part, TM)

    part, moved = call(
        functools.partial(second_kernel, step),
        [((2 * frames, 2 * R, LANES), BF), ((R, LANES), F32)], slim_scratch,
        sums, moved, up, masks, gate2, gate1, *weights)
    groups = [[t * tiles + (k + side) % tiles for side in range(2) for t in range(frames)]
              for k in range(1, tiles, 2)]
    received = lax.all_to_all(part, TM + SPACE, 0, 0, axis_index_groups=groups, tiled=True)
    field, = call(functools.partial(update_kernel, step), [((R, LANES), F32)], [],
                  table, received, moved, up, masks)
    near = lax.all_gather(field, SPACE[-1])
    part, moved = call(
        functools.partial(third_kernel, step), wide_outs, [copies, d2, d1, taps, ext],
        table, received, field, near, up, masks, gate2, gate1, *weights)
    sums = exchange(part, TM)

    near_sizes = [lax.axis_size(name) for name in NEAR]
    far_sizes = [lax.axis_size(name) for name in FAR]
    near_count = math.prod(near_sizes)
    far_count = math.prod(far_sizes)
    rows = 3 * C // near_count
    piece = -(-(rows + R // 2 // near_sizes[0]) // 8) * 8
    adjoint, grads = call(
        functools.partial(last_kernel, step, near_sizes[0]),
        [((R, LANES), F32), ((near_count, piece, LANES), BF)],
        slim_scratch + [((3 * C + piece, LANES), F32)],
        sums, moved, up, masks, gate2, gate1, hidden2, hidden, inputs, *weights)

    received = exchange(grads, NEAR)
    near_stride = near_count // near_sizes[0]
    far_stride = far_count // far_sizes[0]
    received, = call(
        functools.partial(sum_kernel, rows, near_stride, NEAR_AT),
        [((far_count, piece, LANES), BF)], [], table, received)
    received = exchange(received, FAR)
    received, = call(
        functools.partial(sum_kernel, rows, far_stride, FAR_AT),
        [((near_count, piece, LANES), BF)], [], table, received)
    received = exchange(received, NEAR)
    return call(
        functools.partial(output_kernel, step, scale, near_sizes[0]),
        [((2, R, W), F32), ((R, W), F32), ((9, C), F32), ((9, C, C), F32), ((9, C), F32)],
        [((3 * C, LANES), F32)], table, received, adjoint)


AXES = (("zh", 4), ("core", 2), ("zl", 2), ("yh", 4), ("yl", 2), ("xh", 2), ("xl", 2))


def solution(mesh, axes=AXES):
    names = tuple(name for name, _ in axes)
    sizes = tuple(size for _, size in axes)
    fine = Mesh(mesh.devices.reshape(sizes), names)
    placed = (
        P(TM, SPACE, None),
        P(SPACE, None),
        P(TM, SPACE, None),
        P(TM, SPACE, None),
        P(TM, None, SPACE, None),
        P(),
        P(),
        P(),
    )
    return jax.shard_map(
        per_device,
        mesh=fine,
        in_specs=placed,
        out_specs=(P(TM, SPACE, None), P(SPACE, None), P(), P(), P()),
        check_vma=False,
    )
```

```python
import functools
import math

import jax
import jax.numpy as jnp
from jax import lax
from jax.experimental import pallas as pl
from jax.experimental.pallas import tpu as pltpu
from jax.sharding import Mesh, PartitionSpec as P

ITERS = 3
C = 64
W = 128
LANES = 2 * W
R = 8
HALO = 6
EXT = R + 2 * HALO
EDGE = HALO - 1
FIELDS_AT = (R + 3) * C
FIRST_AT = FIELDS_AT + 6 * R
THIRD_AT = FIRST_AT + 16
FIELDS = 6
Q = 16
PIECE = 32
BF = jnp.bfloat16
F32 = jnp.float32

TM = ("zh", "core")
SPACE = ("zl", "yh", "yl", "xh", "xl")
BEFORE, AFTER, ODD, OWN_HALF, THEIR_ENTRY, THEIR_HALF, NEAR_AT, FAR_AT = range(8)
NEAR = ("core", "zl", "yl", "xh", "xl")
FAR = ("zh", "yh")


def roll_cols(value, step):
    if step == 0:
        return value
    lane = lax.broadcasted_iota(jnp.int32, (value.shape[0], W), 1)
    edge = 0 if step > 0 else W - 1
    halves = []
    for frame in range(2):
        half = value[:, frame * W:(frame + 1) * W]
        half = pltpu.roll(half, step % W, 1)
        halves.append(jnp.where(lane == edge, 0.0, half))
    return jnp.concatenate(halves, axis=1)


def slope_parts(value):
    logistic = 0.5 * jnp.tanh(0.5 * value) + 0.5
    return logistic, logistic * (1.0 + value * (1.0 - logistic))


def put_slot(ref, at, count, value):
    for frame in range(2):
        ref[frame, pl.ds(at, count, stride=Q), :] = value[:, frame * W:(frame + 1) * W]


def take_slot(ref, at, count):
    return jnp.concatenate(
        [ref[frame, pl.ds(at, count, stride=Q), :] for frame in range(2)], axis=1)


def put_rows(ref, at, value):
    for frame in range(2):
        ref[frame, at:at + value.shape[0], :] = value[:, frame * W:(frame + 1) * W]


def take_rows(ref, first, last):
    return jnp.concatenate([ref[frame, first:last, :] for frame in range(2)], axis=1)


def fill_shifted(field, copies, sign):
    count = field.shape[0]
    for slot, step in enumerate((-1, 0, 1)):
        shifted = roll_cols(field, sign * step)
        high = shifted.astype(BF).astype(F32)
        put_slot(copies, slot, count, high)
        put_slot(copies, 3 + slot, count, shifted - high)


def dot(left, right):
    return jnp.dot(left, right, preferred_element_type=F32)


def dot_nt(left, right):
    return lax.dot_general(left, right, (((1,), (1,)), ((), ())), preferred_element_type=F32)


def back_rows(first, field, gate2, third_w, second_w, copies, d2):
    rows = EXT - 2 * first
    fill_shifted(field, copies, 1)
    for k in range(rows - 2):
        third = dot(third_w, take_rows(copies, k * Q, (k + 3) * Q).astype(BF))
        at = first + k
        d2[k * C:(k + 1) * C, :] = (gate2[at * C:(at + 1) * C, :] * third).astype(BF)
    for k in range(rows - 4):
        parts = dot(second_w, d2[k * C:(k + 3) * C, :])
        total = (
            roll_cols(parts[:C], -1) + parts[C:2 * C] + roll_cols(parts[2 * C:], 1)
        )
        yield k, total


def adjoint_map(first, field, gate2, gate1, third_w, second_w, first_w, copies, d2, d1, taps):
    for k, total in back_rows(first, field, gate2, third_w, second_w, copies, d2):
        at = first + k
        row = (gate1[at * C:(at + 1) * C, :] * total).astype(BF)
        d1[k * C:(k + 1) * C, :] = row
    return map_end(first, field, first_w, d1, taps)


def map_end(first, field, first_w, d1, taps):
    count = EXT - 2 * first - 6
    for k in range(count + 2):
        put_rows(taps, k * Q, dot(first_w, d1[k * C:(k + 1) * C, :]))
    result = field[3:3 + count]
    for j in (-1, 0, 1):
        column = None
        for i in (-1, 0, 1):
            tap = 3 * (i + 1) + (j + 1)
            part = take_slot(taps, (1 - i) * Q + tap, count)
            column = part if column is None else column + part
        result = result + roll_cols(column, j)
    return result


def masked_sum(masks, field):
    product = masks * field
    return product[:, :W] + product[:, W:]


def twice(field):
    return jnp.concatenate([field, field], axis=1)


def gathered_sum(ref):
    total = ref[0].astype(F32)
    for k in range(1, ref.shape[0]):
        total = total + ref[k].astype(F32)
    return total


def send_all(part, value):
    fill = jnp.zeros((part.shape[1] - value.shape[0], value.shape[1]), F32)
    value = jnp.concatenate([value, fill], axis=0).astype(part.dtype)
    for k in range(part.shape[0]):
        part[k] = value


def pack_kernel(upstream, equilibrium, masks, measurement, saved, conv_first, conv_second,
                conv_third, to_near, to_far, bundle, up_in, fixed_in, masks_in,
                snapshot_in, saved_in, first_in, second_in, third_in, sems):
    odd = lax.broadcast_in_dim(lax.axis_index(SPACE[-1]), (1, W), ()) == 1
    copies = [
        pltpu.make_async_copy(source, target, sems.at[k])
        for k, (source, target) in enumerate((
            (saved, saved_in), (upstream, up_in), (equilibrium, fixed_in), (masks, masks_in),
            (measurement, snapshot_in), (conv_first, first_in), (conv_second, second_in),
            (conv_third, third_in)))
    ]
    for copy in copies:
        copy.start()
    for copy in copies[1:]:
        copy.wait()

    def by_frame(ref):
        return jnp.concatenate([ref[0], ref[1]], axis=1)

    up = by_frame(up_in)
    fixed = by_frame(fixed_in)
    mask = by_frame(masks_in).astype(F32)
    snapshot = snapshot_in[...]
    for at, ref in ((FIRST_AT, first_in), (THIRD_AT, third_in)):
        taps = jnp.concatenate([ref[...].astype(F32), jnp.zeros((Q - 9, C), F32)], axis=0)
        taps = jnp.concatenate([taps, jnp.zeros((Q, 3 * C), F32)], axis=1)
        bundle[at:at + Q, :] = taps.astype(BF)
    for k in range(9):
        at = R * C + (k // 4) * C
        bundle[at:at + C, (k % 4) * C:(k % 4 + 1) * C] = second_in[k]
    bundle[(R + 2) * C:FIELDS_AT, C:] = jnp.zeros((C, 3 * C), BF)
    fields = (*split_parts(up), *split_parts(fixed), mask.astype(BF),
              jnp.concatenate(split_parts(snapshot), axis=1))
    for k in range(0, len(fields), 2):
        pair = jnp.concatenate([field.astype(F32) for field in fields[k:k + 2]], axis=0).astype(BF)
        at = EDGE * C + k * R
        to_near[at:at + 2 * R, :] = pair
        to_far[at:at + 2 * R, :] = pair
        bundle[FIELDS_AT + k * R:FIELDS_AT + (k + 2) * R, :] = pair
    copies[0].wait()
    for frame in range(2):
        lanes = slice(frame * W, (frame + 1) * W)
        rows = jnp.swapaxes(saved_in[frame].astype(F32), 0, 1).reshape(R * C, W)
        bundle[:R * C, lanes] = rows.astype(BF)
        top = rows[:EDGE * C]
        bottom = rows[(R - EDGE) * C:]
        to_near[:EDGE * C, lanes] = jnp.where(odd, top, bottom).astype(BF)
        to_far[:EDGE * C, lanes] = jnp.where(odd, bottom, top).astype(BF)


def stage_kernel(frames, tiles, bundle, forward_w, third_w, second_w, first_w, gate2, hidden2,
                 fields, table):
    place = lax.axis_index(SPACE)
    odd = lax.axis_index(SPACE[-1])
    entries = {BEFORE: jnp.minimum(place, 1), AFTER: jnp.minimum(tiles - 1 - place, 1), ODD: odd,
               OWN_HALF: frames * (1 - odd), THEIR_ENTRY: frames * odd + lax.axis_index(TM),
               THEIR_HALF: frames * odd, NEAR_AT: lax.axis_index(NEAR[1:]),
               FAR_AT: lax.axis_index(FAR[1:])}
    for k, entry in entries.items():
        table[k:k + 1, :] = lax.broadcast_in_dim(entry.astype(jnp.int32), (1, W), ())
    rows = bundle[FIELDS_AT:FIRST_AT, :].astype(F32)
    pair = rows[5 * R:]
    for k, field in enumerate((rows[:R] + rows[R:2 * R], rows[4 * R:5 * R],
                               rows[2 * R:3 * R] + rows[3 * R:4 * R],
                               twice(pair[:, :W] + pair[:, W:]))):
        fields[k * R:(k + 1) * R, :] = field
    for r in range(R):
        value = saved_row(bundle, r).astype(F32)
        logistic, slope = slope_parts(value)
        gate2[r * C:(r + 1) * C, :] = slope
        hidden2[r * C:(r + 1) * C, :] = (value * logistic).astype(BF)
    forward = bundle[FIRST_AT:FIRST_AT + Q, :].astype(F32)[:9, :C]
    backward = bundle[THIRD_AT:THIRD_AT + Q, :].astype(F32)[:9, :C]
    pad = jnp.zeros((Q - 6, C), F32)
    ahead = []
    back = []
    for i in range(3):
        row = forward[3 * i:3 * i + 3]
        ahead += [row, row, pad]
        row = backward[6 - 3 * i:9 - 3 * i]
        back += [row, row, pad]
        for j in range(3):
            tap = 3 * (2 - i) + j
            at = R * C + (tap // 4) * C
            tile = bundle[at:at + C, (tap % 4) * C:(tap % 4 + 1) * C].astype(F32)
            second_w[j * C:(j + 1) * C, i * C:(i + 1) * C] = jnp.transpose(tile).astype(BF)
    forward_w[...] = jnp.transpose(jnp.concatenate(ahead, axis=0)).astype(BF)
    third_w[...] = jnp.transpose(jnp.concatenate(back, axis=0)).astype(BF)
    first_w[...] = jnp.concatenate([forward, jnp.zeros((Q - 9, C), F32)], axis=0).astype(BF)


def unpack_kernel(step, places, near, far, own_fields, _, part, up, masks, base, fixed, snapshot):
    for k, target in enumerate((up, masks, fixed, snapshot)):
        target[HALO:HALO + R, :] = own_fields[k * R:(k + 1) * R, :]
    for side, at, first in ((0, 0, R - HALO), (1, HALO + R, 0)):
        fields = edge_rows(places, near, far, side, EDGE * C, FIELDS * R)

        def field(k):
            return fields[k * R:(k + 1) * R]

        for target, value in ((up, field(0) + field(1)), (fixed, field(2) + field(3)),
                              (masks, field(4)),
                              (snapshot, twice(field(5)[:, :W] + field(5)[:, W:]))):
            target[at:at + HALO, :] = value[first:first + HALO]
    send_all(part, masked_sum(masks[...], fixed[...]))
    base[...] = fixed[...] + step * masks[...] * snapshot[...]


def edge_rows(places, near, far, side, at, count):
    from_pair = twice(places[ODD:ODD + 1, :]) == 1 - side
    return jnp.where(from_pair, near[side, at:at + count, :].astype(F32),
                     far[at:at + count, :].astype(F32))


def saved_row(ref, at):
    return ref[at * C:(at + 1) * C, :]


def keep_row(value, at, before, after):
    if at < HALO:
        return value * before
    if at >= HALO + R:
        return value * after
    return value


def ends(places):
    return tuple(twice(places[k:k + 1, :]).astype(F32) for k in (BEFORE, AFTER))


def first_kernel(step, places, sums, near, far, own, up, masks, base, third_w, second_w, first_w,
                 forward_w, part, moved, gate2, gate1, hidden, inputs, copies, d2, d1, taps):
    before, after = ends(places)
    for k in range(EXT - 2):
        at = k + 1
        if HALO <= at < HALO + R:
            gate2[k * C:(k + 1) * C, :] = saved_row(own, at - HALO)
        else:
            side, row = (0, k) if at < HALO else (1, at - HALO - R)
            slope = slope_parts(edge_rows(places, near, far, side, row * C, C))[1]
            gate2[k * C:(k + 1) * C, :] = keep_row(slope, at, before, after)
    frame_sum = gathered_sum(sums)[:EXT]
    denoiser_input = base[...] - step * masks[...] * twice(frame_sum)
    copies[...] = jnp.zeros_like(copies)
    fill_shifted(denoiser_input, copies, -1)
    inputs[...] = take_rows(copies, (HALO - 1) * Q, (HALO + R + 1) * Q).astype(BF)
    for k in range(EXT - 4):
        at = k + 2
        value = dot(forward_w[...], take_rows(copies, (at - 1) * Q, (at + 2) * Q).astype(BF))
        logistic, slope = slope_parts(value)
        gate1[k * C:(k + 1) * C, :] = keep_row(slope, at, before, after)
        if HALO <= at < HALO + R:
            own_at = at - HALO
            hidden[own_at * C:(own_at + 1) * C, :] = (value * logistic).astype(BF)
    field = adjoint_map(0, up[...], gate2, gate1, third_w[...], second_w[...], first_w[...],
                        copies, d2, d1, taps)
    finish_wide(field, before, after, masks, part, moved)


def finish_wide(field, before, after, masks, part, moved):
    count = EXT - 6
    row = lax.broadcasted_iota(jnp.int32, field.shape, 0)
    keep = jnp.where(row < HALO - 3, before, jnp.where(row >= HALO - 3 + R, after, 1.0))
    field = field * keep
    moved[...] = field
    send_all(part, masked_sum(masks[3:3 + count, :], field))


def narrow_field(step, sums, moved, up, masks):
    count = EXT - 6
    totals = gathered_sum(sums)[:count]
    return up[3:3 + count, :] + moved[...] - step * masks[3:3 + count, :] * twice(totals)


def second_kernel(step, sums, moved, up, masks, gate2, gate1, third_w, second_w, first_w,
                  part, out, copies, d2, d1, taps):
    copies[...] = jnp.zeros_like(copies)
    field = narrow_field(step, sums, moved, up, masks)
    result = adjoint_map(3, field, gate2, gate1, third_w[...], second_w[...], first_w[...],
                         copies, d2, d1, taps)
    out[...] = result
    total = masked_sum(masks[HALO:HALO + R, :], result)
    half = jnp.concatenate([total[:R // 2], total[R // 2:]], axis=1)
    send_all(part, jnp.concatenate([result, half], axis=0))


def pair_total(received, first):
    count = received.shape[0] // 2
    half = received[first].astype(F32)
    for k in range(1, count):
        half = half + received[first + k].astype(F32)
    half = half[R:R + R // 2]
    return jnp.concatenate([half[:, :W], half[:, W:]], axis=0)


def update_kernel(step, places, received, moved, up, masks, out, sent):
    totals = pair_total(received, places[OWN_HALF, 0])
    out[...] = (up[HALO:HALO + R, :] + moved[...]
                - step * masks[HALO:HALO + R, :] * twice(totals))
    sent[...] = out[...].astype(BF)


def third_kernel(step, places, received, own, near, up, masks, gate2, gate1, third_w,
                 second_w, first_w, part, moved, copies, d2, d1, taps, whole):
    copies[...] = jnp.zeros_like(copies)
    before, after = ends(places)
    totals = twice(pair_total(received, places[THEIR_HALF, 0]))
    theirs = received[places[THEIR_ENTRY, 0]].astype(F32)[:R]
    after_rows = slice(HALO + R, EXT)
    low = (up[0:HALO, :] + theirs[R - HALO:]
           - step * masks[0:HALO, :] * totals[R - HALO:]) * before
    high = (up[after_rows, :] + theirs[:HALO]
            - step * masks[after_rows, :] * totals[:HALO]) * after
    odd = twice(places[ODD:ODD + 1, :]) == 1
    whole[0:HALO, :] = jnp.where(odd, near[0].astype(F32)[R - HALO:], low)
    whole[HALO:HALO + R, :] = own[...]
    whole[HALO + R:, :] = jnp.where(odd, high, near[1].astype(F32)[:HALO])
    field = adjoint_map(0, whole[...], gate2, gate1, third_w[...], second_w[...], first_w[...],
                        copies, d2, d1, taps)
    finish_wide(field, before, after, masks, part, moved)


def last_kernel(step, cores, sums, moved, up, masks, gate2, gate1, hidden2, hidden, inputs, third_w,
                second_w, first_w, adjoint, grads, copies, d2, d1, taps, total):
    copies[...] = jnp.zeros_like(copies)
    field = narrow_field(step, sums, moved, up, masks)
    adjoint[...] = field[3:3 + R]
    result = adjoint_map(3, field, gate2, gate1, third_w[...], second_w[...], first_w[...],
                         copies, d2, d1, taps)
    snapshot = masked_sum(masks[HALO:HALO + R, :], result)
    left = []
    right = []
    left_first = []
    right_first = []
    left_third = []
    right_third = []
    for r in range(R):
        left.append(d2[(r + 1) * C:(r + 4) * C, :])
        value = hidden[r * C:(r + 1) * C, :].astype(F32)
        right.append(jnp.concatenate(
            [roll_cols(value, 1), value, roll_cols(value, -1)], axis=0).astype(BF))
        left_first.append(inputs[r * Q:(r + 3) * Q, :])
        right_first.append(d1[(r + 1) * C:(r + 2) * C, :])
        left_third.append(take_rows(copies, (r + 2) * Q, (r + 5) * Q).astype(BF))
        right_third.append(saved_row(hidden2, r))
    def join(parts):
        return jnp.concatenate(parts, axis=1)
    second = dot_nt(join(left), join(right))
    first = dot_nt(join(left_first), join(right_first))
    third = dot_nt(join(left_third), join(right_third))
    total[0:3 * C, 0:3 * C] = second
    total[0:3 * Q, 3 * C:] = first
    total[3 * Q:6 * Q, 3 * C:] = third
    total[6 * Q:, 3 * C:] = jnp.zeros((total.shape[0] - 6 * Q, C), F32)
    total[3 * C:, 0:3 * C] = jnp.zeros((total.shape[0] - 3 * C, 3 * C), F32)
    count = grads.shape[0]
    rows = 3 * C // count
    line = lax.broadcasted_iota(jnp.int32, grads.shape[1:], 0)
    extras = []
    for core in range(cores):
        extra = jnp.zeros(grads.shape[1:], F32)
        for k in range(R // 2 // cores):
            at = 2 * (core * (R // 2 // cores) + k)
            pair = jnp.concatenate([snapshot[at:at + 1], snapshot[at + 1:at + 2]], axis=1)
            extra = jnp.where(line == rows + k, pair, extra)
        extras.append(extra)
    for k in range(count):
        grads[k] = jnp.where(line < rows, total[k * rows:k * rows + grads.shape[1], :],
                             extras[k * cores // count]).astype(BF)


def reduce_pieces(rows, place, stride, received):
    count = received.shape[0]
    total = received[0].astype(F32)
    for k in range(1, count):
        total = total + received[k].astype(F32)
    extra = received[place].astype(F32)
    for k in range(1, count // stride):
        extra = extra + received[place + k * stride].astype(F32)
    line = lax.broadcasted_iota(jnp.int32, total.shape, 0)
    return jnp.where(line < rows, total, extra)


def sum_kernel(rows, stride, at, places, received, out):
    total = reduce_pieces(rows, places[at, 0], stride, received).astype(BF)
    for k in range(out.shape[0]):
        out[k] = total


def output_kernel(step, scale, cores, places, received, field, adjoint, snapshot, first, second,
                  third, total):
    adjoint[0] = field[:, :W]
    adjoint[1] = field[:, W:]
    count = received.shape[0]
    rows = 3 * C // count
    for core in range(cores):
        piece = received[places[NEAR_AT, 0] + core * (count // cores)].astype(F32) * step
        for k in range(R // 2 // cores):
            at = 2 * (core * (R // 2 // cores) + k)
            snapshot[at:at + 1, :] = piece[rows + k:rows + k + 1, :W]
            snapshot[at + 1:at + 2, :] = piece[rows + k:rows + k + 1, W:]
    for k in range(count):
        total[k * rows:(k + 1) * rows, :] = received[k].astype(F32)[:rows] * scale
    for i in (-1, 0, 1):
        for j in (-1, 0, 1):
            tap = 3 * (i + 1) + (j + 1)
            back = 1 - i
            ahead = 1 + i
            second[tap] = total[back * C:(back + 1) * C, (j + 1) * C:(j + 2) * C]
            at = ahead * Q + j + 1
            first[tap:tap + 1, :] = total[at:at + 1, 3 * C:] + total[at + 3:at + 4, 3 * C:]
            at = 3 * Q + back * Q + j + 1
            third[tap:tap + 1, :] = total[at:at + 1, 3 * C:] + total[at + 3:at + 4, 3 * C:]


def call(kernel, outs, scratch, *operands, specs=None, cost=None, sems=0, limit=40):
    if specs is None:
        specs = [pl.BlockSpec(memory_space=pltpu.VMEM)] * len(operands)
    return pl.pallas_call(
        kernel,
        out_shape=[jax.ShapeDtypeStruct(shape, dtype) for shape, dtype in outs],
        in_specs=specs,
        out_specs=[pl.BlockSpec(memory_space=pltpu.VMEM)] * len(outs),
        scratch_shapes=[pltpu.VMEM(shape, dtype) for shape, dtype in scratch]
        + [pltpu.SemaphoreType.DMA((sems,))] * (sems > 0),
        compiler_params=pltpu.CompilerParams(vmem_limit_bytes=limit * 2**20),
        cost_estimate=cost,
    )(*operands)


def split_parts(field):
    high = field.astype(BF)
    return high, (field - high.astype(F32)).astype(BF)


def exchange(value, axis):
    return lax.all_to_all(value, axis, 0, 0, tiled=True)


def per_device(equilibrium, measurement, coding_masks, upstream, saved_second, conv_first,
               conv_second, conv_third):
    frames = lax.axis_size(TM)
    tiles = lax.axis_size(SPACE)
    total_frames = 2 * frames
    step = 1.0 / total_frames
    scale = 1.0 / math.sqrt(total_frames * R * tiles * W)
    hbm = pl.BlockSpec(memory_space=pltpu.HBM)
    whole = pl.BlockSpec(memory_space=pltpu.VMEM)
    edge = ((EDGE * C + FIELDS * R, LANES), BF)
    fields = ((4 * R, LANES), F32)
    frame = ((2, R, W), F32)
    to_near, to_far, bundle = call(
        pack_kernel, [edge, edge, ((THIRD_AT + Q, LANES), BF)],
        [frame, frame, ((2, R, W), jnp.int32), ((R, W), F32), ((2, C, R, W), BF), ((9, C), BF),
         ((9, C, C), BF), ((9, C), BF)],
        upstream, equilibrium, coding_masks, measurement, saved_second, conv_first, conv_second,
        conv_third, specs=[hbm] * 8, sems=8, limit=60)
    far = lax.ppermute(to_far, SPACE, [(k + side, k + 1 - side) for k in range(1, tiles - 1, 2)
                                       for side in range(2)])
    near = lax.all_gather(to_near, SPACE[-1])

    forward_w, third_w, second_w, first_w, gate2_own, hidden2, own_fields, table = call(
        functools.partial(stage_kernel, frames, tiles),
        [((C, 3 * Q), BF), ((C, 3 * Q), BF), ((3 * C, 3 * C), BF), ((Q, C), BF),
         ((R * C, LANES), F32), ((R * C, LANES), BF), fields, ((8, W), jnp.int32)], [],
        bundle,
        cost=pl.CostEstimate(flops=2 * 10**6, bytes_accessed=10**6, transcendentals=0))

    ext = ((EXT, LANES), F32)
    part, up, masks, base = call(
        functools.partial(unpack_kernel, step),
        [((frames, 24, W), BF), ext, ext, ext], [ext, ext],
        table, near, far, own_fields, gate2_own)
    sums = exchange(part, TM)

    narrow = EXT - 6
    weights = (third_w, second_w, first_w)
    copies = ((2, EXT * Q, W), F32)
    d2 = (((EXT - 2) * C, LANES), BF)
    d1 = (((EXT - 4) * C, LANES), BF)
    taps = ((2, (EXT - 4) * Q, W), F32)
    slim_scratch = [((2, narrow * Q, W), F32), (((narrow - 2) * C, LANES), BF),
                    (((narrow - 4) * C, LANES), BF), ((2, (narrow - 4) * Q, W), F32)]
    wide_outs = [((frames, 16, W), BF), ((narrow, LANES), F32)]
    part, moved, gate2, gate1, hidden, inputs = call(
        functools.partial(first_kernel, step),
        wide_outs + [(((EXT - 2) * C, LANES), F32), (((EXT - 4) * C, LANES), F32),
                     ((R * C, LANES), BF), (((R + 2) * Q, LANES), BF)],
        [copies, d2, d1, taps],
        table, sums, near, far, gate2_own, up, masks, base, *weights, forward_w)
    sums = exchange(part, TM)

    part, moved = call(
        functools.partial(second_kernel, step),
        [((2 * frames, 2 * R, LANES), BF), ((R, LANES), F32)], slim_scratch,
        sums, moved, up, masks, gate2, gate1, *weights)
    groups = [[t * tiles + (k + side) % tiles for side in range(2) for t in range(frames)]
              for k in range(1, tiles, 2)]
    received = lax.all_to_all(part, TM + SPACE, 0, 0, axis_index_groups=groups, tiled=True)
    field, sent = call(functools.partial(update_kernel, step),
                       [((R, LANES), F32), ((R, LANES), BF)], [],
                  table, received, moved, up, masks)
    near = lax.all_gather(sent, SPACE[-1])
    part, moved = call(
        functools.partial(third_kernel, step), wide_outs, [copies, d2, d1, taps, ext],
        table, received, field, near, up, masks, gate2, gate1, *weights)
    sums = exchange(part, TM)

    near_sizes = [lax.axis_size(name) for name in NEAR]
    far_sizes = [lax.axis_size(name) for name in FAR]
    near_count = math.prod(near_sizes)
    far_count = math.prod(far_sizes)
    rows = 3 * C // near_count
    piece = -(-(rows + R // 2 // near_sizes[0]) // 8) * 8
    adjoint, grads = call(
        functools.partial(last_kernel, step, near_sizes[0]),
        [((R, LANES), F32), ((near_count, piece, LANES), BF)],
        slim_scratch + [((3 * C + piece, LANES), F32)],
        sums, moved, up, masks, gate2, gate1, hidden2, hidden, inputs, *weights)

    received = exchange(grads, NEAR)
    near_stride = near_count // near_sizes[0]
    far_stride = far_count // far_sizes[0]
    received, = call(
        functools.partial(sum_kernel, rows, near_stride, NEAR_AT),
        [((far_count, piece, LANES), BF)], [], table, received)
    received = exchange(received, FAR)
    received, = call(
        functools.partial(sum_kernel, rows, far_stride, FAR_AT),
        [((near_count, piece, LANES), BF)], [], table, received)
    received = exchange(received, NEAR)
    return call(
        functools.partial(output_kernel, step, scale, near_sizes[0]),
        [((2, R, W), F32), ((R, W), F32), ((9, C), F32), ((9, C, C), F32), ((9, C), F32)],
        [((3 * C, LANES), F32)], table, received, adjoint)


AXES = (("zh", 4), ("core", 2), ("zl", 2), ("yh", 4), ("yl", 2), ("xh", 2), ("xl", 2))


def solution(mesh, axes=AXES):
    names = tuple(name for name, _ in axes)
    sizes = tuple(size for _, size in axes)
    fine = Mesh(mesh.devices.reshape(sizes), names)
    placed = (
        P(TM, SPACE, None),
        P(SPACE, None),
        P(TM, SPACE, None),
        P(TM, SPACE, None),
        P(TM, None, SPACE, None),
        P(),
        P(),
        P(),
    )
    return jax.shard_map(
        per_device,
        mesh=fine,
        in_specs=placed,
        out_specs=(P(TM, SPACE, None), P(SPACE, None), P(), P(), P()),
        check_vma=False,
    )
```
